32 devices in a mesh: seq: 4 (over y, x), batch: 8 (over z, core).
Axes of the slice: x: 2, y: 2, z: 4, core: 2. Of those that a mesh axis runs over, the one named last changes fastest.
Arguments:
- inputs: bfloat16 [8, 8192, 512], P('batch', 'seq'), may hold values from -6 to 6
- cotangent: bfloat16 [8, 8192, 512], P('batch', 'seq'), may hold values from -6 to 6
- short_lengths: int32 [4, 4], replicated, may hold values from 1 to 3072, 8192 in all within a row
- long_lengths: int32 [4, 2], replicated, may hold values from 1 to 7680, 8192 in all within a row
- norm_gain: float32 [512], replicated, may hold values from 0.1 to 1.9
- w_gates: bfloat16 [512, 3072], replicated, may hold values from -0.25 to 0.25
- gate_bias: float32 [3072], replicated, may hold values from -12 to 4, as said below
- w_out: bfloat16 [1024, 512], replicated, may hold values from -0.1875 to 0.1875
- out_bias: float32 [512], replicated, may hold values from -3 to 3
- mlp_gain: float32 [512], replicated, may hold values from 0.1 to 1.9
- w_up: bfloat16 [512, 2048], replicated, may hold values from -0.25 to 0.25
- up_bias: float32 [2048], replicated, may hold values from -3 to 3
- w_down: bfloat16 [2048, 512], replicated, may hold values from -0.125 to 0.125
- down_bias: float32 [512], replicated, may hold values from -3 to 3
Outputs:
- result: bfloat16 [8, 8192, 512], P('batch', 'seq')
- grad_input: float32 [8, 8192, 512], P('batch', 'seq')
- grad_norm_gain: float32 [512], replicated
- grad_w_gates: float32 [512, 3072], replicated
- grad_gate_bias: float32 [3072], replicated
- grad_w_out: float32 [1024, 512], replicated
- grad_out_bias: float32 [512], replicated
- grad_mlp_gain: float32 [512], replicated
- grad_w_up: float32 [512, 2048], replicated
- grad_up_bias: float32 [2048], replicated
- grad_w_down: float32 [2048, 512], replicated
- grad_down_bias: float32 [512], replicated
The draws below stay inside these ranges and needn't reach their ends.
Inputs may be any that keep to these rules, and one draw needn't show every extreme that they name: `short_lengths`: row g gives, in order, the lengths of the 4 sequences that fill the 8192 tokens of group g. `long_lengths`: row g gives, in order, the lengths of the two sequences that fill the 8192 tokens of group 4 + g. `gate_bias`: three blocks of 1024: forget biases, input biases, candidate biases.
All inputs are finite; a program needn't handle non-finite values.
Results may differ from the reference program's by a relative error of at most 0.0068.
Values sent between devices are 32-bit elements; how exact they have to be, the bound alone decides.
A program may use at most 256 MiB of HBM per device.

```python
import math
import jax
import jax.numpy as jnp
import numpy as np
from jax import lax

D = 512
H = 1024
FF = 2048
TOK_DEV = 2048
SHORT_SEGS = 4
GROUP = 8192
GROUPS = 8
HALF = 4


def draw_gate_bias(key, part):
    key = jax.random.fold_in(key, 7)
    key_forget, key_inputs, key_candidate = jax.random.split(key, 3)
    forget = jax.random.uniform(key_forget, (H,), jnp.float32, 1.0, 4.0)
    inputs_part = jax.random.uniform(key_inputs, (H,), jnp.float32, -12.0, -2.0)
    candidate = jnp.clip(jax.random.normal(key_candidate, (H,), jnp.float32), -4.0, 4.0)
    return jnp.concatenate([forget, inputs_part, candidate])


def block_scale(rng, shape, pieces, smallest, high):
    loudness = 1.0
    for axis_at, shards_of in pieces:
        steps = jax.random.uniform(jax.random.fold_in(jax.random.fold_in(rng, 6), axis_at), (shards_of,), jnp.float32, smallest / len(pieces), high / len(pieces))
        loudness = loudness * jnp.repeat(jnp.exp(steps), shape[axis_at] // shards_of).reshape((-1,) + (1,) * (len(shape) - 1 - axis_at))
    return loudness


def split_up(number_of, total, limit, slope):
    weights = [(1 << 20) // math.isqrt(rank ** slope) + 1 for rank in range(2, number_of + 1)]
    rest, counts = total - limit - (number_of - 1), [1] * (number_of - 1)
    while rest > 0:
        free = [i for i in range(number_of - 1) if counts[i] < limit]
        mass, left = sum([weights[i] for i in free]), rest
        for i in free:
            more = min(limit - counts[i], max(1, left * weights[i] // mass), rest)
            counts[i] = counts[i] + more
            rest = rest - more
    return np.array([limit] + counts)


def ragged(own_key, count, total, bound, slope):
    if count == 2:
        one = jax.random.randint(own_key, (), max(1, total - bound), min(bound, total - 1) + 1)
        return jnp.stack([one, total - one])
    tallies = jnp.asarray(split_up(count, total, bound, slope), jnp.int32)
    pairs = (count - 1) // 2
    donor, taker = tallies[1:1 + 2 * pairs:2], tallies[2:2 + 2 * pairs:2]
    slack = jnp.minimum(donor - 1, bound - taker)
    moved = jax.random.randint(jax.random.fold_in(own_key, 1), (pairs,), 0, 1 << 20) % (slack + 1)
    tallies = tallies.at[1:1 + 2 * pairs:2].set(donor - moved).at[2:2 + 2 * pairs:2].set(taker + moved)
    return tallies[jax.random.permutation(jax.random.fold_in(own_key, 2), count)]


def gaussian(rng, shape, scale, reach, shards=(), kind=jnp.bfloat16):
    factor_of = block_scale(rng, shape, shards, -0.22, 0.18) if shards else 1.0
    array = jax.random.normal(rng, shape, jnp.float32) * scale * factor_of
    return jnp.minimum(jnp.maximum(array, -reach), reach).astype(kind)


def setup_inputs(seed: int = 0) -> dict:
    key_of = jax.random.split(jax.random.key(seed), 15)
    return {
        "inputs": gaussian(key_of[0], (GROUPS, GROUP, D), 1.0, 6.0, ((0, 8), (1, 4))),
        "cotangent": gaussian(key_of[1], (GROUPS, GROUP, D), 1.0, 6.0, ((0, 8), (1, 4))),
        "short_lengths": jax.vmap(lambda own: ragged(own, SHORT_SEGS, GROUP, GROUP * 3 // 8, 1))(jax.random.split(key_of[2], HALF)).reshape((HALF, SHORT_SEGS)).astype(jnp.int32),
        "long_lengths": jax.vmap(lambda own: ragged(own, 2, GROUP, GROUP - TOK_DEV // 4, 0))(jax.random.split(key_of[3], HALF)).reshape((HALF, 2)).astype(jnp.int32),
        "norm_gain": jnp.clip(1.0 + 0.18 * jax.random.normal(key_of[4], (D,), jnp.float32), 0.1, 1.9),
        "w_gates": gaussian(key_of[5], (D, 3 * H), D ** -0.5, 0.25),
        "gate_bias": draw_gate_bias(jax.random.fold_in(key_of[14], 71), 0),
        "w_out": gaussian(key_of[7], (H, D), H ** -0.5, 0.1875),
        "out_bias": gaussian(key_of[8], (D,), 0.5, 3.0, (), jnp.float32),
        "mlp_gain": jnp.clip(1.0 + 0.18 * jax.random.normal(key_of[9], (D,), jnp.float32), 0.1, 1.9),
        "w_up": gaussian(key_of[10], (D, FF), D ** -0.5, 0.25),
        "up_bias": gaussian(key_of[11], (FF,), 0.5, 3.0, (), jnp.float32),
        "w_down": gaussian(key_of[12], (FF, D), FF ** -0.5, 0.125),
        "down_bias": gaussian(key_of[13], (D,), 0.5, 3.0, (), jnp.float32),
    }


@jax.custom_vjp
def low(v):
    return lax.optimization_barrier(v.astype(jnp.bfloat16)).astype(jnp.float32)

@jax.custom_vjp
def low_back(v):
    return v

def low_keep(v):
    return (low(v), None)

def low_pass(kept, grad):
    return (grad,)

def back_keep(v):
    return (v, None)

def back_low(kept, grad):
    return (low(grad),)
low.defvjp(low_keep, low_pass)
low_back.defvjp(back_keep, back_low)
epsilon = 1e-06
highest = lax.Precision.HIGHEST

def combine(earlier, later):
    return (earlier[0] * later[0], later[0] * earlier[1] + later[1])

def rms_scale(values):
    return lax.rsqrt(lax.optimization_barrier(jnp.mean(values * values, axis=-1, keepdims=True)) + epsilon)

def gate_terms(mixed_in, keep_mask):
    width = mixed_in.shape[-1] // 3
    forget = jax.nn.sigmoid(mixed_in[:, :width])
    inputs_gate = jax.nn.sigmoid(mixed_in[:, width:2 * width])
    candidate = mixed_in[:, 2 * width:]
    totals = forget + inputs_gate
    return (forget / totals * keep_mask, inputs_gate / totals * candidate)

def block(source, keep_mask, params):
    norm_gain, w_gates, gate_bias, w_out, out_bias, mlp_gain, w_up, up_bias, w_down, down_bias = params
    normed = low(source * rms_scale(source) * norm_gain)
    mixed_in = low_back(jnp.dot(normed, w_gates, precision=highest) + gate_bias)
    decays, drives = gate_terms(mixed_in, keep_mask)
    unused, states = lax.associative_scan(combine, (decays, drives), axis=0)
    resid = source + low_back(jnp.dot(low(states), w_out, precision=highest) + out_bias)
    normed_two = low(resid * rms_scale(resid) * mlp_gain)
    upper_in = low_back(jnp.dot(normed_two, w_up, precision=highest) + up_bias)
    active = low(jax.nn.gelu(upper_in, approximate=False))
    return resid + jnp.dot(active, w_down, precision=highest) + down_bias

def start_masks(lengths):
    starts = jnp.cumsum(lengths, axis=1) - lengths
    position = jnp.arange(GROUP, dtype=jnp.int32)
    return jnp.any(position[None, :, None] == starts[:, None, :], axis=-1)

def reference(inputs, cotangent, short_lengths, long_lengths, norm_gain, w_gates, gate_bias, w_out, out_bias, mlp_gain, w_up, up_bias, w_down, down_bias):
    starting = jnp.concatenate([start_masks(short_lengths), start_masks(long_lengths)], axis=0)
    keep_all = 1.0 - starting.astype(jnp.float32)
    params = (norm_gain.astype(jnp.float32), w_gates.astype(jnp.float32), gate_bias.astype(jnp.float32), w_out.astype(jnp.float32), out_bias.astype(jnp.float32), mlp_gain.astype(jnp.float32), w_up.astype(jnp.float32), up_bias.astype(jnp.float32), w_down.astype(jnp.float32), down_bias.astype(jnp.float32))

    def one_group(totals, item):
        source, keep_row, grad_row = item
        keep_mask = keep_row[:, None]
        output, pullback = jax.vjp(lambda values, weights: block(values, keep_mask, weights), source.astype(jnp.float32), params)
        grad_source, grad_params = pullback(grad_row.astype(jnp.float32))
        totals = jax.tree.map(lambda left, right: left + right, totals, grad_params)
        return (totals, (output.astype(jnp.bfloat16), grad_source))
    zeros = jax.tree.map(jnp.zeros_like, params)
    totals, (outputs, grad_inputs) = lax.scan(one_group, zeros, (inputs, keep_all, cotangent))
    return (outputs, grad_inputs, totals[0], totals[1], totals[2], totals[3], totals[4], totals[5], totals[6], totals[7], totals[8], totals[9])
```

```python
import functools

import jax
import jax.numpy as jnp
from jax import lax
from jax.experimental import pallas as pl
from jax.experimental.pallas import tpu as pltpu
from jax.sharding import PartitionSpec as P

MESH = pl.DeviceIdType.MESH
F32 = jnp.float32
BF16 = jnp.bfloat16
epsilon = 1e-06
SUB = 8
LANES = 256


def flip(v, w):
    return v + w - 2 * w * ((v // w) % 2)


def dot(a, b):
    return jnp.dot(a, b, preferred_element_type=F32)


def dot_t(a, b):
    return lax.dot_general(a, b, (((1,), (1,)), ((), ())), preferred_element_type=F32)


def fold_rows(v):
    return jnp.sum(v.reshape(v.shape[0] // SUB, SUB, v.shape[1]), axis=0)


def inv_rms(v):
    return lax.rsqrt(jnp.mean(v * v, axis=-1, keepdims=True) + epsilon)


def to_steps(block, scratch):
    pieces, steps, n = block.shape
    flat = block.astype(F32).reshape(pieces * steps, n)
    parts = []
    for k in range(n // 128):
        scratch[k] = flat[:, k * 128 : (k + 1) * 128]
        parts.append(
            jnp.concatenate([scratch[k, pl.ds(r, pieces, stride=steps), :] for r in range(steps)], axis=0)
        )
    return jnp.concatenate(parts, axis=1)


def from_steps(value, scratch, steps):
    n = value.shape[1]
    parts = []
    for k in range(n // 128):
        for r in range(steps):
            scratch[k, pl.ds(r, SUB, stride=steps), :] = value[
                r * SUB : (r + 1) * SUB, k * 128 : (k + 1) * 128
            ]
        parts.append(scratch[k])
    return jnp.concatenate(parts, axis=1).reshape(SUB, steps, n)


def gates_kernel(
    piece, short_ref, long_ref, x_ref, gain_ref, wg_ref, bias_ref,
    a_ref, b_ref, zc_ref, fc_ref, ic_ref, xp_ref, nt_ref, prod_ref, sum_ref, perm,
):
    i = pl.program_id(0)
    steps = x_ref.shape[1]
    rows = steps * SUB
    hid = wg_ref.shape[1] // 3
    source = to_steps(x_ref[...], perm)
    xp_ref[...] = source.astype(BF16)
    normed = (source * inv_rms(source) * gain_ref[...]).astype(BF16)
    nt_ref[...] = normed.T

    group = lax.axis_index("batch")
    half = short_ref.shape[0]
    first = lax.axis_index("seq") * piece * SUB
    row = lax.broadcasted_iota(jnp.int32, (rows, 128), 0)
    pos = first + (row % SUB) * piece + i * steps + row // SUB
    short = group < half
    srow = jnp.minimum(group, half - 1)
    lrow = jnp.maximum(group - half, 0)
    begins = jnp.zeros((rows, 128), jnp.bool_)
    at = jnp.int32(0)
    for k in range(short_ref.shape[1]):
        begins = begins | (pos == jnp.where(short, at, -1))
        at = at + short_ref[srow, k]
    at = jnp.int32(0)
    for k in range(long_ref.shape[1]):
        begins = begins | (pos == jnp.where(short, -1, at))
        at = at + long_ref[lrow, k]
    keep = jnp.where(begins, 0.0, 1.0).astype(F32)

    @pl.when(i == 0)
    def _():
        prod_ref[...] = jnp.ones_like(prod_ref)
        sum_ref[...] = jnp.zeros_like(sum_ref)

    for j in range(hid // LANES):
        cols = [slice(g * hid + j * LANES, g * hid + (j + 1) * LANES) for g in range(3)]
        zf, zi, zc = [dot(normed, wg_ref[:, c]) + bias_ref[:, c] for c in cols]
        f = 1.0 / (1.0 + jnp.exp(-zf))
        g = 1.0 / (1.0 + jnp.exp(-zi))
        inv = 1.0 / (f + g)
        a = f * inv * jnp.concatenate([keep] * (LANES // 128), axis=1)
        b = g * inv
        here = cols[0]
        a_ref[:, here] = a
        b_ref[:, here] = b
        zc_ref[:, here] = zc
        fc_ref[:, here] = (1.0 - f).astype(BF16)
        ic_ref[:, here] = (1.0 - g).astype(BF16)
        u = b * zc
        prod = prod_ref[:, here]
        total = sum_ref[:, here]
        for r in range(steps):
            sl = slice(r * SUB, (r + 1) * SUB)
            prod = prod * a[sl]
            total = total * a[sl] + u[sl]
        prod_ref[:, here] = prod
        sum_ref[:, here] = total


def carry_kernel(devices, reverse, prod_ref, sum_ref, out_ref, mine, got, ssem, rsem):
    s = lax.axis_index("seq")
    b = lax.axis_index("batch")
    bar = pltpu.get_barrier_semaphore()
    others = [lax.rem(s + k, devices) for k in range(1, devices)]
    for o in others:
        pl.semaphore_signal(bar, inc=1, device_id=(o, b), device_id_type=MESH)
    order = list(range(SUB))[::-1] if reverse else list(range(SUB))
    width = prod_ref.shape[1]
    prod = jnp.ones((1, width), F32)
    total = jnp.zeros((1, width), F32)
    for c in order:
        prod = prod * prod_ref[c : c + 1, :]
        total = total * prod_ref[c : c + 1, :] + sum_ref[c : c + 1, :]
    mine[0:1, :] = prod
    mine[1:2, :] = total
    pl.semaphore_wait(bar, devices - 1)
    copies = []
    for k in range(1, devices):
        copies.append(
            pltpu.make_async_remote_copy(
                src_ref=mine, dst_ref=got.at[k - 1], send_sem=ssem.at[k - 1], recv_sem=rsem.at[k - 1],
                device_id=(others[k - 1], b), device_id_type=MESH,
            )
        )
        copies[-1].start()
    for c in copies:
        c.wait()
    state = jnp.zeros((1, width), F32)
    for turn in range(devices - 1):
        if reverse:
            owner = devices - 1 - turn
            ahead = owner > s
            back = lax.rem(s - owner + devices, devices)
        else:
            owner = turn
            ahead = owner < s
            back = lax.rem(s - owner + devices, devices)
        slot = jnp.where(back == 0, 0, back - 1)
        new = got[slot, 0:1, :] * state + got[slot, 1:2, :]
        state = jnp.where(ahead, new, state)
    for c in order:
        out_ref[c : c + 1, :] = state
        state = prod_ref[c : c + 1, :] * state + sum_ref[c : c + 1, :]


def carry(devices, reverse, prod, total):
    width = prod.shape[1]
    return pl.pallas_call(
        functools.partial(carry_kernel, devices, reverse),
        out_shape=jax.ShapeDtypeStruct((SUB, width), F32),
        in_specs=[pl.BlockSpec(memory_space=pltpu.VMEM)] * 2,
        out_specs=pl.BlockSpec(memory_space=pltpu.VMEM),
        scratch_shapes=[
            pltpu.VMEM((SUB, width), F32),
            pltpu.VMEM((devices - 1, SUB, width), F32),
            pltpu.SemaphoreType.DMA((devices - 1,)),
            pltpu.SemaphoreType.DMA((devices - 1,)),
        ],
        compiler_params=pltpu.CompilerParams(
            collective_id=1 + int(reverse), has_side_effects=True
        ),
    )(prod, total)


KA = 0.3275911 * 2.0**-0.5
ERF = [0.5 * c for c in (0.254829592, -0.284496736, 1.421413741, -1.453152027, 1.061405429)]
PHI = 0.3989422804014327


def gelu_parts(x):
    t = 1.0 / (1.0 + KA * jnp.abs(x))
    e = jnp.exp2(x * x * (-0.5 * 1.4426950408889634))
    poly = t * (ERF[0] + t * (ERF[1] + t * (ERF[2] + t * (ERF[3] + t * ERF[4]))))
    tail = poly * e
    phi = jnp.where(x >= 0.0, 1.0 - tail, tail)
    return x * phi, phi + x * (e * PHI)


def mlp_kernel(
    a_ref, b_ref, zc_ref, xp_ref, dy_ref, carry_ref, wo_ref, wu_ref, wd_ref,
    obias_ref, gain_ref, ubias_ref, dbias_ref,
    s_ref, sb_ref, act_ref, gu_ref, dyt_ref, n2t_ref, grt_ref, gres_ref, gs_ref, result_ref,
    mu_ref, gdb_ref, gub_ref, ggain_ref, gob_ref,
    state, prod, perm,
):
    i = pl.program_id(0)
    steps = dy_ref.shape[1]

    @pl.when(i == 0)
    def _():
        state[...] = carry_ref[...]
        prod[...] = jnp.ones_like(prod)
        for ref in (mu_ref, gdb_ref, gub_ref, ggain_ref, gob_ref):
            ref[...] = jnp.zeros_like(ref)

    st = state[...]
    for r in range(steps):
        sl = slice(r * SUB, (r + 1) * SUB)
        st = a_ref[sl, :] * st + b_ref[sl, :] * zc_ref[sl, :]
        s_ref[sl, :] = st
    state[...] = st
    sb = s_ref[...].astype(BF16)
    sb_ref[...] = sb
    source = xp_ref[...].astype(F32)
    resid = source + dot(sb, wo_ref[...]) + obias_ref[...]
    scale = inv_rms(resid)
    n2 = (resid * scale * gain_ref[...]).astype(BF16)
    n2t_ref[...] = n2.T
    dy32 = to_steps(dy_ref[...], perm)
    dy = dy32.astype(BF16)
    dyt_ref[...] = dy.T
    gdb_ref[...] += fold_rows(dy32)
    down = None
    gn2 = None
    for j in range(wu_ref.shape[1] // LANES):
        cols = slice(j * LANES, (j + 1) * LANES)
        upper = dot(n2, wu_ref[:, cols]) + ubias_ref[:, cols]
        act, slope = gelu_parts(upper)
        act = act.astype(BF16)
        act_ref[:, cols] = act
        gact = dot_t(dy, wd_ref[cols, :])
        gu = (gact * slope).astype(BF16)
        gu_ref[:, cols] = gu
        gub_ref[:, cols] += fold_rows(gu.astype(F32))
        d = dot(act, wd_ref[cols, :])
        n = dot_t(gu, wu_ref[:, cols])
        down = d if down is None else down + d
        gn2 = n if gn2 is None else gn2 + n
    result = resid + down + dbias_ref[...]
    result_ref[...] = from_steps(result, perm, steps).astype(BF16)
    w = gn2 * gain_ref[...]
    ggain_ref[...] += fold_rows(gn2 * resid * scale)
    gres = dy32 + scale * w - resid * (scale * scale * scale) * jnp.mean(
        w * resid, axis=-1, keepdims=True
    )
    gres_ref[...] = gres
    gr = gres.astype(BF16)
    gob_ref[...] += fold_rows(gr.astype(F32))
    grt_ref[...] = gr.T
    gs = dot_t(gr, wo_ref[...])
    gs_ref[...] = gs
    pr = prod[...]
    mu = mu_ref[...]
    for r in range(steps):
        sl = slice(r * SUB, (r + 1) * SUB)
        pr = pr * a_ref[sl, :]
        mu = mu + pr * gs[sl, :]
    prod[...] = pr
    mu_ref[...] = mu


def back_kernel(
    a_ref, b_ref, zc_ref, fc_ref, ic_ref, s_ref, gs_ref, xp_ref, gres_ref, carry_ref, wg_ref,
    gain_ref,
    gm_ref, gin_ref, ggb_ref, ggain_ref,
    state, perm,
):
    i = pl.program_id(0)
    steps = gin_ref.shape[1]
    hid = wg_ref.shape[1] // 3

    @pl.when(i == 0)
    def _():
        state[...] = carry_ref[...]
        for ref in (ggb_ref, ggain_ref):
            ref[...] = jnp.zeros_like(ref)

    gn = None
    for j in range(hid // LANES):
        here = slice(j * LANES, (j + 1) * LANES)
        mu = state[:, here]
        lams = [None] * steps
        for r in range(steps - 1, -1, -1):
            sl = slice(r * SUB, (r + 1) * SUB)
            lams[r] = gs_ref[sl, here] + mu
            mu = a_ref[sl, here] * lams[r]
        state[:, here] = mu
        lam = jnp.concatenate(lams, axis=0)
        gzc = lam * b_ref[:, here]
        big = gzc * (s_ref[:, here] - zc_ref[:, here])
        parts = (
            (big * fc_ref[:, here].astype(F32)).astype(BF16),
            (-big * ic_ref[:, here].astype(F32)).astype(BF16),
            gzc.astype(BF16),
        )
        for g in range(3):
            cols = slice(g * hid + j * LANES, g * hid + (j + 1) * LANES)
            gm_ref[:, cols] = parts[g]
            ggb_ref[:, cols] += fold_rows(parts[g].astype(F32))
            n = dot_t(parts[g], wg_ref[:, cols])
            gn = n if gn is None else gn + n
    source = xp_ref[...].astype(F32)
    scale = inv_rms(source)
    w = gn * gain_ref[...]
    ggain_ref[...] += fold_rows(gn * source * scale)
    gin = gres_ref[...] + scale * w - source * (scale * scale * scale) * jnp.mean(
        w * source, axis=-1, keepdims=True
    )
    gin_ref[...] = from_steps(gin, perm, steps)


def bits_of(size):
    w = 1
    out = []
    while w < size:
        out.append(w); w *= 2
    return out

class Plan:
    def __init__(self, seq, batch, rows):
        sb = [("seq", w) for w in bits_of(seq)]
        bb = [("batch", w) for w in bits_of(batch)][1:]
        self.orders = [sb + bb, sb[::-1] + bb, bb[:1] + sb + bb[1:], sb + bb, sb[::-1] + bb, bb[:1] + sb[::-1] + bb[1:]]
        self.K = len(sb) + len(bb)
        self.rows = rows
        self.sizes = [rows]
        self.halve = []
        for k in range(self.K + 1):
            h = self.sizes[-1] >= 16
            self.halve.append(h)
            self.sizes.append(self.sizes[-1] // 2 if h else self.sizes[-1])
        self.stages = 2 * (self.K + 1)
        self.colors = len(self.orders)
        self.base = []
        tot = 0
        for k in range(self.K + 1):
            self.base.append(tot); tot += self.sizes[k + 1]
        self.recv_rows = tot

def pick(color, values):
    out = values[-1]
    for i in range(len(values) - 1):
        out = jnp.where(color == i, values[i], out)
    return out

def step_info(plan, k, color):
    s = lax.axis_index("seq"); b = lax.axis_index("batch")
    if k == 0:
        return b % 2, (s, flip(b, 1))
    mine, ps, pb = [], [], []
    for order in plan.orders:
        axis, w = order[k - 1]
        if axis == "seq":
            mine.append((s // w) % 2); ps.append(flip(s, w)); pb.append(b)
        else:
            mine.append((b // w) % 2); ps.append(s); pb.append(flip(b, w))
    return pick(color, mine), (pick(color, ps), pick(color, pb))

def offsets(plan, c, color, upto):
    off = c * plan.rows
    for k in range(upto):
        if plan.halve[k]:
            bit, _ = step_info(plan, k, color)
            off = off + bit * plan.sizes[k + 1]
    return pl.multiple_of(off, 8)

def copy_of(plan, acc, recv, ssem, rsem, c, j):
    color = c % plan.colors
    slot = color * 2 + (c // plan.colors) % 2
    K = plan.K
    if j <= K:
        k = j
        bit, dev = step_info(plan, k, color)
        n = plan.sizes[k + 1]
        base = offsets(plan, c, color, k)
        src = base + (1 - bit) * n if plan.halve[k] else base
        return pltpu.make_async_remote_copy(
            src_ref=acc.at[pl.ds(pl.multiple_of(src, 8), n)], dst_ref=recv.at[slot, pl.ds(plan.base[k], n)],
            send_sem=ssem.at[slot, j], recv_sem=rsem.at[slot, j], device_id=dev, device_id_type=MESH)
    k = 2 * K + 1 - j
    if not plan.halve[k]:
        return None
    bit, dev = step_info(plan, k, color)
    n = plan.sizes[k + 1]
    mine = offsets(plan, c, color, k + 1)
    return pltpu.make_async_remote_copy(
        src_ref=acc.at[pl.ds(mine, n)], dst_ref=acc.at[pl.ds(mine, n)],
        send_sem=ssem.at[slot, j], recv_sem=rsem.at[slot, j], device_id=dev, device_id_type=MESH)

def finish(plan, acc, recv, ssem, rsem, free, c, j):
    cp = copy_of(plan, acc, recv, ssem, rsem, c, j)
    if cp is None:
        return
    cp.wait()
    if j <= plan.K:
        color = c % plan.colors
        slot = color * 2 + (c // plan.colors) % 2
        n = plan.sizes[j + 1]
        if plan.halve[j]:
            _, dev = step_info(plan, j, color)
            pl.semaphore_signal(free.at[slot, j], inc=1, device_id=dev, device_id_type=MESH)
        off = offsets(plan, c, color, j + 1)
        acc[pl.ds(off, n), :] = acc[pl.ds(off, n), :] + recv[slot, pl.ds(plan.base[j], n), :]

def tick(plan, nchunks, acc, recv, ssem, rsem, free, t, done, L=1):
    for j in range(plan.stages, -1, -1):
        c = t - L * j
        @pl.when((c >= 0) & (c < nchunks))
        def _():
            if j > 0:
                finish(plan, acc, recv, ssem, rsem, free, c, j - 1)
            if j < plan.stages:
                cp = copy_of(plan, acc, recv, ssem, rsem, c, j)
                if cp is not None:
                    if j > plan.K:
                        color = c % plan.colors
                        slot = color * 2 + (c // plan.colors) % 2
                        pl.semaphore_wait(free.at[slot, 2 * plan.K + 1 - j], 1)
                    cp.start()
            else:
                done(c)

def greet(plan, extra=()):
    s = lax.axis_index("seq"); b = lax.axis_index("batch")
    who = [(s, flip(b, 1))]
    for axis, w in plan.orders[0]:
        who.append((flip(s, w), b) if axis == "seq" else (s, flip(b, w)))
    who += list(extra)
    bar = pltpu.get_barrier_semaphore()
    for p in who:
        pl.semaphore_signal(bar, inc=1, device_id=p, device_id_type=MESH)
    pl.semaphore_wait(bar, len(who))


def small_copy(plan, small, got, ssem, rsem, k):
    _, dev = step_info(plan, k, 0)
    return pltpu.make_async_remote_copy(
        src_ref=small, dst_ref=got.at[k], send_sem=ssem.at[k], recv_sem=rsem.at[k],
        device_id=dev, device_id_type=MESH)


def ar_kernel(plan, nchunks, lag, x_hbm, small_in, o_hbm, small_out,
              acc, recv, ssem, rsem, free, isem, osem, small, got, s2sem, r2sem):
    cp = pltpu.make_async_copy(x_hbm, acc, isem)
    cp.start()
    small[...] = small_in[...]
    greet(plan)
    cp.wait()
    def out_copy(c):
        rows = pl.ds(pl.multiple_of(c * plan.rows, 8), plan.rows)
        return pltpu.make_async_copy(acc.at[rows], o_hbm.at[rows], osem.at[c])
    def body(t, _):
        for k in range(plan.K + 2):
            @pl.when(t == k * lag)
            def _():
                if k > 0:
                    small_copy(plan, small, got, s2sem, r2sem, k - 1).wait()
                    small[...] = small[...] + got[k - 1]
                if k <= plan.K:
                    small_copy(plan, small, got, s2sem, r2sem, k).start()
        tick(plan, nchunks, acc, recv, ssem, rsem, free, t, lambda c: out_copy(c).start(), lag)
        return 0
    lax.fori_loop(0, nchunks + lag * plan.stages, body, 0)
    small_out[...] = small[...]
    def wait(c, _):
        out_copy(c).wait()
        return 0
    lax.fori_loop(0, nchunks, wait, 0)

def all_reduce(x, small, seq, batch, chunk_rows, lag):
    plan = Plan(seq, batch, chunk_rows)
    n = x.shape[0] // chunk_rows
    slots = plan.colors * 2
    any_space = pl.BlockSpec(memory_space=pl.ANY)
    vmem = pl.BlockSpec(memory_space=pltpu.VMEM)
    return pl.pallas_call(
        functools.partial(ar_kernel, plan, n, lag),
        out_shape=[jax.ShapeDtypeStruct(x.shape, F32), jax.ShapeDtypeStruct(small.shape, F32)],
        in_specs=[any_space, vmem],
        out_specs=[any_space, vmem],
        scratch_shapes=[
            pltpu.VMEM(x.shape, F32),
            pltpu.VMEM((slots, plan.recv_rows, x.shape[1]), F32),
            pltpu.SemaphoreType.DMA((slots, plan.stages)),
            pltpu.SemaphoreType.DMA((slots, plan.stages)),
            pltpu.SemaphoreType.REGULAR((slots, plan.K + 1)),
            pltpu.SemaphoreType.DMA,
            pltpu.SemaphoreType.DMA((n,)),
            pltpu.VMEM(small.shape, F32),
            pltpu.VMEM((plan.K + 1,) + small.shape, F32),
            pltpu.SemaphoreType.DMA((plan.K + 1,)),
            pltpu.SemaphoreType.DMA((plan.K + 1,)),
        ],
        compiler_params=pltpu.CompilerParams(collective_id=0, has_side_effects=True, vmem_limit_bytes=60 << 20),
    )(x, small)


def full(shape):
    return pl.BlockSpec(shape, lambda i: (0,) * len(shape), pipeline_mode=pl.Buffered(1))


def held(shape):
    return pl.BlockSpec(shape, lambda i: (0,) * len(shape))


def local_part(mesh_seq, inputs, cotangent, short_lengths, long_lengths, norm_gain, w_gates, gate_bias, w_out,
               out_bias, mlp_gain, w_up, up_bias, w_down, down_bias, tile=256):
    tok, d = inputs.shape[1:]
    hid = w_out.shape[0]
    ff = w_up.shape[1]
    piece = tok // SUB
    steps = tile // SUB
    grid = tok // tile
    x = inputs.reshape(SUB, piece, d)
    dy = cotangent.reshape(SUB, piece, d)
    gain1 = norm_gain.reshape(1, d)
    gain2 = mlp_gain.reshape(1, d)
    sds = jax.ShapeDtypeStruct
    rows = lambda n: pl.BlockSpec((tile, n), lambda i: (i, 0))
    natural = pl.BlockSpec((SUB, steps, d), lambda i: (0, i, 0))
    turned = pl.BlockSpec((d, tile), lambda i: (0, i))
    params = pltpu.CompilerParams(
        dimension_semantics=("arbitrary",), vmem_limit_bytes=56 << 20
    )
    a, b, zc, fc, ic, xp, nt, prod, total = pl.pallas_call(
        functools.partial(gates_kernel, piece),
        grid=(grid,),
        in_specs=[
            pl.BlockSpec(memory_space=pltpu.SMEM), pl.BlockSpec(memory_space=pltpu.SMEM),
            natural, full((1, d)), full((d, 3 * hid)), full((1, 3 * hid)),
        ],
        out_specs=[rows(hid)] * 5 + [rows(d), turned, held((SUB, hid)), held((SUB, hid))],
        out_shape=[sds((tok, hid), F32)] * 3 + [sds((tok, hid), BF16)] * 2
        + [sds((tok, d), BF16), sds((d, tok), BF16), sds((SUB, hid), F32), sds((SUB, hid), F32)],
        scratch_shapes=[pltpu.VMEM((d // 128, tile, 128), F32)],
        compiler_params=params,
    )(short_lengths, long_lengths, x, gain1, w_gates, gate_bias.reshape(1, 3 * hid))

    enter = carry(mesh_seq, False, prod, total)

    outs = pl.pallas_call(
        mlp_kernel,
        grid=(grid,),
        in_specs=[rows(hid)] * 3 + [rows(d), natural, full((SUB, hid)), full((hid, d)), full((d, ff)), full((ff, d)),
                  full((1, d)), full((1, d)), full((1, ff)), full((1, d))],
        out_specs=[rows(hid), rows(hid), rows(ff), rows(ff), turned, turned, turned, rows(d), rows(hid), natural,
                   held((SUB, hid)), held((SUB, d)), held((SUB, ff)), held((SUB, d)), held((SUB, d))],
        out_shape=[sds((tok, hid), F32), sds((tok, hid), BF16), sds((tok, ff), BF16), sds((tok, ff), BF16),
                   sds((d, tok), BF16), sds((d, tok), BF16), sds((d, tok), BF16), sds((tok, d), F32),
                   sds((tok, hid), F32), sds((SUB, piece, d), BF16),
                   sds((SUB, hid), F32), sds((SUB, d), F32), sds((SUB, ff), F32), sds((SUB, d), F32), sds((SUB, d), F32)],
        scratch_shapes=[pltpu.VMEM((SUB, hid), F32), pltpu.VMEM((SUB, hid), F32), pltpu.VMEM((d // 128, tile, 128), F32)],
        compiler_params=params,
    )(a, b, zc, xp, dy, enter, w_out, w_up, w_down, out_bias.reshape(1, d), gain2, up_bias.reshape(1, ff),
      down_bias.reshape(1, d))
    s, sb, act, gu, dyt, n2t, grt, gres, gs, result, mu, gdb, gub, ggain2, gob = outs

    enter_back = carry(mesh_seq, True, prod, mu)

    back = lambda n: pl.BlockSpec((tile, n), lambda i: (grid - 1 - i, 0))
    gm, gin, ggb, ggain1 = pl.pallas_call(
        back_kernel,
        grid=(grid,),
        in_specs=[back(hid)] * 7 + [back(d), back(d), full((SUB, hid)), full((d, 3 * hid)), full((1, d))],
        out_specs=[back(3 * hid), pl.BlockSpec((SUB, steps, d), lambda i: (0, grid - 1 - i, 0)),
                   held((SUB, 3 * hid)), held((SUB, d))],
        out_shape=[sds((tok, 3 * hid), BF16), sds((SUB, piece, d), F32), sds((SUB, 3 * hid), F32), sds((SUB, d), F32)],
        scratch_shapes=[pltpu.VMEM((SUB, hid), F32), pltpu.VMEM((d // 128, tile, 128), F32)],
        compiler_params=params,
    )(a, b, zc, fc, ic, s, gs, xp, gres, enter_back, w_gates, gain1)
    return (result, gin, (nt, gm), (grt, sb), (n2t, gu), (dyt, act),
            (ggain1, ggb, gob, ggain2, gub, gdb))


def blocks_of(v):
    d, n = v.shape
    return v.reshape(d, n // LANES, LANES).transpose(1, 0, 2).reshape(-1, LANES)


def unblock(v, d):
    n = v.shape[0] // d
    return v.reshape(n, d, LANES).transpose(1, 0, 2).reshape(d, n * LANES)


def per_device(seq, batch, *args):
    result, gin, gates, out, up, down, small = local_part(seq, *args)
    inputs = args[0]
    d = inputs.shape[2]
    big = [dot(*pair) for pair in (down, up, out, gates)]
    vecs = [jnp.sum(v, axis=0) for v in small]
    flat = jnp.concatenate(vecs)
    lines = -(-flat.shape[0] // (8 * LANES)) * 8
    flat = jnp.pad(flat, (0, lines * LANES - flat.shape[0])).reshape(lines, LANES)
    total, flat = all_reduce(jnp.concatenate([blocks_of(v) for v in big]), flat, seq, batch, d, 3)
    flat = flat.reshape(-1)
    grads = []
    at = 0
    for v in big:
        n = v.shape[1] // LANES * d
        grads.append(unblock(total[at : at + n], d))
        at += n
    svecs = []
    at = 0
    for v in vecs:
        svecs.append(flat[at : at + v.shape[0]])
        at += v.shape[0]
    g_down, g_up, g_out, g_gates = grads
    ggain1, ggb, gob, ggain2, gub, gdb = svecs
    return (result.reshape(inputs.shape), gin.reshape(inputs.shape), ggain1, g_gates, ggb, g_out.T, gob,
            ggain2, g_up, gub, g_down.T, gdb)


def solution(mesh):
    rows = P("batch", "seq", None)
    return jax.shard_map(
        functools.partial(per_device, mesh.shape["seq"], mesh.shape["batch"]),
        mesh=mesh,
        in_specs=(rows, rows) + (P(),) * 12,
        out_specs=(rows, rows) + (P(),) * 10,
        check_vma=False,
    )
```

```python
import functools

import jax
import jax.numpy as jnp
from jax import lax
from jax.experimental import pallas as pl
from jax.experimental.pallas import tpu as pltpu
from jax.sharding import PartitionSpec as P

MESH = pl.DeviceIdType.MESH
F32 = jnp.float32
BF16 = jnp.bfloat16
epsilon = 1e-06
SUB = 8
LANES = 256
LAG = 3


def flip(v, w):
    return v + w - 2 * w * ((v // w) % 2)


def dot(a, b):
    return jnp.dot(a, b, preferred_element_type=F32)


def dot_t(a, b):
    return lax.dot_general(a, b, (((1,), (1,)), ((), ())), preferred_element_type=F32)


def fold_rows(v):
    return jnp.sum(v.reshape(v.shape[0] // SUB, SUB, v.shape[1]), axis=0)


def inv_rms(v):
    return lax.rsqrt(jnp.mean(v * v, axis=-1, keepdims=True) + epsilon)


def to_steps(block, scratch):
    pieces, steps, n = block.shape
    flat = block.astype(F32).reshape(pieces * steps, n)
    parts = []
    for k in range(n // 128):
        scratch[k] = flat[:, k * 128 : (k + 1) * 128]
        parts.append(
            jnp.concatenate([scratch[k, pl.ds(r, pieces, stride=steps), :] for r in range(steps)], axis=0)
        )
    return jnp.concatenate(parts, axis=1)


def from_steps(value, scratch, steps):
    n = value.shape[1]
    parts = []
    for k in range(n // 128):
        for r in range(steps):
            scratch[k, pl.ds(r, SUB, stride=steps), :] = value[
                r * SUB : (r + 1) * SUB, k * 128 : (k + 1) * 128
            ]
        parts.append(scratch[k])
    return jnp.concatenate(parts, axis=1).reshape(SUB, steps, n)


def gates_kernel(
    piece, short_ref, long_ref, x_ref, gain_ref, wg_ref, bias_ref,
    a_ref, b_ref, zc_ref, fc_ref, ic_ref, xp_ref, nt_ref, prod_ref, sum_ref, perm,
):
    i = pl.program_id(0)
    steps = x_ref.shape[1]
    rows = steps * SUB
    hid = wg_ref.shape[1] // 3
    source = to_steps(x_ref[...], perm)
    xp_ref[...] = source.astype(BF16)
    normed = (source * inv_rms(source) * gain_ref[...]).astype(BF16)
    nt_ref[...] = normed.T

    group = lax.axis_index("batch")
    half = short_ref.shape[0]
    first = lax.axis_index("seq") * piece * SUB
    row = lax.broadcasted_iota(jnp.int32, (rows, 128), 0)
    pos = first + (row % SUB) * piece + i * steps + row // SUB
    short = group < half
    srow = jnp.minimum(group, half - 1)
    lrow = jnp.maximum(group - half, 0)
    begins = jnp.zeros((rows, 128), jnp.bool_)
    at = jnp.int32(0)
    for k in range(short_ref.shape[1]):
        begins = begins | (pos == jnp.where(short, at, -1))
        at = at + short_ref[srow, k]
    at = jnp.int32(0)
    for k in range(long_ref.shape[1]):
        begins = begins | (pos == jnp.where(short, -1, at))
        at = at + long_ref[lrow, k]
    keep = jnp.where(begins, 0.0, 1.0).astype(F32)

    @pl.when(i == 0)
    def _():
        prod_ref[...] = jnp.ones_like(prod_ref)
        sum_ref[...] = jnp.zeros_like(sum_ref)

    for j in range(hid // LANES):
        cols = [slice(g * hid + j * LANES, g * hid + (j + 1) * LANES) for g in range(3)]
        zf, zi, zc = [dot(normed, wg_ref[:, c]) + bias_ref[:, c] for c in cols]
        f = 1.0 / (1.0 + jnp.exp(-zf))
        g = 1.0 / (1.0 + jnp.exp(-zi))
        inv = 1.0 / (f + g)
        a = f * inv * jnp.concatenate([keep] * (LANES // 128), axis=1)
        b = g * inv
        here = cols[0]
        a_ref[:, here] = a
        b_ref[:, here] = b
        zc_ref[:, here] = zc
        fc_ref[:, here] = (1.0 - f).astype(BF16)
        ic_ref[:, here] = (1.0 - g).astype(BF16)
        u = b * zc
        prod = prod_ref[:, here]
        total = sum_ref[:, here]
        for r in range(steps):
            sl = slice(r * SUB, (r + 1) * SUB)
            prod = prod * a[sl]
            total = total * a[sl] + u[sl]
        prod_ref[:, here] = prod
        sum_ref[:, here] = total


def carry_kernel(devices, reverse, prod_ref, sum_ref, out_ref, mine, got, ssem, rsem):
    s = lax.axis_index("seq")
    b = lax.axis_index("batch")
    bar = pltpu.get_barrier_semaphore()
    others = [lax.rem(s + k, devices) for k in range(1, devices)]
    for o in others:
        pl.semaphore_signal(bar, inc=1, device_id=(o, b), device_id_type=MESH)
    order = list(range(SUB))[::-1] if reverse else list(range(SUB))
    width = prod_ref.shape[1]
    prod = jnp.ones((1, width), F32)
    total = jnp.zeros((1, width), F32)
    for c in order:
        prod = prod * prod_ref[c : c + 1, :]
        total = total * prod_ref[c : c + 1, :] + sum_ref[c : c + 1, :]
    mine[0:1, :] = prod
    mine[1:2, :] = total
    pl.semaphore_wait(bar, devices - 1)
    copies = []
    for k in range(1, devices):
        copies.append(
            pltpu.make_async_remote_copy(
                src_ref=mine, dst_ref=got.at[k - 1], send_sem=ssem.at[k - 1], recv_sem=rsem.at[k - 1],
                device_id=(others[k - 1], b), device_id_type=MESH,
            )
        )
        copies[-1].start()
    for c in copies:
        c.wait()
    state = jnp.zeros((1, width), F32)
    for turn in range(devices - 1):
        if reverse:
            owner = devices - 1 - turn
            ahead = owner > s
            back = lax.rem(s - owner + devices, devices)
        else:
            owner = turn
            ahead = owner < s
            back = lax.rem(s - owner + devices, devices)
        slot = jnp.where(back == 0, 0, back - 1)
        new = got[slot, 0:1, :] * state + got[slot, 1:2, :]
        state = jnp.where(ahead, new, state)
    for c in order:
        out_ref[c : c + 1, :] = state
        state = prod_ref[c : c + 1, :] * state + sum_ref[c : c + 1, :]


def carry(devices, reverse, prod, total):
    width = prod.shape[1]
    return pl.pallas_call(
        functools.partial(carry_kernel, devices, reverse),
        out_shape=jax.ShapeDtypeStruct((SUB, width), F32),
        in_specs=[pl.BlockSpec(memory_space=pltpu.VMEM)] * 2,
        out_specs=pl.BlockSpec(memory_space=pltpu.VMEM),
        scratch_shapes=[
            pltpu.VMEM((SUB, width), F32),
            pltpu.VMEM((devices - 1, SUB, width), F32),
            pltpu.SemaphoreType.DMA((devices - 1,)),
            pltpu.SemaphoreType.DMA((devices - 1,)),
        ],
        compiler_params=pltpu.CompilerParams(
            collective_id=1 + int(reverse), has_side_effects=True
        ),
    )(prod, total)


KA = 0.3275911 * 2.0**-0.5
ERF = [0.5 * c for c in (0.254829592, -0.284496736, 1.421413741, -1.453152027, 1.061405429)]
PHI = 0.3989422804014327


def gelu_parts(x):
    t = 1.0 / (1.0 + KA * jnp.abs(x))
    e = jnp.exp2(x * x * (-0.5 * 1.4426950408889634))
    poly = t * (ERF[0] + t * (ERF[1] + t * (ERF[2] + t * (ERF[3] + t * ERF[4]))))
    tail = poly * e
    phi = jnp.where(x >= 0.0, 1.0 - tail, tail)
    return x * phi, phi + x * (e * PHI)


def mlp_kernel(
    a_ref, b_ref, zc_ref, xp_ref, nt_ref, dy_ref, carry_ref, wo_ref, wu_ref, wd_ref,
    obias_ref, gain_ref, ubias_ref, dbias_ref,
    s_ref, acts_ref, gu_ref, rows_ref, turned_ref, gres_ref, gs_ref, result_ref,
    mu_ref, gdb_ref, gub_ref, ggain_ref, gob_ref,
    state, prod, perm,
):
    i = pl.program_id(0)
    steps = dy_ref.shape[1]

    @pl.when(i == 0)
    def _():
        state[...] = carry_ref[...]
        prod[...] = jnp.ones_like(prod)
        for ref in (mu_ref, gdb_ref, gub_ref, ggain_ref, gob_ref):
            ref[...] = jnp.zeros_like(ref)

    st = state[...]
    for r in range(steps):
        sl = slice(r * SUB, (r + 1) * SUB)
        st = a_ref[sl, :] * st + b_ref[sl, :] * zc_ref[sl, :]
        s_ref[sl, :] = st
    state[...] = st
    sb = s_ref[...].astype(BF16)
    ff = wu_ref.shape[1]
    acts_ref[:, ff:] = sb
    source = xp_ref[...].astype(F32)
    resid = source + dot(sb, wo_ref[...]) + obias_ref[...]
    scale = inv_rms(resid)
    n2 = (resid * scale * gain_ref[...]).astype(BF16)
    half = turned_ref.shape[2]
    turned_ref[0] = n2.T.reshape(-1, half, n2.shape[0])
    turned_ref[1] = nt_ref[...].reshape(-1, half, n2.shape[0])
    dy32 = to_steps(dy_ref[...], perm)
    dy = dy32.astype(BF16)
    rows_ref[0] = dy
    gdb_ref[...] += fold_rows(dy32)
    down = None
    gn2 = None
    for j in range(wu_ref.shape[1] // LANES):
        cols = slice(j * LANES, (j + 1) * LANES)
        upper = dot(n2, wu_ref[:, cols]) + ubias_ref[:, cols]
        act, slope = gelu_parts(upper)
        act = act.astype(BF16)
        acts_ref[:, cols] = act
        gact = dot_t(dy, wd_ref[cols, :])
        gu = (gact * slope).astype(BF16)
        gu_ref[:, cols] = gu
        gub_ref[:, cols] += fold_rows(gu.astype(F32))
        d = dot(act, wd_ref[cols, :])
        n = dot_t(gu, wu_ref[:, cols])
        down = d if down is None else down + d
        gn2 = n if gn2 is None else gn2 + n
    result = resid + down + dbias_ref[...]
    result_ref[...] = from_steps(result, perm, steps).astype(BF16)
    w = gn2 * gain_ref[...]
    ggain_ref[...] += fold_rows(gn2 * resid * scale)
    gres = dy32 + scale * w - resid * (scale * scale * scale) * jnp.mean(
        w * resid, axis=-1, keepdims=True
    )
    gres_ref[...] = gres
    gr = gres.astype(BF16)
    gob_ref[...] += fold_rows(gr.astype(F32))
    rows_ref[1] = gr
    gs = dot_t(gr, wo_ref[...])
    gs_ref[...] = gs
    pr = prod[...]
    mu = mu_ref[...]
    for r in range(steps):
        sl = slice(r * SUB, (r + 1) * SUB)
        pr = pr * a_ref[sl, :]
        mu = mu + pr * gs[sl, :]
    prod[...] = pr
    mu_ref[...] = mu


def bits_of(size):
    w = 1
    out = []
    while w < size:
        out.append(w); w *= 2
    return out

class Plan:
    def __init__(self, seq, batch, rows):
        sb = [("seq", w) for w in bits_of(seq)]
        bb = [("batch", w) for w in bits_of(batch)][1:]
        self.orders = [sb + bb, sb[::-1] + bb, bb[:1] + sb + bb[1:]]
        self.K = len(sb) + len(bb)
        self.rows = rows
        self.sizes = [rows]
        self.halve = []
        for k in range(self.K + 1):
            h = self.sizes[-1] >= 16
            self.halve.append(h)
            self.sizes.append(self.sizes[-1] // 2 if h else self.sizes[-1])
        self.stages = 2 * (self.K + 1)
        self.colors = len(self.orders)
        self.base = []
        tot = 0
        for k in range(self.K + 1):
            self.base.append(tot); tot += self.sizes[k + 1]
        self.recv_rows = tot

def pick(color, values):
    out = values[-1]
    for i in range(len(values) - 1):
        out = jnp.where(color == i, values[i], out)
    return out

def step_info(plan, k, color):
    s = lax.axis_index("seq"); b = lax.axis_index("batch")
    if k == 0:
        return b % 2, (s, flip(b, 1))
    mine, ps, pb = [], [], []
    for order in plan.orders:
        axis, w = order[k - 1]
        if axis == "seq":
            mine.append((s // w) % 2); ps.append(flip(s, w)); pb.append(b)
        else:
            mine.append((b // w) % 2); ps.append(s); pb.append(flip(b, w))
    return pick(color, mine), (pick(color, ps), pick(color, pb))

def offsets(plan, c, color, upto):
    off = c * plan.rows
    for k in range(upto):
        if plan.halve[k]:
            bit, _ = step_info(plan, k, color)
            off = off + bit * plan.sizes[k + 1]
    return pl.multiple_of(off, 8)

def copy_of(plan, acc, recv, ssem, rsem, c, j):
    color = c % plan.colors
    slot = color * 2 + (c // plan.colors) % 2
    K = plan.K
    if j <= K:
        k = j
        bit, dev = step_info(plan, k, color)
        n = plan.sizes[k + 1]
        base = offsets(plan, c, color, k)
        src = base + (1 - bit) * n if plan.halve[k] else base
        return pltpu.make_async_remote_copy(
            src_ref=acc.at[pl.ds(pl.multiple_of(src, 8), n)], dst_ref=recv.at[slot, pl.ds(plan.base[k], n)],
            send_sem=ssem.at[slot, j], recv_sem=rsem.at[slot, j], device_id=dev, device_id_type=MESH)
    k = 2 * K + 1 - j
    if not plan.halve[k]:
        return None
    bit, dev = step_info(plan, k, color)
    n = plan.sizes[k + 1]
    mine = offsets(plan, c, color, k + 1)
    return pltpu.make_async_remote_copy(
        src_ref=acc.at[pl.ds(mine, n)], dst_ref=acc.at[pl.ds(mine, n)],
        send_sem=ssem.at[slot, j], recv_sem=rsem.at[slot, j], device_id=dev, device_id_type=MESH)

def finish(plan, acc, recv, ssem, rsem, free, c, j):
    cp = copy_of(plan, acc, recv, ssem, rsem, c, j)
    if cp is None:
        return
    cp.wait()
    if j <= plan.K:
        color = c % plan.colors
        slot = color * 2 + (c // plan.colors) % 2
        n = plan.sizes[j + 1]
        if plan.halve[j]:
            _, dev = step_info(plan, j, color)
            pl.semaphore_signal(free.at[slot, j], inc=1, device_id=dev, device_id_type=MESH)
        off = offsets(plan, c, color, j + 1)
        acc[pl.ds(off, n), :] = acc[pl.ds(off, n), :] + recv[slot, pl.ds(plan.base[j], n), :]

def tick(plan, nchunks, acc, recv, ssem, rsem, free, t, done, L=1):
    for j in range(plan.stages, -1, -1):
        c = t - L * j
        @pl.when((c >= 0) & (c < nchunks))
        def _():
            if j > 0:
                finish(plan, acc, recv, ssem, rsem, free, c, j - 1)
            if j < plan.stages:
                cp = copy_of(plan, acc, recv, ssem, rsem, c, j)
                if cp is not None:
                    if j > plan.K:
                        color = c % plan.colors
                        slot = color * 2 + (c // plan.colors) % 2
                        pl.semaphore_wait(free.at[slot, 2 * plan.K + 1 - j], 1)
                    cp.start()
            else:
                done(c)


def small_copy(plan, small, got, ssem, rsem, k):
    _, dev = step_info(plan, k, 0)
    return pltpu.make_async_remote_copy(
        src_ref=small, dst_ref=got.at[k], send_sem=ssem.at[k], recv_sem=rsem.at[k],
        device_id=dev, device_id_type=MESH)


def tdot(a, b):
    return lax.dot_general(a, b, (((0,), (0,)), ((), ())), preferred_element_type=F32)


class Work:
    def __init__(self, d, hid, ff, rows, tiles, lag, seq, batch):
        self.rows = rows
        self.halves = d // rows
        self.down = ff // rows
        self.up = ff // d * self.halves
        self.out = hid // rows
        self.gates = 3 * hid // d * self.halves
        self.at_up = self.down
        self.at_out = self.at_up + self.up
        self.at_gates = self.at_out + self.out
        self.chunks = self.at_gates + self.gates
        self.plan = Plan(seq, batch, rows)
        self.lag = lag
        self.tiles = tiles
        self.first_tile = 2
        self.small_at = max(self.first_tile + tiles, self.at_gates)
        self.ticks = max(self.chunks + lag * self.plan.stages, self.small_at + lag * (self.plan.K + 1)) + 1
        self.seq = seq


def back_tile(i, a_ref, b_ref, zc_ref, fc_ref, ic_ref, s_ref, gs_ref, xp_ref, gres_ref, wg_ref, gain_ref,
              gin_ref, gm, ggb, ggain, state, perm):
    steps = gin_ref.shape[1]
    rows = steps * SUB
    hid = wg_ref.shape[1] // 3
    width = gm.shape[2]
    at = pl.ds(pl.multiple_of(gm.shape[1] - (i + 1) * rows, rows), rows)
    gn = None
    for j in range(hid // LANES):
        here = slice(j * LANES, (j + 1) * LANES)
        mu = state[:, here]
        lams = [None] * steps
        for r in range(steps - 1, -1, -1):
            sl = slice(r * SUB, (r + 1) * SUB)
            lams[r] = gs_ref[sl, here] + mu
            mu = a_ref[sl, here] * lams[r]
        state[:, here] = mu
        lam = jnp.concatenate(lams, axis=0)
        gzc = lam * b_ref[:, here]
        big = gzc * (s_ref[:, here] - zc_ref[:, here])
        parts = (
            (big * fc_ref[:, here].astype(F32)).astype(BF16),
            (-big * ic_ref[:, here].astype(F32)).astype(BF16),
            gzc.astype(BF16),
        )
        for g in range(3):
            first = g * hid + j * LANES
            cols = slice(first, first + LANES)
            gm[first // width, at, first % width : first % width + LANES] = parts[g]
            ggb[:, cols] += fold_rows(parts[g].astype(F32))
            n = dot_t(parts[g], wg_ref[:, cols])
            gn = n if gn is None else gn + n
    source = xp_ref[...].astype(F32)
    scale = inv_rms(source)
    w = gn * gain_ref[...]
    ggain[...] += fold_rows(gn * source * scale)
    gin = gres_ref[...] + scale * w - source * (scale * scale * scale) * jnp.mean(
        w * source, axis=-1, keepdims=True
    )
    gin_ref[...] = from_steps(gin, perm, steps)


def sum_kernel(
    work,
    prod_ref, mu_ref, gdb_ref, gub_ref, ggain2_ref, gob_ref, gain_ref, wg_ref,
    acts_ref, rows_ref, turned_ref, gu_ref,
    a_ref, b_ref, zc_ref, fc_ref, ic_ref, s_ref, gs_ref, xp_ref, gres_ref,
    gin_ref, small_ref, down_hbm, up_hbm, out_hbm, gates_hbm,
    acc, recv, gm, state, ggb, ggain, perm, small, got, mine, theirs,
    ssem, rsem, free, osem, s2sem, r2sem, csem, crsem,
):
    t = pl.program_id(0)
    plan = work.plan
    rows = work.rows
    s = lax.axis_index("seq")
    b = lax.axis_index("batch")
    others = [lax.rem(s + k, work.seq) for k in range(1, work.seq)]
    ends = [
        pltpu.make_async_remote_copy(
            src_ref=mine, dst_ref=theirs.at[k], send_sem=csem.at[k], recv_sem=crsem.at[k],
            device_id=(others[k], b), device_id_type=MESH,
        )
        for k in range(work.seq - 1)
    ]
    width = prod_ref.shape[1]

    @pl.when(t == 0)
    def _():
        who = [(s, flip(b, 1))] + [(o, b) for o in others]
        who += [(s, flip(b, w)) for axis, w in plan.orders[0] if axis == "batch"]
        bar = pltpu.get_barrier_semaphore()
        for p in who:
            pl.semaphore_signal(bar, inc=1, device_id=p, device_id_type=MESH)
        prod = jnp.ones((1, width), F32)
        total = jnp.zeros((1, width), F32)
        for c in range(SUB - 1, -1, -1):
            prod = prod * prod_ref[c : c + 1, :]
            total = total * prod_ref[c : c + 1, :] + mu_ref[c : c + 1, :]
        mine[0:1, :] = prod
        mine[1:2, :] = total
        ggb[...] = jnp.zeros_like(ggb)
        ggain[...] = jnp.zeros_like(ggain)
        pl.semaphore_wait(bar, len(who))
        for c in ends:
            c.start()

    @pl.when(t == work.first_tile)
    def _():
        for c in ends:
            c.wait()
        now = jnp.zeros((1, width), F32)
        for owner in range(work.seq - 1, 0, -1):
            back = lax.rem(s - owner + work.seq, work.seq)
            slot = jnp.where(back == 0, 0, back - 1)
            new = theirs[slot, 0:1, :] * now + theirs[slot, 1:2, :]
            now = jnp.where(owner > s, new, now)
        for c in range(SUB - 1, -1, -1):
            state[c : c + 1, :] = now
            now = prod_ref[c : c + 1, :] * now + mu_ref[c : c + 1, :]

    def put(value):
        acc[pl.ds(pl.multiple_of(t * rows, rows), rows), :] = value

    @pl.when((t < work.at_up) | ((t >= work.at_out) & (t < work.at_gates)))
    def _():
        put(tdot(acts_ref[...], rows_ref[0]))

    @pl.when((t >= work.at_up) & (t < work.at_out))
    def _():
        put(dot(turned_ref[0], gu_ref[...]))

    @pl.when((t >= work.at_gates) & (t < work.chunks))
    def _():
        put(dot(turned_ref[0], gm[(t - work.at_gates) // work.halves]))

    @pl.when(t == work.small_at)
    def _():
        line = 0
        for v in (ggain, ggb, gob_ref, ggain2_ref, gub_ref, gdb_ref):
            total = jnp.sum(v[...], axis=0, keepdims=True)
            for k in range(total.shape[1] // LANES):
                small[line : line + 1, :] = total[:, k * LANES : (k + 1) * LANES]
                line += 1
        if line < small.shape[0]:
            small[line:, :] = jnp.zeros((small.shape[0] - line, LANES), F32)

    for k in range(plan.K + 2):
        @pl.when(t == work.small_at + k * work.lag)
        def _():
            if k > 0:
                small_copy(plan, small, got, s2sem, r2sem, k - 1).wait()
                small[...] = small[...] + got[k - 1]
            if k <= plan.K:
                small_copy(plan, small, got, s2sem, r2sem, k).start()

    d = rows * work.halves

    def to_result(c, action):
        src = acc.at[pl.ds(pl.multiple_of(c * rows, rows), rows)]

        def case(first, count, ref, tall):
            @pl.when((c >= first) & (c < first + count))
            def _():
                k = c - first
                if tall:
                    dst = ref.at[pl.ds(pl.multiple_of(k * rows, rows), rows)]
                else:
                    dst = ref.at[
                        pl.ds(pl.multiple_of((k % work.halves) * rows, rows), rows),
                        pl.ds(pl.multiple_of((k // work.halves) * d, d), d),
                    ]
                action(pltpu.make_async_copy(src, dst, osem.at[c]))

        case(0, work.down, down_hbm, True)
        case(work.at_up, work.up, up_hbm, False)
        case(work.at_out, work.out, out_hbm, True)
        case(work.at_gates, work.gates, gates_hbm, False)

    tick(plan, work.chunks, acc, recv, ssem, rsem, free, t,
         lambda c: to_result(c, lambda copy: copy.start()), work.lag)

    i = t - work.first_tile

    @pl.when((i >= 0) & (i < work.tiles))
    def _():
        back_tile(i, a_ref, b_ref, zc_ref, fc_ref, ic_ref, s_ref, gs_ref, xp_ref, gres_ref, wg_ref,
                  gain_ref, gin_ref, gm, ggb, ggain, state, perm)

    @pl.when(t == work.ticks - 1)
    def _():
        small_ref[...] = small[...]

        def wait(c, _):
            to_result(c, lambda copy: copy.wait())
            return 0

        lax.fori_loop(0, work.chunks, wait, 0)


def full(shape):
    return pl.BlockSpec(shape, lambda i: (0,) * len(shape), pipeline_mode=pl.Buffered(1))


def held(shape):
    return pl.BlockSpec(shape, lambda i: (0,) * len(shape))


def per_device(seq, batch, inputs, cotangent, short_lengths, long_lengths, norm_gain, w_gates, gate_bias, w_out,
               out_bias, mlp_gain, w_up, up_bias, w_down, down_bias, tile=256, back=128):
    tok, d = inputs.shape[1:]
    hid = w_out.shape[0]
    ff = w_up.shape[1]
    piece = tok // SUB
    steps = tile // SUB
    grid = tok // tile
    halves = 2
    x = inputs.reshape(SUB, piece, d)
    dy = cotangent.reshape(SUB, piece, d)
    gain1 = norm_gain.reshape(1, d)
    gain2 = mlp_gain.reshape(1, d)
    sds = jax.ShapeDtypeStruct
    rows = lambda n: pl.BlockSpec((tile, n), lambda i: (i, 0))
    natural = pl.BlockSpec((SUB, steps, d), lambda i: (0, i, 0))
    turned = pl.BlockSpec((d, tile), lambda i: (0, i))
    params = pltpu.CompilerParams(
        dimension_semantics=("arbitrary",), vmem_limit_bytes=56 << 20
    )
    a, b, zc, fc, ic, xp, nt, prod, total = pl.pallas_call(
        functools.partial(gates_kernel, piece),
        grid=(grid,),
        in_specs=[
            pl.BlockSpec(memory_space=pltpu.SMEM), pl.BlockSpec(memory_space=pltpu.SMEM),
            natural, full((1, d)), full((d, 3 * hid)), full((1, 3 * hid)),
        ],
        out_specs=[rows(hid)] * 5 + [rows(d), turned, held((SUB, hid)), held((SUB, hid))],
        out_shape=[sds((tok, hid), F32)] * 3 + [sds((tok, hid), BF16)] * 2
        + [sds((tok, d), BF16), sds((d, tok), BF16), sds((SUB, hid), F32), sds((SUB, hid), F32)],
        scratch_shapes=[pltpu.VMEM((d // 128, tile, 128), F32)],
        compiler_params=params,
    )(short_lengths, long_lengths, x, gain1, w_gates, gate_bias.reshape(1, 3 * hid))

    enter = carry(seq, False, prod, total)

    outs = pl.pallas_call(
        mlp_kernel,
        grid=(grid,),
        in_specs=[rows(hid)] * 3 + [rows(d), turned, natural, full((SUB, hid)), full((hid, d)), full((d, ff)), full((ff, d)),
                  full((1, d)), full((1, d)), full((1, ff)), full((1, d))],
        out_specs=[rows(hid), rows(ff + hid), rows(ff), pl.BlockSpec((2, tile, d), lambda i: (0, i, 0)),
                   pl.BlockSpec((2, halves, d // halves, tile), lambda i: (0, 0, 0, i)), rows(d), rows(hid), natural,
                   held((SUB, hid)), held((SUB, d)), held((SUB, ff)), held((SUB, d)), held((SUB, d))],
        out_shape=[sds((tok, hid), F32), sds((tok, ff + hid), BF16), sds((tok, ff), BF16), sds((2, tok, d), BF16),
                   sds((2, halves, d // halves, tok), BF16), sds((tok, d), F32),
                   sds((tok, hid), F32), sds((SUB, piece, d), BF16),
                   sds((SUB, hid), F32), sds((SUB, d), F32), sds((SUB, ff), F32), sds((SUB, d), F32), sds((SUB, d), F32)],
        scratch_shapes=[pltpu.VMEM((SUB, hid), F32), pltpu.VMEM((SUB, hid), F32), pltpu.VMEM((d // 128, tile, 128), F32)],
        compiler_params=params,
    )(a, b, zc, xp, nt, dy, enter, w_out, w_up, w_down, out_bias.reshape(1, d), gain2, up_bias.reshape(1, ff),
      down_bias.reshape(1, d))
    s, acts, gu, pairs, turns, gres, gs, result, mu, gdb, gub, ggain2, gob = outs

    turns = turns.reshape(2 * halves, d // halves, tok)
    work = Work(d, hid, ff, d // halves, tok // back, LAG, seq, batch)
    plan = work.plan
    slots = plan.colors * 2
    bsteps = back // SUB
    lines = -(-(4 * d + 3 * hid + ff) // (8 * LANES)) * 8

    def at_tile(t):
        return work.tiles - 1 - jnp.clip(t - work.first_tile, 0, work.tiles - 1)

    btile = lambda n: pl.BlockSpec((back, n), lambda t: (at_tile(t), 0))
    any_space = pl.BlockSpec(memory_space=pl.ANY)

    def acts_at(t):
        late = jnp.clip(t - work.up, work.down, work.down + work.out - 1)
        return (0, jnp.where(t < work.down, t, late))

    def turned_at(t):
        up = jnp.clip(t - work.at_up, 0, work.up - 1) % halves
        gates = halves + jnp.clip(t - work.at_gates, 0, work.gates - 1) % halves
        return (jnp.where(t < work.at_out, up, gates), 0, 0)

    gin, small, g_down, g_up, g_out, g_gates = pl.pallas_call(
        functools.partial(sum_kernel, work),
        grid=(work.ticks,),
        in_specs=[full((SUB, hid)), full((SUB, hid)), full((SUB, d)), full((SUB, ff)), full((SUB, d)), full((SUB, d)),
                  full((1, d)), full((d, 3 * hid)),
                  pl.BlockSpec((tok, work.rows), acts_at),
                  pl.BlockSpec((1, tok, d), lambda t: (jnp.where(t < work.at_up, 0, 1), 0, 0)),
                  pl.BlockSpec((1, work.rows, tok), turned_at),
                  pl.BlockSpec((tok, d), lambda t: (0, jnp.clip(t - work.at_up, 0, work.up - 1) // halves))]
        + [btile(hid)] * 7 + [btile(d)] * 2,
        out_specs=[pl.BlockSpec((SUB, bsteps, d), lambda t: (0, at_tile(t), 0)), held((lines, LANES))] + [any_space] * 4,
        out_shape=[sds((SUB, piece, d), F32), sds((lines, LANES), F32), sds((ff, d), F32), sds((d, ff), F32),
                   sds((hid, d), F32), sds((d, 3 * hid), F32)],
        scratch_shapes=[
            pltpu.VMEM((work.chunks * work.rows, d), F32),
            pltpu.VMEM((slots, plan.recv_rows, d), F32),
            pltpu.VMEM((3 * hid // d, tok, d), BF16),
            pltpu.VMEM((SUB, hid), F32),
            pltpu.VMEM((SUB, 3 * hid), F32),
            pltpu.VMEM((SUB, d), F32),
            pltpu.VMEM((d // 128, back, 128), F32),
            pltpu.VMEM((lines, LANES), F32),
            pltpu.VMEM((plan.K + 1, lines, LANES), F32),
            pltpu.VMEM((SUB, hid), F32),
            pltpu.VMEM((seq - 1, SUB, hid), F32),
            pltpu.SemaphoreType.DMA((slots, plan.stages)),
            pltpu.SemaphoreType.DMA((slots, plan.stages)),
            pltpu.SemaphoreType.REGULAR((slots, plan.K + 1)),
            pltpu.SemaphoreType.DMA((work.chunks,)),
            pltpu.SemaphoreType.DMA((plan.K + 1,)),
            pltpu.SemaphoreType.DMA((plan.K + 1,)),
            pltpu.SemaphoreType.DMA((seq - 1,)),
            pltpu.SemaphoreType.DMA((seq - 1,)),
        ],
        compiler_params=pltpu.CompilerParams(
            dimension_semantics=("arbitrary",), collective_id=0, has_side_effects=True, vmem_limit_bytes=62 << 20
        ),
    )(prod, mu, gdb, gub, ggain2, gob, gain1, w_gates, acts, pairs, turns, gu,
      a, b, zc, fc, ic, s, gs, xp, gres)
    small = small.reshape(-1)
    vecs = []
    at = 0
    for n in (d, 3 * hid, d, d, ff, d):
        vecs.append(small[at : at + n])
        at += n
    ggain1, ggb, gob, ggain2, gub, gdb = vecs
    return (result.reshape(inputs.shape), gin.reshape(inputs.shape), ggain1, g_gates, ggb, g_out, gob,
            ggain2, g_up, gub, g_down, gdb)


def solution(mesh):
    rows = P("batch", "seq", None)
    return jax.shard_map(
        functools.partial(per_device, mesh.shape["seq"], mesh.shape["batch"]),
        mesh=mesh,
        in_specs=(rows, rows) + (P(),) * 12,
        out_specs=(rows, rows) + (P(),) * 10,
        check_vma=False,
    )
```

```python
import functools

import jax
import jax.numpy as jnp
from jax import lax
from jax.experimental import pallas as pl
from jax.experimental.pallas import tpu as pltpu
from jax.sharding import PartitionSpec as P

MESH = pl.DeviceIdType.MESH
F32 = jnp.float32
BF16 = jnp.bfloat16
epsilon = 1e-06
SUB = 8
LANES = 256
LAG = 3


def flip(v, w):
    return v + w - 2 * w * ((v // w) % 2)


def dot(a, b):
    return jnp.dot(a, b, preferred_element_type=F32)


def dot_t(a, b):
    return lax.dot_general(a, b, (((1,), (1,)), ((), ())), preferred_element_type=F32)


def fold_rows(v):
    return jnp.sum(v.reshape(v.shape[0] // SUB, SUB, v.shape[1]), axis=0)


def inv_rms(v):
    return lax.rsqrt(jnp.mean(v * v, axis=-1, keepdims=True) + epsilon)


def to_steps(block, scratch):
    pieces, steps, n = block.shape
    flat = block.astype(F32).reshape(pieces * steps, n)
    parts = []
    for k in range(n // 128):
        for c in range(pieces):
            scratch[k, c * (steps + SUB) : c * (steps + SUB) + steps, :] = flat[
                c * steps : (c + 1) * steps, k * 128 : (k + 1) * 128
            ]
        parts.append(
            jnp.concatenate(
                [scratch[k, pl.ds(r, pieces, stride=steps + SUB), :] for r in range(steps)], axis=0
            )
        )
    return jnp.concatenate(parts, axis=1)


def from_steps(value, scratch, steps):
    n = value.shape[1]
    parts = []
    for k in range(n // 128):
        for r in range(steps):
            scratch[k, pl.ds(r, SUB, stride=steps + SUB), :] = value[
                r * SUB : (r + 1) * SUB, k * 128 : (k + 1) * 128
            ]
        parts.append(
            jnp.concatenate(
                [scratch[k, c * (steps + SUB) : c * (steps + SUB) + steps, :] for c in range(SUB)], axis=0
            )
        )
    return jnp.concatenate(parts, axis=1).reshape(SUB, steps, n)


class Ends:
    def __init__(self, devices, mine, theirs, ssem, rsem):
        self.devices = devices
        self.mine = mine
        self.theirs = theirs
        self.at = lax.axis_index("seq")
        self.group = lax.axis_index("batch")
        self.others = [lax.rem(self.at + k, devices) for k in range(1, devices)]
        self.copies = [
            pltpu.make_async_remote_copy(
                src_ref=mine, dst_ref=theirs.at[k], send_sem=ssem.at[k], recv_sem=rsem.at[k],
                device_id=(other, self.group), device_id_type=MESH,
            )
            for k, other in enumerate(self.others)
        ]

    def greet(self):
        bar = pltpu.get_barrier_semaphore()
        for other in self.others:
            pl.semaphore_signal(bar, inc=1, device_id=(other, self.group), device_id_type=MESH)

    def send(self, prod_ref, sum_ref, reverse):
        width = prod_ref.shape[1]
        prod = jnp.ones((1, width), F32)
        total = jnp.zeros((1, width), F32)
        for c in range(SUB - 1, -1, -1) if reverse else range(SUB):
            prod = prod * prod_ref[c : c + 1, :]
            total = total * prod_ref[c : c + 1, :] + sum_ref[c : c + 1, :]
        self.mine[0:1, :] = prod
        self.mine[1:2, :] = total
        for copy in self.copies:
            copy.start()

    def receive(self, prod_ref, sum_ref, out_ref, reverse):
        for copy in self.copies:
            copy.wait()
        n = self.devices
        now = jnp.zeros((1, prod_ref.shape[1]), F32)
        for owner in range(n - 1, 0, -1) if reverse else range(n - 1):
            back = lax.rem(self.at - owner + n, n)
            slot = jnp.where(back == 0, 0, back - 1)
            new = self.theirs[slot, 0:1, :] * now + self.theirs[slot, 1:2, :]
            now = jnp.where(owner > self.at if reverse else owner < self.at, new, now)
        for c in range(SUB - 1, -1, -1) if reverse else range(SUB):
            out_ref[c : c + 1, :] = now
            now = prod_ref[c : c + 1, :] * now + sum_ref[c : c + 1, :]


def ends_scratch(devices, width):
    return [
        pltpu.VMEM((SUB, width), F32),
        pltpu.VMEM((devices - 1, SUB, width), F32),
        pltpu.SemaphoreType.DMA((devices - 1,)),
        pltpu.SemaphoreType.DMA((devices - 1,)),
    ]


def gates_kernel(
    piece, devices, short_ref, long_ref, x_ref, gain_ref, wg_ref, bias_ref,
    a_ref, b_ref, zc_ref, fc_ref, ic_ref, xp_ref, nt_ref, prod_ref, enter_ref,
    perm, sum_ref, mine, theirs, ssem, rsem,
):
    i = pl.program_id(0)
    ends = Ends(devices, mine, theirs, ssem, rsem)
    steps = x_ref.shape[1]
    rows = steps * SUB
    hid = wg_ref.shape[1] // 3
    source = to_steps(x_ref[...], perm)
    xp_ref[...] = source.astype(BF16)
    normed = (source * inv_rms(source) * gain_ref[...]).astype(BF16)
    nt_ref[...] = normed.T

    group = lax.axis_index("batch")
    half = short_ref.shape[0]
    first = lax.axis_index("seq") * piece * SUB
    row = lax.broadcasted_iota(jnp.int32, (rows, 128), 0)
    pos = first + (row % SUB) * piece + i * steps + row // SUB
    short = group < half
    srow = jnp.minimum(group, half - 1)
    lrow = jnp.maximum(group - half, 0)
    begins = jnp.zeros((rows, 128), jnp.bool_)
    at = jnp.int32(0)
    for k in range(short_ref.shape[1]):
        begins = begins | (pos == jnp.where(short, at, -1))
        at = at + short_ref[srow, k]
    at = jnp.int32(0)
    for k in range(long_ref.shape[1]):
        begins = begins | (pos == jnp.where(short, -1, at))
        at = at + long_ref[lrow, k]
    keep = jnp.where(begins, 0.0, 1.0).astype(F32)

    @pl.when(i == 0)
    def _():
        ends.greet()
        prod_ref[...] = jnp.ones_like(prod_ref)
        sum_ref[...] = jnp.zeros_like(sum_ref)

    for j in range(hid // LANES):
        cols = [slice(g * hid + j * LANES, g * hid + (j + 1) * LANES) for g in range(3)]
        zf, zi, zc = [dot(normed, wg_ref[:, c]) + bias_ref[:, c] for c in cols]
        f = 1.0 / (1.0 + jnp.exp(-zf))
        g = 1.0 / (1.0 + jnp.exp(-zi))
        inv = 1.0 / (f + g)
        a = f * inv * jnp.concatenate([keep] * (LANES // 128), axis=1)
        b = g * inv
        here = cols[0]
        a_ref[:, here] = a
        b_ref[:, here] = b
        zc_ref[:, here] = zc
        fc_ref[:, here] = (1.0 - f).astype(BF16)
        ic_ref[:, here] = (1.0 - g).astype(BF16)
        u = b * zc
        prod = prod_ref[:, here]
        total = sum_ref[:, here]
        for r in range(steps):
            sl = slice(r * SUB, (r + 1) * SUB)
            prod = prod * a[sl]
            total = total * a[sl] + u[sl]
        prod_ref[:, here] = prod
        sum_ref[:, here] = total


    @pl.when(i == pl.num_programs(0) - 1)
    def _():
        pl.semaphore_wait(pltpu.get_barrier_semaphore(), devices - 1)
        ends.send(prod_ref, sum_ref, False)
        ends.receive(prod_ref, sum_ref, enter_ref, False)


KA = 0.3275911 * 2.0**-0.5
ERF = [0.5 * c for c in (0.254829592, -0.284496736, 1.421413741, -1.453152027, 1.061405429)]
PHI = 0.3989422804014327


def gelu_parts(x):
    t = 1.0 / (1.0 + KA * jnp.abs(x))
    e = jnp.exp2(x * x * (-0.5 * 1.4426950408889634))
    poly = t * (ERF[0] + t * (ERF[1] + t * (ERF[2] + t * (ERF[3] + t * ERF[4]))))
    tail = poly * e
    phi = jnp.where(x >= 0.0, 1.0 - tail, tail)
    return x * phi, phi + x * (e * PHI)


def mlp_kernel(
    a_ref, b_ref, zc_ref, xp_ref, nt_ref, dy_ref, carry_ref, wo_ref, wu_ref, wd_ref,
    obias_ref, gain_ref, ubias_ref, dbias_ref,
    s_ref, acts_ref, gu_ref, rows_ref, turned_ref, gres_ref, gs_ref, result_ref,
    mu_ref, gdb_ref, gub_ref, ggain_ref, gob_ref,
    state, prod, perm,
):
    i = pl.program_id(0)
    steps = dy_ref.shape[1]

    @pl.when(i == 0)
    def _():
        state[...] = carry_ref[...]
        prod[...] = jnp.ones_like(prod)
        for ref in (mu_ref, gdb_ref, gub_ref, ggain_ref, gob_ref):
            ref[...] = jnp.zeros_like(ref)

    st = state[...]
    for r in range(steps):
        sl = slice(r * SUB, (r + 1) * SUB)
        st = a_ref[sl, :] * st + b_ref[sl, :] * zc_ref[sl, :]
        s_ref[sl, :] = st
    state[...] = st
    sb = s_ref[...].astype(BF16)
    ff = wu_ref.shape[1]
    acts_ref[:, ff:] = sb
    source = xp_ref[...].astype(F32)
    resid = source + dot(sb, wo_ref[...]) + obias_ref[...]
    scale = inv_rms(resid)
    n2 = (resid * scale * gain_ref[...]).astype(BF16)
    half = turned_ref.shape[2]
    turned_ref[0] = n2.T.reshape(-1, half, n2.shape[0])
    turned_ref[1] = nt_ref[...].reshape(-1, half, n2.shape[0])
    dy32 = to_steps(dy_ref[...], perm)
    dy = dy32.astype(BF16)
    rows_ref[0] = dy
    gdb_ref[...] += fold_rows(dy32)
    down = None
    gn2 = None
    for j in range(wu_ref.shape[1] // LANES):
        cols = slice(j * LANES, (j + 1) * LANES)
        upper = dot(n2, wu_ref[:, cols]) + ubias_ref[:, cols]
        act, slope = gelu_parts(upper)
        act = act.astype(BF16)
        acts_ref[:, cols] = act
        gact = dot_t(dy, wd_ref[cols, :])
        gu = (gact * slope).astype(BF16)
        gu_ref[:, cols] = gu
        gub_ref[:, cols] += fold_rows(gu.astype(F32))
    down = dot(acts_ref[:, :ff], wd_ref[...])
    gn2 = dot_t(gu_ref[...], wu_ref[...])
    result = resid + down + dbias_ref[...]
    result_ref[...] = from_steps(result, perm, steps).astype(BF16)
    w = gn2 * gain_ref[...]
    ggain_ref[...] += fold_rows(gn2 * resid * scale)
    gres = dy32 + scale * w - resid * (scale * scale * scale) * jnp.mean(
        w * resid, axis=-1, keepdims=True
    )
    gres_ref[...] = gres
    gr = gres.astype(BF16)
    gob_ref[...] += fold_rows(gr.astype(F32))
    rows_ref[1] = gr
    gs = dot_t(gr, wo_ref[...])
    gs_ref[...] = gs
    pr = prod[...]
    mu = mu_ref[...]
    for r in range(steps):
        sl = slice(r * SUB, (r + 1) * SUB)
        pr = pr * a_ref[sl, :]
        mu = mu + pr * gs[sl, :]
    prod[...] = pr
    mu_ref[...] = mu


def bits_of(size):
    w = 1
    out = []
    while w < size:
        out.append(w); w *= 2
    return out

def stage_ticks(j, stages):
    return LAG


class Plan:
    def __init__(self, seq, batch, rows):
        sb = [("seq", w) for w in bits_of(seq)]
        bb = [("batch", w) for w in bits_of(batch)][1:]
        self.orders = [sb + bb, sb[::-1] + bb, bb[:1] + sb + bb[1:], sb + bb, sb[::-1] + bb, bb[:1] + sb[::-1] + bb[1:]]
        self.K = len(sb) + len(bb)
        self.rows = rows
        self.sizes = [rows]
        self.halve = []
        for k in range(self.K + 1):
            h = self.sizes[-1] >= 16
            self.halve.append(h)
            self.sizes.append(self.sizes[-1] // 2 if h else self.sizes[-1])
        self.stages = 2 * (self.K + 1)
        self.colors = len(self.orders)
        self.begins = [0]
        for j in range(self.stages):
            self.begins.append(self.begins[-1] + stage_ticks(j, self.stages))
        self.base = []
        tot = 0
        for k in range(self.K + 1):
            self.base.append(tot); tot += self.sizes[k + 1]
        self.recv_rows = tot

def pick(color, values):
    out = values[-1]
    for i in range(len(values) - 1):
        out = jnp.where(color == i, values[i], out)
    return out

def step_info(plan, k, color):
    s = lax.axis_index("seq"); b = lax.axis_index("batch")
    if k == 0:
        return b % 2, (s, flip(b, 1))
    mine, ps, pb = [], [], []
    for order in plan.orders:
        axis, w = order[k - 1]
        if axis == "seq":
            mine.append((s // w) % 2); ps.append(flip(s, w)); pb.append(b)
        else:
            mine.append((b // w) % 2); ps.append(s); pb.append(flip(b, w))
    return pick(color, mine), (pick(color, ps), pick(color, pb))

def offsets(plan, c, color, upto):
    off = c * plan.rows
    for k in range(upto):
        if plan.halve[k]:
            bit, _ = step_info(plan, k, color)
            off = off + bit * plan.sizes[k + 1]
    return pl.multiple_of(off, 8)

def copy_of(plan, acc, recv, ssem, rsem, c, j):
    color = c % plan.colors
    slot = color * 2 + (c // plan.colors) % 2
    K = plan.K
    if j <= K:
        k = j
        bit, dev = step_info(plan, k, color)
        n = plan.sizes[k + 1]
        base = offsets(plan, c, color, k)
        src = base + (1 - bit) * n if plan.halve[k] else base
        return pltpu.make_async_remote_copy(
            src_ref=acc.at[pl.ds(pl.multiple_of(src, 8), n)], dst_ref=recv.at[slot, pl.ds(plan.base[k], n)],
            send_sem=ssem.at[slot, j], recv_sem=rsem.at[slot, j], device_id=dev, device_id_type=MESH)
    k = 2 * K + 1 - j
    if not plan.halve[k]:
        return None
    bit, dev = step_info(plan, k, color)
    n = plan.sizes[k + 1]
    mine = offsets(plan, c, color, k + 1)
    return pltpu.make_async_remote_copy(
        src_ref=acc.at[pl.ds(mine, n)], dst_ref=acc.at[pl.ds(mine, n)],
        send_sem=ssem.at[slot, j], recv_sem=rsem.at[slot, j], device_id=dev, device_id_type=MESH)

def finish(plan, acc, recv, ssem, rsem, free, c, j):
    cp = copy_of(plan, acc, recv, ssem, rsem, c, j)
    if cp is None:
        return
    cp.wait()
    if j <= plan.K:
        color = c % plan.colors
        slot = color * 2 + (c // plan.colors) % 2
        n = plan.sizes[j + 1]
        if plan.halve[j]:
            _, dev = step_info(plan, j, color)
            pl.semaphore_signal(free.at[slot, j], inc=1, device_id=dev, device_id_type=MESH)
        off = offsets(plan, c, color, j + 1)
        acc[pl.ds(off, n), :] = acc[pl.ds(off, n), :] + recv[slot, pl.ds(plan.base[j], n), :]

def tick(plan, nchunks, acc, recv, ssem, rsem, free, t, done):
    for j in range(plan.stages, -1, -1):
        c = t - plan.begins[j]
        @pl.when((c >= 0) & (c < nchunks))
        def _():
            if j > 0:
                finish(plan, acc, recv, ssem, rsem, free, c, j - 1)
            if j < plan.stages:
                cp = copy_of(plan, acc, recv, ssem, rsem, c, j)
                if cp is not None:
                    if j > plan.K:
                        color = c % plan.colors
                        slot = color * 2 + (c // plan.colors) % 2
                        pl.semaphore_wait(free.at[slot, 2 * plan.K + 1 - j], 1)
                    cp.start()
            else:
                done(c)


def small_copy(plan, small, got, ssem, rsem, k):
    _, dev = step_info(plan, k, 0)
    return pltpu.make_async_remote_copy(
        src_ref=small, dst_ref=got.at[k], send_sem=ssem.at[k], recv_sem=rsem.at[k],
        device_id=dev, device_id_type=MESH)


def tdot(a, b):
    return lax.dot_general(a, b, (((0,), (0,)), ((), ())), preferred_element_type=F32)


class Work:
    def __init__(self, d, hid, ff, rows, tiles, lag, seq, batch):
        self.rows = rows
        self.halves = d // rows
        self.down = ff // rows
        self.up = ff // d * self.halves
        self.out = hid // rows
        self.gates = 3 * hid // d * self.halves
        self.at_up = self.down
        self.at_out = self.at_up + self.up
        self.at_gates = self.at_out + self.out
        self.chunks = self.at_gates + self.gates
        self.plan = Plan(seq, batch, rows)
        self.lag = lag
        self.tiles = tiles
        self.first_tile = 2
        self.small_at = max(self.first_tile + tiles, self.at_gates)
        self.ticks = max(self.chunks + self.plan.begins[-1], self.small_at + lag * (self.plan.K + 1)) + 1
        self.steps = max(self.chunks, self.small_at) + 1
        self.seq = seq


def back_tile(i, a_ref, b_ref, zc_ref, fc_ref, ic_ref, s_ref, gs_ref, xp_ref, gres_ref, wg_ref, gain_ref,
              gin_ref, gm, gmt, ggb, ggain, state, perm):
    steps = gin_ref.shape[1]
    rows = steps * SUB
    hid = wg_ref.shape[1] // 3
    width = gm.shape[2]
    at = pl.ds(pl.multiple_of(gm.shape[1] - (i + 1) * rows, rows), rows)
    for j in range(hid // LANES):
        here = slice(j * LANES, (j + 1) * LANES)
        mu = state[:, here]
        lams = [None] * steps
        for r in range(steps - 1, -1, -1):
            sl = slice(r * SUB, (r + 1) * SUB)
            lams[r] = gs_ref[sl, here] + mu
            mu = a_ref[sl, here] * lams[r]
        state[:, here] = mu
        lam = jnp.concatenate(lams, axis=0)
        gzc = lam * b_ref[:, here]
        big = gzc * (s_ref[:, here] - zc_ref[:, here])
        parts = (
            (big * fc_ref[:, here].astype(F32)).astype(BF16),
            (-big * ic_ref[:, here].astype(F32)).astype(BF16),
            gzc.astype(BF16),
        )
        for g in range(3):
            first = g * hid + j * LANES
            cols = slice(first, first + LANES)
            gm[first // width, at, first % width : first % width + LANES] = parts[g]
            gmt[:, cols] = parts[g]
            ggb[:, cols] += fold_rows(parts[g].astype(F32))
    gn = dot_t(gmt[...], wg_ref[...])
    source = xp_ref[...].astype(F32)
    scale = inv_rms(source)
    w = gn * gain_ref[...]
    ggain[...] += fold_rows(gn * source * scale)
    gin = gres_ref[...] + scale * w - source * (scale * scale * scale) * jnp.mean(
        w * source, axis=-1, keepdims=True
    )
    gin_ref[...] = from_steps(gin, perm, steps)


def sum_kernel(
    work,
    prod_ref, mu_ref, gdb_ref, gub_ref, ggain2_ref, gob_ref, gain_ref, wg_ref,
    acts_ref, rows_ref, turned_ref, gu_ref,
    a_ref, b_ref, zc_ref, fc_ref, ic_ref, s_ref, gs_ref, xp_ref, gres_ref,
    gin_ref, small_ref, sums_hbm,
    acc, recv, gm, gmt, state, ggb, ggain, perm, small, got, mine, theirs,
    ssem, rsem, free, osem, s2sem, r2sem, csem, crsem,
):
    t = pl.program_id(0)
    plan = work.plan
    rows = work.rows
    s = lax.axis_index("seq")
    b = lax.axis_index("batch")
    ends = Ends(work.seq, mine, theirs, csem, crsem)

    @pl.when(t == 0)
    def _():
        who = [(s, flip(b, 1))] + [(o, b) for o in ends.others]
        who += [(s, flip(b, w)) for axis, w in plan.orders[0] if axis == "batch"]
        bar = pltpu.get_barrier_semaphore()
        for p in who:
            pl.semaphore_signal(bar, inc=1, device_id=p, device_id_type=MESH)
        ggb[...] = jnp.zeros_like(ggb)
        ggain[...] = jnp.zeros_like(ggain)
        pl.semaphore_wait(bar, len(who))
        ends.send(prod_ref, mu_ref, True)

    @pl.when(t == work.first_tile)
    def _():
        ends.receive(prod_ref, mu_ref, state, True)

    def put(value):
        acc[pl.ds(pl.multiple_of(t * rows, rows), rows), :] = value

    @pl.when((t < work.at_up) | ((t >= work.at_out) & (t < work.at_gates)))
    def _():
        put(tdot(acts_ref[...], rows_ref[0]))

    @pl.when((t >= work.at_up) & (t < work.at_out))
    def _():
        put(dot(turned_ref[0], gu_ref[...]))

    @pl.when((t >= work.at_gates) & (t < work.chunks))
    def _():
        put(dot(turned_ref[0], gm[(t - work.at_gates) // work.halves]))

    @pl.when(t == work.small_at)
    def _():
        line = 0
        for v in (ggain, ggb, gob_ref, ggain2_ref, gub_ref, gdb_ref):
            total = jnp.sum(v[...], axis=0, keepdims=True)
            for k in range(total.shape[1] // LANES):
                small[line : line + 1, :] = total[:, k * LANES : (k + 1) * LANES]
                line += 1
        if line < small.shape[0]:
            small[line:, :] = jnp.zeros((small.shape[0] - line, LANES), F32)

    def to_result(c):
        at = pl.ds(pl.multiple_of(c * rows, rows), rows)
        return pltpu.make_async_copy(acc.at[at], sums_hbm.at[at], osem.at[c])

    def step(now):
        for k in range(plan.K + 2):
            @pl.when(now == work.small_at + k * work.lag)
            def _():
                if k > 0:
                    small_copy(plan, small, got, s2sem, r2sem, k - 1).wait()
                    small[...] = small[...] + got[k - 1]
                if k <= plan.K:
                    small_copy(plan, small, got, s2sem, r2sem, k).start()
        tick(plan, work.chunks, acc, recv, ssem, rsem, free, now, lambda c: to_result(c).start())

    step(t)

    i = t - work.first_tile

    @pl.when((i >= 0) & (i < work.tiles))
    def _():
        back_tile(i, a_ref, b_ref, zc_ref, fc_ref, ic_ref, s_ref, gs_ref, xp_ref, gres_ref, wg_ref,
                  gain_ref, gin_ref, gm, gmt, ggb, ggain, state, perm)

    @pl.when(t == work.steps - 1)
    def _():
        def drain(now, _):
            step(now)
            return 0

        lax.fori_loop(work.steps, work.ticks, drain, 0)
        small_ref[...] = small[...]

        def wait(c, _):
            to_result(c).wait()
            return 0

        lax.fori_loop(0, work.chunks, wait, 0)


def last_kernel(work, sizes, pieces, small_ref, gin, sums, gin_o, down_o, up_o, out_o, gates_o, *rest):
    vecs, (gin_v, sums_v, insem, sem) = rest[:-4], rest[-4:]
    rows = work.rows
    d = rows * work.halves
    step = gin.shape[1] // pieces
    moves = []

    def move(src, via, dst):
        k = len(moves)
        read = pltpu.make_async_copy(src, via, insem.at[k])
        read.start()
        moves.append((read, pltpu.make_async_copy(via, dst, sem.at[k])))

    for k in range(pieces):
        part = lambda ref: ref.at[:, pl.ds(k * step, step)]
        move(part(gin), part(gin_v), part(gin_o))
    for first, count, ref, tall in (
        (0, work.down, down_o, True),
        (work.at_up, work.up, up_o, False),
        (work.at_out, work.out, out_o, True),
        (work.at_gates, work.gates, gates_o, False),
    ):
        for k in range(count):
            at = pl.ds((first + k) * rows, rows)
            if tall:
                dst = ref.at[pl.ds(k * rows, rows)]
            else:
                dst = ref.at[pl.ds(k % work.halves * rows, rows), pl.ds(k // work.halves * d, d)]
            move(sums.at[at], sums_v.at[at], dst)
    line = 0
    for ref, n in zip(vecs, sizes):
        for k in range(n // LANES):
            ref[:, k * LANES : (k + 1) * LANES] = small_ref[line : line + 1, :]
            line += 1
    for read, write in moves:
        read.wait()
        write.start()
    for _, write in moves:
        write.wait()


def full(shape):
    return pl.BlockSpec(shape, lambda i: (0,) * len(shape), pipeline_mode=pl.Buffered(1))


def held(shape):
    return pl.BlockSpec(shape, lambda i: (0,) * len(shape))


def per_device(seq, batch, inputs, cotangent, short_lengths, long_lengths, norm_gain, w_gates, gate_bias, w_out,
               out_bias, mlp_gain, w_up, up_bias, w_down, down_bias, tile=256, back=128):
    tok, d = inputs.shape[1:]
    hid = w_out.shape[0]
    ff = w_up.shape[1]
    piece = tok // SUB
    steps = tile // SUB
    grid = tok // tile
    halves = 2
    x = inputs.reshape(SUB, piece, d)
    dy = cotangent.reshape(SUB, piece, d)
    gain1 = norm_gain.reshape(1, d)
    gain2 = mlp_gain.reshape(1, d)
    sds = jax.ShapeDtypeStruct
    rows = lambda n: pl.BlockSpec((tile, n), lambda i: (i, 0))
    natural = pl.BlockSpec((SUB, steps, d), lambda i: (0, i, 0))
    turned = pl.BlockSpec((d, tile), lambda i: (0, i))
    params = pltpu.CompilerParams(
        dimension_semantics=("arbitrary",), vmem_limit_bytes=56 << 20
    )
    a, b, zc, fc, ic, xp, nt, prod, enter = pl.pallas_call(
        functools.partial(gates_kernel, piece, seq),
        grid=(grid,),
        in_specs=[
            pl.BlockSpec(memory_space=pltpu.SMEM), pl.BlockSpec(memory_space=pltpu.SMEM),
            natural, full((1, d)), full((d, 3 * hid)), full((1, 3 * hid)),
        ],
        out_specs=[rows(hid)] * 5 + [rows(d), turned, held((SUB, hid)), held((SUB, hid))],
        out_shape=[sds((tok, hid), F32)] * 3 + [sds((tok, hid), BF16)] * 2
        + [sds((tok, d), BF16), sds((d, tok), BF16), sds((SUB, hid), F32), sds((SUB, hid), F32)],
        scratch_shapes=[pltpu.VMEM((d // 128, tile + SUB * SUB, 128), F32), pltpu.VMEM((SUB, hid), F32)]
        + ends_scratch(seq, hid),
        compiler_params=pltpu.CompilerParams(
            dimension_semantics=("arbitrary",), collective_id=1, has_side_effects=True, vmem_limit_bytes=56 << 20
        ),
    )(short_lengths, long_lengths, x, gain1, w_gates, gate_bias.reshape(1, 3 * hid))

    outs = pl.pallas_call(
        mlp_kernel,
        grid=(grid,),
        in_specs=[rows(hid)] * 3 + [rows(d), turned, natural, full((SUB, hid)), full((hid, d)), full((d, ff)), full((ff, d)),
                  full((1, d)), full((1, d)), full((1, ff)), full((1, d))],
        out_specs=[rows(hid), rows(ff + hid), rows(ff), pl.BlockSpec((2, tile, d), lambda i: (0, i, 0)),
                   pl.BlockSpec((2, halves, d // halves, tile), lambda i: (0, 0, 0, i)), rows(d), rows(hid), natural,
                   held((SUB, hid)), held((SUB, d)), held((SUB, ff)), held((SUB, d)), held((SUB, d))],
        out_shape=[sds((tok, hid), F32), sds((tok, ff + hid), BF16), sds((tok, ff), BF16), sds((2, tok, d), BF16),
                   sds((2, halves, d // halves, tok), BF16), sds((tok, d), F32),
                   sds((tok, hid), F32), sds((SUB, piece, d), BF16),
                   sds((SUB, hid), F32), sds((SUB, d), F32), sds((SUB, ff), F32), sds((SUB, d), F32), sds((SUB, d), F32)],
        scratch_shapes=[pltpu.VMEM((SUB, hid), F32), pltpu.VMEM((SUB, hid), F32), pltpu.VMEM((d // 128, tile + SUB * SUB, 128), F32)],
        compiler_params=params,
    )(a, b, zc, xp, nt, dy, enter, w_out, w_up, w_down, out_bias.reshape(1, d), gain2, up_bias.reshape(1, ff),
      down_bias.reshape(1, d))
    s, acts, gu, pairs, turns, gres, gs, result, mu, gdb, gub, ggain2, gob = outs

    turns = turns.reshape(2 * halves, d // halves, tok)
    work = Work(d, hid, ff, d // halves, tok // back, LAG, seq, batch)
    plan = work.plan
    slots = plan.colors * 2
    bsteps = back // SUB
    lines = -(-(4 * d + 3 * hid + ff) // (8 * LANES)) * 8

    def at_tile(t):
        return work.tiles - 1 - jnp.clip(t - work.first_tile, 0, work.tiles - 1)

    btile = lambda n: pl.BlockSpec((back, n), lambda t: (at_tile(t), 0))
    any_space = pl.BlockSpec(memory_space=pl.ANY)

    def acts_at(t):
        late = jnp.clip(t - work.up, work.down, work.down + work.out - 1)
        return (0, jnp.where(t < work.down, t, late))

    def turned_at(t):
        up = jnp.clip(t - work.at_up, 0, work.up - 1) % halves
        gates = halves + jnp.clip(t - work.at_gates, 0, work.gates - 1) % halves
        return (jnp.where(t < work.at_out, up, gates), 0, 0)

    gin, small, sums = pl.pallas_call(
        functools.partial(sum_kernel, work),
        grid=(work.steps,),
        in_specs=[full((SUB, hid)), full((SUB, hid)), full((SUB, d)), full((SUB, ff)), full((SUB, d)), full((SUB, d)),
                  full((1, d)), full((d, 3 * hid)),
                  pl.BlockSpec((tok, work.rows), acts_at),
                  pl.BlockSpec((1, tok, d), lambda t: (jnp.where(t < work.at_up, 0, 1), 0, 0)),
                  pl.BlockSpec((1, work.rows, tok), turned_at),
                  pl.BlockSpec((tok, d), lambda t: (0, jnp.clip(t - work.at_up, 0, work.up - 1) // halves))]
        + [btile(hid)] * 7 + [btile(d)] * 2,
        out_specs=[pl.BlockSpec((SUB, bsteps, d), lambda t: (0, at_tile(t), 0)), held((lines, LANES)), any_space],
        out_shape=[sds((SUB, piece, d), F32), sds((lines, LANES), F32), sds((work.chunks * work.rows, d), F32)],
        scratch_shapes=[
            pltpu.VMEM((work.chunks * work.rows, d), F32),
            pltpu.VMEM((slots, plan.recv_rows, d), F32),
            pltpu.VMEM((3 * hid // d, tok, d), BF16),
            pltpu.VMEM((back, 3 * hid), BF16),
            pltpu.VMEM((SUB, hid), F32),
            pltpu.VMEM((SUB, 3 * hid), F32),
            pltpu.VMEM((SUB, d), F32),
            pltpu.VMEM((d // 128, back + SUB * SUB, 128), F32),
            pltpu.VMEM((lines, LANES), F32),
            pltpu.VMEM((plan.K + 1, lines, LANES), F32),
            *ends_scratch(seq, hid)[:2],
            pltpu.SemaphoreType.DMA((slots, plan.stages)),
            pltpu.SemaphoreType.DMA((slots, plan.stages)),
            pltpu.SemaphoreType.REGULAR((slots, plan.K + 1)),
            pltpu.SemaphoreType.DMA((work.chunks,)),
            pltpu.SemaphoreType.DMA((plan.K + 1,)),
            pltpu.SemaphoreType.DMA((plan.K + 1,)),
            *ends_scratch(seq, hid)[2:],
        ],
        compiler_params=pltpu.CompilerParams(
            dimension_semantics=("arbitrary",), collective_id=0, has_side_effects=True, vmem_limit_bytes=62 << 20
        ),
    )(prod, mu, gdb, gub, ggain2, gob, gain1, w_gates, acts, pairs, turns, gu,
      a, b, zc, fc, ic, s, gs, xp, gres)
    sizes = (d, 3 * hid, d, d, ff, d)
    vmem = pl.BlockSpec(memory_space=pltpu.VMEM)
    gin, g_down, g_up, g_out, g_gates, *vecs = pl.pallas_call(
        functools.partial(last_kernel, work, sizes, grid),
        in_specs=[vmem, any_space, any_space],
        out_specs=[any_space] * 5 + [vmem] * 6,
        out_shape=[sds(gin.shape, F32), sds((ff, d), F32), sds((d, ff), F32), sds((hid, d), F32), sds((d, 3 * hid), F32)]
        + [sds((1, n), F32) for n in sizes],
        scratch_shapes=[pltpu.VMEM(gin.shape, F32), pltpu.VMEM(sums.shape, F32),
                        pltpu.SemaphoreType.DMA((grid + work.chunks,)), pltpu.SemaphoreType.DMA((grid + work.chunks,))],
        compiler_params=pltpu.CompilerParams(vmem_limit_bytes=62 << 20),
    )(small, gin, sums)
    ggain1, ggb, gob, ggain2, gub, gdb = [v.reshape(-1) for v in vecs]
    return (result.reshape(inputs.shape), gin.reshape(inputs.shape), ggain1, g_gates, ggb, g_out, gob,
            ggain2, g_up, gub, g_down, gdb)


def solution(mesh):
    rows = P("batch", "seq", None)
    return jax.shard_map(
        functools.partial(per_device, mesh.shape["seq"], mesh.shape["batch"]),
        mesh=mesh,
        in_specs=(rows, rows) + (P(),) * 12,
        out_specs=(rows, rows) + (P(),) * 10,
        check_vma=False,
    )
```

```python
import functools

import jax
import jax.numpy as jnp
from jax import lax
from jax.experimental import pallas as pl
from jax.experimental.pallas import tpu as pltpu
from jax.sharding import PartitionSpec as P

MESH = pl.DeviceIdType.MESH
F32 = jnp.float32
BF16 = jnp.bfloat16
epsilon = 1e-06
SUB = 8
LANES = 256
LAG = 3


def flip(v, w):
    return v + w - 2 * w * ((v // w) % 2)


def dot(a, b):
    return jnp.dot(a, b, preferred_element_type=F32)


def dot_t(a, b):
    return lax.dot_general(a, b, (((1,), (1,)), ((), ())), preferred_element_type=F32)


def fold_rows(v):
    return jnp.sum(v.reshape(v.shape[0] // SUB, SUB, v.shape[1]), axis=0)


def inv_rms(v):
    return lax.rsqrt(jnp.mean(v * v, axis=-1, keepdims=True) + epsilon)


def to_steps(block, scratch):
    pieces, steps, n = block.shape
    flat = block.astype(F32).reshape(pieces * steps, n)
    parts = []
    for k in range(n // 128):
        for c in range(pieces):
            scratch[k, c * (steps + SUB) : c * (steps + SUB) + steps, :] = flat[
                c * steps : (c + 1) * steps, k * 128 : (k + 1) * 128
            ]
        parts.append(
            jnp.concatenate(
                [scratch[k, pl.ds(r, pieces, stride=steps + SUB), :] for r in range(steps)], axis=0
            )
        )
    return jnp.concatenate(parts, axis=1)


def from_steps(value, scratch, steps):
    n = value.shape[1]
    parts = []
    for k in range(n // 128):
        for r in range(steps):
            scratch[k, pl.ds(r, SUB, stride=steps + SUB), :] = value[
                r * SUB : (r + 1) * SUB, k * 128 : (k + 1) * 128
            ]
        parts.append(
            jnp.concatenate(
                [scratch[k, c * (steps + SUB) : c * (steps + SUB) + steps, :] for c in range(SUB)], axis=0
            )
        )
    return jnp.concatenate(parts, axis=1).reshape(SUB, steps, n)


class Ends:
    def __init__(self, devices, mine, theirs, ssem, rsem):
        self.devices = devices
        self.mine = mine
        self.theirs = theirs
        self.at = lax.axis_index("seq")
        self.group = lax.axis_index("batch")
        self.others = [lax.rem(self.at + k, devices) for k in range(1, devices)]
        self.copies = [
            pltpu.make_async_remote_copy(
                src_ref=mine, dst_ref=theirs.at[k], send_sem=ssem.at[k], recv_sem=rsem.at[k],
                device_id=(other, self.group), device_id_type=MESH,
            )
            for k, other in enumerate(self.others)
        ]

    def greet(self):
        bar = pltpu.get_barrier_semaphore()
        for other in self.others:
            pl.semaphore_signal(bar, inc=1, device_id=(other, self.group), device_id_type=MESH)

    def send(self, prod_ref, sum_ref, reverse):
        width = prod_ref.shape[1]
        prod = jnp.ones((1, width), F32)
        total = jnp.zeros((1, width), F32)
        for c in range(SUB - 1, -1, -1) if reverse else range(SUB):
            prod = prod * prod_ref[c : c + 1, :]
            total = total * prod_ref[c : c + 1, :] + sum_ref[c : c + 1, :]
        self.mine[0:1, :] = prod
        self.mine[1:2, :] = total
        for copy in self.copies:
            copy.start()

    def receive(self, prod_ref, sum_ref, out_ref, reverse):
        for copy in self.copies:
            copy.wait()
        n = self.devices
        now = jnp.zeros((1, prod_ref.shape[1]), F32)
        for owner in range(n - 1, 0, -1) if reverse else range(n - 1):
            back = lax.rem(self.at - owner + n, n)
            slot = jnp.where(back == 0, 0, back - 1)
            new = self.theirs[slot, 0:1, :] * now + self.theirs[slot, 1:2, :]
            now = jnp.where(owner > self.at if reverse else owner < self.at, new, now)
        for c in range(SUB - 1, -1, -1) if reverse else range(SUB):
            out_ref[c : c + 1, :] = now
            now = prod_ref[c : c + 1, :] * now + sum_ref[c : c + 1, :]


def ends_scratch(devices, width):
    return [
        pltpu.VMEM((SUB, width), F32),
        pltpu.VMEM((devices - 1, SUB, width), F32),
        pltpu.SemaphoreType.DMA((devices - 1,)),
        pltpu.SemaphoreType.DMA((devices - 1,)),
    ]


def gates_kernel(
    piece, devices, short_ref, long_ref, x_ref, gain_ref, wg_ref, bias_ref,
    a_ref, b_ref, zc_ref, fc_ref, ic_ref, xp_ref, nt_ref, prod_ref, enter_ref,
    perm, sum_ref, mine, theirs, ssem, rsem,
):
    i = pl.program_id(0)
    ends = Ends(devices, mine, theirs, ssem, rsem)
    steps = x_ref.shape[1]
    rows = steps * SUB
    hid = wg_ref.shape[1] // 3
    source = to_steps(x_ref[...], perm)
    xp_ref[...] = source.astype(BF16)
    normed = (source * inv_rms(source) * gain_ref[...]).astype(BF16)
    nt_ref[...] = normed.T

    group = lax.axis_index("batch")
    half = short_ref.shape[0]
    first = lax.axis_index("seq") * piece * SUB
    row = lax.broadcasted_iota(jnp.int32, (rows, 128), 0)
    pos = first + (row % SUB) * piece + i * steps + row // SUB
    short = group < half
    srow = jnp.minimum(group, half - 1)
    lrow = jnp.maximum(group - half, 0)
    begins = jnp.zeros((rows, 128), jnp.bool_)
    at = jnp.int32(0)
    for k in range(short_ref.shape[1]):
        begins = begins | (pos == jnp.where(short, at, -1))
        at = at + short_ref[srow, k]
    at = jnp.int32(0)
    for k in range(long_ref.shape[0]):
        begins = begins | (pos == jnp.where(short, -1, at))
        at = at + long_ref[k, lrow]
    keep = jnp.where(begins, 0.0, 1.0).astype(F32)

    @pl.when(i == 0)
    def _():
        ends.greet()
        prod_ref[...] = jnp.ones_like(prod_ref)
        sum_ref[...] = jnp.zeros_like(sum_ref)

    for j in range(hid // LANES):
        cols = [slice(g * hid + j * LANES, g * hid + (j + 1) * LANES) for g in range(3)]
        zf, zi, zc = [dot(normed, wg_ref[:, c]) + bias_ref[:, c] for c in cols]
        f = 1.0 / (1.0 + jnp.exp(-zf))
        g = 1.0 / (1.0 + jnp.exp(-zi))
        inv = 1.0 / (f + g)
        a = f * inv * jnp.concatenate([keep] * (LANES // 128), axis=1)
        b = g * inv
        here = cols[0]
        a_ref[:, here] = a
        b_ref[:, here] = b
        zc_ref[:, here] = zc
        fc_ref[:, here] = (1.0 - f).astype(BF16)
        ic_ref[:, here] = (1.0 - g).astype(BF16)
        u = b * zc
        prod = prod_ref[:, here]
        total = sum_ref[:, here]
        for r in range(steps):
            sl = slice(r * SUB, (r + 1) * SUB)
            prod = prod * a[sl]
            total = total * a[sl] + u[sl]
        prod_ref[:, here] = prod
        sum_ref[:, here] = total


    @pl.when(i == pl.num_programs(0) - 1)
    def _():
        pl.semaphore_wait(pltpu.get_barrier_semaphore(), devices - 1)
        ends.send(prod_ref, sum_ref, False)
        ends.receive(prod_ref, sum_ref, enter_ref, False)


KA = 0.3275911 * 2.0**-0.5
ERF = [0.5 * c for c in (0.254829592, -0.284496736, 1.421413741, -1.453152027, 1.061405429)]
PHI = 0.3989422804014327


def gelu_parts(x):
    t = 1.0 / (1.0 + KA * jnp.abs(x))
    e = jnp.exp2(x * x * (-0.5 * 1.4426950408889634))
    poly = t * (ERF[0] + t * (ERF[1] + t * (ERF[2] + t * (ERF[3] + t * ERF[4]))))
    tail = poly * e
    phi = jnp.where(x >= 0.0, 1.0 - tail, tail)
    return x * phi, phi + x * (e * PHI)


def mlp_kernel(
    a_ref, b_ref, zc_ref, xp_ref, nt_ref, dy_ref, carry_ref, wo_ref, wu_ref, wd_ref,
    obias_ref, gain_ref, ubias_ref, dbias_ref,
    gate_ref, slant_ref, acts_ref, gu_ref, rows_ref, turned_ref, gres_ref, result_ref,
    mu_ref, gdb_ref, gub_ref, ggain_ref, gob_ref,
    state, prod, perm, s_ref,
):
    i = pl.program_id(0)
    steps = dy_ref.shape[1]

    @pl.when(i == 0)
    def _():
        state[...] = carry_ref[...]
        prod[...] = jnp.ones_like(prod)
        for ref in (mu_ref, gdb_ref, gub_ref, ggain_ref, gob_ref):
            ref[...] = jnp.zeros_like(ref)

    st = state[...]
    for r in range(steps):
        sl = slice(r * SUB, (r + 1) * SUB)
        st = a_ref[sl, :] * st + b_ref[sl, :] * zc_ref[sl, :]
        s_ref[sl, :] = st
    state[...] = st
    sb = s_ref[...].astype(BF16)
    gate_ref[...] = b_ref[...].astype(BF16)
    slant_ref[...] = (b_ref[...] * (s_ref[...] - zc_ref[...])).astype(BF16)
    ff = wu_ref.shape[1]
    acts_ref[:, ff:] = sb
    source = xp_ref[...].astype(F32)
    resid = source + dot(sb, wo_ref[...]) + obias_ref[...]
    scale = inv_rms(resid)
    n2 = (resid * scale * gain_ref[...]).astype(BF16)
    half = turned_ref.shape[2]
    turned_ref[0] = n2.T.reshape(-1, half, n2.shape[0])
    turned_ref[1] = nt_ref[...].reshape(-1, half, n2.shape[0])
    dy32 = to_steps(dy_ref[...], perm)
    dy = dy32.astype(BF16)
    rows_ref[0] = dy
    gdb_ref[...] += fold_rows(dy32)
    down = None
    gn2 = None
    for j in range(wu_ref.shape[1] // LANES):
        cols = slice(j * LANES, (j + 1) * LANES)
        upper = dot(n2, wu_ref[:, cols]) + ubias_ref[:, cols]
        act, slope = gelu_parts(upper)
        act = act.astype(BF16)
        acts_ref[:, cols] = act
        gact = dot_t(dy, wd_ref[cols, :])
        gu = (gact * slope).astype(BF16)
        gu_ref[:, cols] = gu
        gub_ref[:, cols] += fold_rows(gu.astype(F32))
    down = dot(acts_ref[:, :ff], wd_ref[...])
    gn2 = dot_t(gu_ref[...], wu_ref[...])
    result = resid + down + dbias_ref[...]
    result_ref[...] = from_steps(result, perm, steps).astype(BF16)
    w = gn2 * gain_ref[...]
    ggain_ref[...] += fold_rows(gn2 * resid * scale)
    gres = dy32 + scale * w - resid * (scale * scale * scale) * jnp.mean(
        w * resid, axis=-1, keepdims=True
    )
    gres_ref[...] = gres
    gr = gres.astype(BF16)
    gob_ref[...] += fold_rows(gr.astype(F32))
    rows_ref[1] = gr
    gs = dot_t(gr, wo_ref[...])
    pr = prod[...]
    mu = mu_ref[...]
    for r in range(steps):
        sl = slice(r * SUB, (r + 1) * SUB)
        pr = pr * a_ref[sl, :]
        mu = mu + pr * gs[sl, :]
    prod[...] = pr
    mu_ref[...] = mu


def bits_of(size):
    w = 1
    out = []
    while w < size:
        out.append(w); w *= 2
    return out

def stage_ticks(j, stages):
    return LAG


class Plan:
    def __init__(self, seq, batch, rows):
        sb = [("seq", w) for w in bits_of(seq)]
        bb = [("batch", w) for w in bits_of(batch)][1:]
        self.orders = [sb + bb, sb[::-1] + bb, bb[:1] + sb + bb[1:]]
        self.K = len(sb) + len(bb)
        self.rows = rows
        self.sizes = [rows]
        self.halve = []
        for k in range(self.K + 1):
            h = self.sizes[-1] >= 16
            self.halve.append(h)
            self.sizes.append(self.sizes[-1] // 2 if h else self.sizes[-1])
        self.stages = 2 * (self.K + 1)
        self.colors = len(self.orders)
        self.begins = [0]
        for j in range(self.stages):
            self.begins.append(self.begins[-1] + stage_ticks(j, self.stages))
        self.base = []
        tot = 0
        for k in range(self.K + 1):
            self.base.append(tot); tot += self.sizes[k + 1]
        self.recv_rows = tot

def pick(color, values):
    out = values[-1]
    for i in range(len(values) - 1):
        out = jnp.where(color == i, values[i], out)
    return out

def step_info(plan, k, color):
    s = lax.axis_index("seq"); b = lax.axis_index("batch")
    if k == 0:
        return b % 2, (s, flip(b, 1))
    mine, ps, pb = [], [], []
    for order in plan.orders:
        axis, w = order[k - 1]
        if axis == "seq":
            mine.append((s // w) % 2); ps.append(flip(s, w)); pb.append(b)
        else:
            mine.append((b // w) % 2); ps.append(s); pb.append(flip(b, w))
    return pick(color, mine), (pick(color, ps), pick(color, pb))

def offsets(plan, c, color, upto):
    off = c * plan.rows
    for k in range(upto):
        if plan.halve[k]:
            bit, _ = step_info(plan, k, color)
            off = off + bit * plan.sizes[k + 1]
    return pl.multiple_of(off, 8)

def copy_of(plan, acc, recv, ssem, rsem, c, j):
    color = c % plan.colors
    slot = color * 2 + (c // plan.colors) % 2
    K = plan.K
    if j <= K:
        k = j
        bit, dev = step_info(plan, k, color)
        n = plan.sizes[k + 1]
        base = offsets(plan, c, color, k)
        src = base + (1 - bit) * n if plan.halve[k] else base
        return pltpu.make_async_remote_copy(
            src_ref=acc.at[pl.ds(pl.multiple_of(src, 8), n)], dst_ref=recv.at[slot, pl.ds(plan.base[k], n)],
            send_sem=ssem.at[slot, j], recv_sem=rsem.at[slot, j], device_id=dev, device_id_type=MESH)
    k = 2 * K + 1 - j
    if not plan.halve[k]:
        return None
    bit, dev = step_info(plan, k, color)
    n = plan.sizes[k + 1]
    mine = offsets(plan, c, color, k + 1)
    return pltpu.make_async_remote_copy(
        src_ref=acc.at[pl.ds(mine, n)], dst_ref=acc.at[pl.ds(mine, n)],
        send_sem=ssem.at[slot, j], recv_sem=rsem.at[slot, j], device_id=dev, device_id_type=MESH)

def finish(plan, acc, recv, ssem, rsem, free, c, j):
    cp = copy_of(plan, acc, recv, ssem, rsem, c, j)
    if cp is None:
        return
    cp.wait()
    if j <= plan.K:
        color = c % plan.colors
        slot = color * 2 + (c // plan.colors) % 2
        n = plan.sizes[j + 1]
        if plan.halve[j]:
            _, dev = step_info(plan, j, color)
            pl.semaphore_signal(free.at[slot, j], inc=1, device_id=dev, device_id_type=MESH)
        off = offsets(plan, c, color, j + 1)
        acc[pl.ds(off, n), :] = acc[pl.ds(off, n), :] + recv[slot, pl.ds(plan.base[j], n), :]

def tick(plan, nchunks, acc, recv, ssem, rsem, free, t, done):
    for j in range(plan.stages, -1, -1):
        c = t - plan.begins[j]
        @pl.when((c >= 0) & (c < nchunks))
        def _():
            if j > 0:
                finish(plan, acc, recv, ssem, rsem, free, c, j - 1)
            if j < plan.stages:
                cp = copy_of(plan, acc, recv, ssem, rsem, c, j)
                if cp is not None:
                    if j > plan.K:
                        color = c % plan.colors
                        slot = color * 2 + (c // plan.colors) % 2
                        pl.semaphore_wait(free.at[slot, 2 * plan.K + 1 - j], 1)
                    cp.start()
            else:
                done(c)


def small_copy(plan, small, got, ssem, rsem, k):
    _, dev = step_info(plan, k, 0)
    return pltpu.make_async_remote_copy(
        src_ref=small, dst_ref=got.at[k], send_sem=ssem.at[k], recv_sem=rsem.at[k],
        device_id=dev, device_id_type=MESH)


def tdot(a, b):
    return lax.dot_general(a, b, (((0,), (0,)), ((), ())), preferred_element_type=F32)


class Work:
    def __init__(self, d, hid, ff, rows, tiles, lag, seq, batch):
        self.rows = rows
        self.halves = d // rows
        self.down = ff // rows
        self.up = ff // d * self.halves
        self.out = hid // rows
        self.gates = 3 * hid // d * self.halves
        self.at_up = self.down
        self.at_out = self.at_up + self.up
        self.at_gates = self.at_out + self.out
        self.chunks = self.at_gates + self.gates
        self.plan = Plan(seq, batch, rows)
        self.lag = lag
        self.tiles = tiles
        self.first_tile = max(2, min(6, self.at_gates - tiles))
        self.small_at = max(self.first_tile + tiles, self.at_gates)
        self.ticks = max(self.chunks + self.plan.begins[-1], self.small_at + lag * (self.plan.K + 1)) + 1
        self.steps = max(self.chunks, self.small_at) + 1
        self.seq = seq


def back_tile(i, a_ref, gate_ref, slant_ref, fc_ref, ic_ref, gr_ref, xp_ref, gres_ref, wg_ref, wo_ref, gain_ref,
              gin_ref, gm, gmt, ggb, ggain, state, perm):
    steps = gin_ref.shape[1]
    rows = steps * SUB
    hid = wg_ref.shape[1] // 3
    width = gm.shape[2]
    at = pl.ds(pl.multiple_of(gm.shape[1] - (i + 1) * rows, rows), rows)
    for j in range(hid // LANES):
        here = slice(j * LANES, (j + 1) * LANES)
        gs = dot_t(gr_ref[0], wo_ref[here, :])
        mu = state[:, here]
        lams = [None] * steps
        for r in range(steps - 1, -1, -1):
            sl = slice(r * SUB, (r + 1) * SUB)
            lams[r] = gs[sl] + mu
            mu = a_ref[sl, here] * lams[r]
        state[:, here] = mu
        lam = jnp.concatenate(lams, axis=0)
        gzc = lam * gate_ref[:, here].astype(F32)
        big = lam * slant_ref[:, here].astype(F32)
        parts = (
            (big * fc_ref[:, here].astype(F32)).astype(BF16),
            (-big * ic_ref[:, here].astype(F32)).astype(BF16),
            gzc.astype(BF16),
        )
        for g in range(3):
            first = g * hid + j * LANES
            cols = slice(first, first + LANES)
            gm[first // width, at, first % width : first % width + LANES] = parts[g]
            gmt[:, cols] = parts[g]
            ggb[:, cols] += fold_rows(parts[g].astype(F32))
    gn = dot_t(gmt[...], wg_ref[...])
    source = xp_ref[...].astype(F32)
    scale = inv_rms(source)
    w = gn * gain_ref[...]
    ggain[...] += fold_rows(gn * source * scale)
    gin = gres_ref[...] + scale * w - source * (scale * scale * scale) * jnp.mean(
        w * source, axis=-1, keepdims=True
    )
    gin_ref[...] = from_steps(gin, perm, steps)


def sum_kernel(
    work,
    prod_ref, mu_ref, gdb_ref, gub_ref, ggain2_ref, gob_ref, gain_ref, wg_ref, wo_ref,
    acts_ref, rows_ref, turned_ref, gu_ref,
    a_ref, gate_ref, slant_ref, fc_ref, ic_ref, gr_ref, xp_ref, gres_ref,
    gin_ref, small_ref, sums_hbm,
    acc, recv, gm, gmt, state, ggb, ggain, perm, small, got, mine, theirs,
    ssem, rsem, free, osem, s2sem, r2sem, csem, crsem,
):
    t = pl.program_id(0)
    plan = work.plan
    rows = work.rows
    s = lax.axis_index("seq")
    b = lax.axis_index("batch")
    ends = Ends(work.seq, mine, theirs, csem, crsem)

    @pl.when(t == 0)
    def _():
        who = [(s, flip(b, 1))] + [(o, b) for o in ends.others]
        who += [(s, flip(b, w)) for axis, w in plan.orders[0] if axis == "batch"]
        bar = pltpu.get_barrier_semaphore()
        for p in who:
            pl.semaphore_signal(bar, inc=1, device_id=p, device_id_type=MESH)
        ggb[...] = jnp.zeros_like(ggb)
        ggain[...] = jnp.zeros_like(ggain)
        pl.semaphore_wait(bar, len(who))
        ends.send(prod_ref, mu_ref, True)

    @pl.when(t == work.first_tile)
    def _():
        ends.receive(prod_ref, mu_ref, state, True)

    def put(value):
        acc[pl.ds(pl.multiple_of(t * rows, rows), rows), :] = value

    @pl.when((t < work.at_up) | ((t >= work.at_out) & (t < work.at_gates)))
    def _():
        put(tdot(acts_ref[...], rows_ref[0]))

    @pl.when((t >= work.at_up) & (t < work.at_out))
    def _():
        put(dot(turned_ref[0], gu_ref[...]))

    @pl.when((t >= work.at_gates) & (t < work.chunks))
    def _():
        put(dot(turned_ref[0], gm[(t - work.at_gates) // work.halves]))

    @pl.when(t == work.small_at)
    def _():
        line = 0
        for v in (ggain, ggb, gob_ref, ggain2_ref, gub_ref, gdb_ref):
            total = jnp.sum(v[...], axis=0, keepdims=True)
            for k in range(total.shape[1] // LANES):
                small[line : line + 1, :] = total[:, k * LANES : (k + 1) * LANES]
                line += 1
        if line < small.shape[0]:
            small[line:, :] = jnp.zeros((small.shape[0] - line, LANES), F32)

    def to_result(c):
        at = pl.ds(pl.multiple_of(c * rows, rows), rows)
        return pltpu.make_async_copy(acc.at[at], sums_hbm.at[at], osem.at[c])

    def step(now):
        for k in range(plan.K + 2):
            @pl.when(now == work.small_at + k * work.lag)
            def _():
                if k > 0:
                    small_copy(plan, small, got, s2sem, r2sem, k - 1).wait()
                    small[...] = small[...] + got[k - 1]
                if k <= plan.K:
                    small_copy(plan, small, got, s2sem, r2sem, k).start()
        tick(plan, work.chunks, acc, recv, ssem, rsem, free, now, lambda c: to_result(c).start())

    step(t)

    i = t - work.first_tile

    @pl.when((i >= 0) & (i < work.tiles))
    def _():
        back_tile(i, a_ref, gate_ref, slant_ref, fc_ref, ic_ref, gr_ref, xp_ref, gres_ref, wg_ref, wo_ref,
                  gain_ref, gin_ref, gm, gmt, ggb, ggain, state, perm)

    @pl.when(t == work.steps - 1)
    def _():
        def drain(now, _):
            step(now)
            return 0

        lax.fori_loop(work.steps, work.ticks, drain, 0)
        small_ref[...] = small[...]

        def wait(c, _):
            to_result(c).wait()
            return 0

        lax.fori_loop(0, work.chunks, wait, 0)


def last_kernel(work, sizes, pieces, small_ref, gin, sums, gin_o, down_o, up_o, out_o, gates_o, *rest):
    vecs, (gin_v, sums_v, insem, sem) = rest[:-4], rest[-4:]
    rows = work.rows
    d = rows * work.halves
    step = gin.shape[1] // pieces
    moves = []

    def move(src, via, dst):
        k = len(moves)
        read = pltpu.make_async_copy(src, via, insem.at[k])
        read.start()
        moves.append((read, pltpu.make_async_copy(via, dst, sem.at[k])))

    for k in range(pieces):
        part = lambda ref: ref.at[:, pl.ds(k * step, step)]
        move(part(gin), part(gin_v), part(gin_o))
    for first, count, ref, tall in (
        (0, work.down, down_o, True),
        (work.at_up, work.up, up_o, False),
        (work.at_out, work.out, out_o, True),
        (work.at_gates, work.gates, gates_o, False),
    ):
        for k in range(count):
            at = pl.ds((first + k) * rows, rows)
            if tall:
                dst = ref.at[pl.ds(k * rows, rows)]
            else:
                dst = ref.at[pl.ds(k % work.halves * rows, rows), pl.ds(k // work.halves * d, d)]
            move(sums.at[at], sums_v.at[at], dst)
    line = 0
    for ref, n in zip(vecs, sizes):
        for k in range(n // LANES):
            ref[:, k * LANES : (k + 1) * LANES] = small_ref[line : line + 1, :]
            line += 1
    for read, write in moves:
        read.wait()
        write.start()
    for _, write in moves:
        write.wait()


def full(shape):
    return pl.BlockSpec(shape, lambda i: (0,) * len(shape), pipeline_mode=pl.Buffered(1))


def held(shape):
    return pl.BlockSpec(shape, lambda i: (0,) * len(shape))


def per_device(seq, batch, inputs, cotangent, short_lengths, long_lengths, norm_gain, w_gates, gate_bias, w_out,
               out_bias, mlp_gain, w_up, up_bias, w_down, down_bias, tile=256, back=256):
    tok, d = inputs.shape[1:]
    hid = w_out.shape[0]
    ff = w_up.shape[1]
    piece = tok // SUB
    steps = tile // SUB
    grid = tok // tile
    halves = 2
    x = inputs.reshape(SUB, piece, d)
    dy = cotangent.reshape(SUB, piece, d)
    gain1 = norm_gain.reshape(1, d)
    gain2 = mlp_gain.reshape(1, d)
    sds = jax.ShapeDtypeStruct
    rows = lambda n: pl.BlockSpec((tile, n), lambda i: (i, 0))
    natural = pl.BlockSpec((SUB, steps, d), lambda i: (0, i, 0))
    turned = pl.BlockSpec((d, tile), lambda i: (0, i))
    params = pltpu.CompilerParams(
        dimension_semantics=("arbitrary",), vmem_limit_bytes=56 << 20
    )
    a, b, zc, fc, ic, xp, nt, prod, enter = pl.pallas_call(
        functools.partial(gates_kernel, piece, seq),
        grid=(grid,),
        in_specs=[
            pl.BlockSpec(memory_space=pltpu.SMEM), pl.BlockSpec(memory_space=pltpu.SMEM),
            natural, full((1, d)), full((d, 3 * hid)), full((1, 3 * hid)),
        ],
        out_specs=[rows(hid)] * 5 + [rows(d), turned, held((SUB, hid)), held((SUB, hid))],
        out_shape=[sds((tok, hid), F32)] * 3 + [sds((tok, hid), BF16)] * 2
        + [sds((tok, d), BF16), sds((d, tok), BF16), sds((SUB, hid), F32), sds((SUB, hid), F32)],
        scratch_shapes=[pltpu.VMEM((d // 128, tile + SUB * SUB, 128), F32), pltpu.VMEM((SUB, hid), F32)]
        + ends_scratch(seq, hid),
        compiler_params=pltpu.CompilerParams(
            dimension_semantics=("arbitrary",), collective_id=1, has_side_effects=True, vmem_limit_bytes=56 << 20
        ),
    )(short_lengths, long_lengths.T, x, gain1, w_gates, gate_bias.reshape(1, 3 * hid))

    outs = pl.pallas_call(
        mlp_kernel,
        grid=(grid,),
        in_specs=[rows(hid)] * 3 + [rows(d), turned, natural, full((SUB, hid)), full((hid, d)), full((d, ff)), full((ff, d)),
                  full((1, d)), full((1, d)), full((1, ff)), full((1, d))],
        out_specs=[rows(hid), rows(hid), rows(ff + hid), rows(ff), pl.BlockSpec((2, tile, d), lambda i: (0, i, 0)),
                   pl.BlockSpec((2, halves, d // halves, tile), lambda i: (0, 0, 0, i)), rows(d), natural,
                   held((SUB, hid)), held((SUB, d)), held((SUB, ff)), held((SUB, d)), held((SUB, d))],
        out_shape=[sds((tok, hid), BF16), sds((tok, hid), BF16), sds((tok, ff + hid), BF16), sds((tok, ff), BF16), sds((2, tok, d), BF16),
                   sds((2, halves, d // halves, tok), BF16), sds((tok, d), F32),
                   sds((SUB, piece, d), BF16),
                   sds((SUB, hid), F32), sds((SUB, d), F32), sds((SUB, ff), F32), sds((SUB, d), F32), sds((SUB, d), F32)],
        scratch_shapes=[pltpu.VMEM((SUB, hid), F32), pltpu.VMEM((SUB, hid), F32), pltpu.VMEM((d // 128, tile + SUB * SUB, 128), F32),
                        pltpu.VMEM((tile, hid), F32)],
        compiler_params=params,
    )(a, b, zc, xp, nt, dy, enter, w_out, w_up, w_down, out_bias.reshape(1, d), gain2, up_bias.reshape(1, ff),
      down_bias.reshape(1, d))
    gate, slant, acts, gu, pairs, turns, gres, result, mu, gdb, gub, ggain2, gob = outs

    turns = turns.reshape(2 * halves, d // halves, tok)
    work = Work(d, hid, ff, d // halves, tok // back, LAG, seq, batch)
    plan = work.plan
    slots = plan.colors * 2
    bsteps = back // SUB
    lines = -(-(4 * d + 3 * hid + ff) // (8 * LANES)) * 8

    def at_tile(t):
        return work.tiles - 1 - jnp.clip(t - work.first_tile, 0, work.tiles - 1)

    btile = lambda n: pl.BlockSpec((back, n), lambda t: (at_tile(t), 0))
    any_space = pl.BlockSpec(memory_space=pl.ANY)

    def acts_at(t):
        late = jnp.clip(t - work.up, work.down, work.down + work.out - 1)
        return (0, jnp.where(t < work.down, t, late))

    def turned_at(t):
        up = jnp.clip(t - work.at_up, 0, work.up - 1) % halves
        gates = halves + jnp.clip(t - work.at_gates, 0, work.gates - 1) % halves
        return (jnp.where(t < work.at_out, up, gates), 0, 0)

    gin, small, sums = pl.pallas_call(
        functools.partial(sum_kernel, work),
        grid=(work.steps,),
        in_specs=[full((SUB, hid)), full((SUB, hid)), full((SUB, d)), full((SUB, ff)), full((SUB, d)), full((SUB, d)),
                  full((1, d)), full((d, 3 * hid)), full((hid, d)),
                  pl.BlockSpec((tok, work.rows), acts_at),
                  pl.BlockSpec((1, tok, d), lambda t: (jnp.where(t < work.at_up, 0, 1), 0, 0), pipeline_mode=pl.Buffered(1)),
                  pl.BlockSpec((1, work.rows, tok), turned_at),
                  pl.BlockSpec((tok, d), lambda t: (0, jnp.clip(t - work.at_up, 0, work.up - 1) // halves))]
        + [btile(hid)] * 5 + [pl.BlockSpec((1, back, d), lambda t: (1, at_tile(t), 0))] + [btile(d)] * 2,
        out_specs=[pl.BlockSpec((SUB, bsteps, d), lambda t: (0, at_tile(t), 0)), held((lines, LANES)), any_space],
        out_shape=[sds((SUB, piece, d), F32), sds((lines, LANES), F32), sds((work.chunks * work.rows, d), F32)],
        scratch_shapes=[
            pltpu.VMEM((work.chunks * work.rows, d), F32),
            pltpu.VMEM((slots, plan.recv_rows, d), F32),
            pltpu.VMEM((3 * hid // d, tok, d), BF16),
            pltpu.VMEM((back, 3 * hid), BF16),
            pltpu.VMEM((SUB, hid), F32),
            pltpu.VMEM((SUB, 3 * hid), F32),
            pltpu.VMEM((SUB, d), F32),
            pltpu.VMEM((d // 128, back + SUB * SUB, 128), F32),
            pltpu.VMEM((lines, LANES), F32),
            pltpu.VMEM((plan.K + 1, lines, LANES), F32),
            *ends_scratch(seq, hid)[:2],
            pltpu.SemaphoreType.DMA((slots, plan.stages)),
            pltpu.SemaphoreType.DMA((slots, plan.stages)),
            pltpu.SemaphoreType.REGULAR((slots, plan.K + 1)),
            pltpu.SemaphoreType.DMA((work.chunks,)),
            pltpu.SemaphoreType.DMA((plan.K + 1,)),
            pltpu.SemaphoreType.DMA((plan.K + 1,)),
            *ends_scratch(seq, hid)[2:],
        ],
        compiler_params=pltpu.CompilerParams(
            dimension_semantics=("arbitrary",), collective_id=0, has_side_effects=True, vmem_limit_bytes=62 << 20
        ),
    )(prod, mu, gdb, gub, ggain2, gob, gain1, w_gates, w_out, acts, pairs, turns, gu,
      a, gate, slant, fc, ic, pairs, xp, gres)
    sizes = (d, 3 * hid, d, d, ff, d)
    vmem = pl.BlockSpec(memory_space=pltpu.VMEM)
    gin, g_down, g_up, g_out, g_gates, *vecs = pl.pallas_call(
        functools.partial(last_kernel, work, sizes, grid),
        in_specs=[vmem, any_space, any_space],
        out_specs=[any_space] * 5 + [vmem] * 6,
        out_shape=[sds(gin.shape, F32), sds((ff, d), F32), sds((d, ff), F32), sds((hid, d), F32), sds((d, 3 * hid), F32)]
        + [sds((1, n), F32) for n in sizes],
        scratch_shapes=[pltpu.VMEM(gin.shape, F32), pltpu.VMEM(sums.shape, F32),
                        pltpu.SemaphoreType.DMA((grid + work.chunks,)), pltpu.SemaphoreType.DMA((grid + work.chunks,))],
        compiler_params=pltpu.CompilerParams(vmem_limit_bytes=62 << 20),
    )(small, gin, sums)
    ggain1, ggb, gob, ggain2, gub, gdb = [v.reshape(-1) for v in vecs]
    return (result.reshape(inputs.shape), gin.reshape(inputs.shape), ggain1, g_gates, ggb, g_out, gob,
            ggain2, g_up, gub, g_down, gdb)


def solution(mesh):
    rows = P("batch", "seq", None)
    return jax.shard_map(
        functools.partial(per_device, mesh.shape["seq"], mesh.shape["batch"]),
        mesh=mesh,
        in_specs=(rows, rows) + (P(),) * 12,
        out_specs=(rows, rows) + (P(),) * 10,
        check_vma=False,
    )
```

```python
import functools

import jax
import jax.numpy as jnp
from jax import lax
from jax.experimental import pallas as pl
from jax.experimental.pallas import tpu as pltpu
from jax.sharding import PartitionSpec as P

MESH = pl.DeviceIdType.MESH
F32 = jnp.float32
BF16 = jnp.bfloat16
epsilon = 1e-06
SUB = 8
LANES = 256
LAG = 3


def flip(v, w):
    return v + w - 2 * w * ((v // w) % 2)


def dot(a, b):
    return jnp.dot(a, b, preferred_element_type=F32)


def dot_t(a, b):
    return lax.dot_general(a, b, (((1,), (1,)), ((), ())), preferred_element_type=F32)


def fold_rows(v):
    return jnp.sum(v.reshape(v.shape[0] // SUB, SUB, v.shape[1]), axis=0)


def inv_rms(v):
    return lax.rsqrt(jnp.mean(v * v, axis=-1, keepdims=True) + epsilon)


def to_steps(block, scratch):
    pieces, steps, n = block.shape
    flat = block.astype(F32).reshape(pieces * steps, n)
    parts = []
    for k in range(n // 128):
        for c in range(pieces):
            scratch[k, c * (steps + SUB) : c * (steps + SUB) + steps, :] = flat[
                c * steps : (c + 1) * steps, k * 128 : (k + 1) * 128
            ]
        parts.append(
            jnp.concatenate(
                [scratch[k, pl.ds(r, pieces, stride=steps + SUB), :] for r in range(steps)], axis=0
            )
        )
    return jnp.concatenate(parts, axis=1)


def from_steps(value, scratch, steps):
    n = value.shape[1]
    parts = []
    for k in range(n // 128):
        for r in range(steps):
            scratch[k, pl.ds(r, SUB, stride=steps + SUB), :] = value[
                r * SUB : (r + 1) * SUB, k * 128 : (k + 1) * 128
            ]
        parts.append(
            jnp.concatenate(
                [scratch[k, c * (steps + SUB) : c * (steps + SUB) + steps, :] for c in range(SUB)], axis=0
            )
        )
    return jnp.concatenate(parts, axis=1).reshape(SUB, steps, n)


class Ends:
    def __init__(self, devices, mine, theirs, ssem, rsem):
        self.devices = devices
        self.mine = mine
        self.theirs = theirs
        self.at = lax.axis_index("seq")
        self.group = lax.axis_index("batch")
        self.others = [lax.rem(self.at + k, devices) for k in range(1, devices)]
        self.copies = [
            pltpu.make_async_remote_copy(
                src_ref=mine, dst_ref=theirs.at[k], send_sem=ssem.at[k], recv_sem=rsem.at[k],
                device_id=(other, self.group), device_id_type=MESH,
            )
            for k, other in enumerate(self.others)
        ]

    def greet(self):
        bar = pltpu.get_barrier_semaphore()
        for other in self.others:
            pl.semaphore_signal(bar, inc=1, device_id=(other, self.group), device_id_type=MESH)

    def send(self, prod_ref, sum_ref, reverse):
        width = prod_ref.shape[1]
        prod = jnp.ones((1, width), F32)
        total = jnp.zeros((1, width), F32)
        for c in range(SUB - 1, -1, -1) if reverse else range(SUB):
            prod = prod * prod_ref[c : c + 1, :]
            total = total * prod_ref[c : c + 1, :] + sum_ref[c : c + 1, :]
        self.mine[0:1, :] = prod
        self.mine[1:2, :] = total
        for copy in self.copies:
            copy.start()

    def receive(self, prod_ref, sum_ref, out_ref, reverse):
        for copy in self.copies:
            copy.wait()
        n = self.devices
        now = jnp.zeros((1, prod_ref.shape[1]), F32)
        for owner in range(n - 1, 0, -1) if reverse else range(n - 1):
            back = lax.rem(self.at - owner + n, n)
            slot = jnp.where(back == 0, 0, back - 1)
            new = self.theirs[slot, 0:1, :] * now + self.theirs[slot, 1:2, :]
            now = jnp.where(owner > self.at if reverse else owner < self.at, new, now)
        for c in range(SUB - 1, -1, -1) if reverse else range(SUB):
            out_ref[c : c + 1, :] = now
            now = prod_ref[c : c + 1, :] * now + sum_ref[c : c + 1, :]


def ends_scratch(devices, width):
    return [
        pltpu.VMEM((SUB, width), F32),
        pltpu.VMEM((devices - 1, SUB, width), F32),
        pltpu.SemaphoreType.DMA((devices - 1,)),
        pltpu.SemaphoreType.DMA((devices - 1,)),
    ]


def gates_kernel(
    piece, devices, short_ref, long_ref, x_ref, gain_ref, wg_ref, bias_ref,
    a_ref, b_ref, zc_ref, fc_ref, ic_ref, xp_ref, nt_ref, prod_ref, enter_ref,
    perm, sum_ref, mine, theirs, ssem, rsem,
):
    i = pl.program_id(0)
    ends = Ends(devices, mine, theirs, ssem, rsem)
    steps = x_ref.shape[1]
    rows = steps * SUB
    hid = wg_ref.shape[1] // 3
    source = to_steps(x_ref[...], perm)
    xp_ref[...] = source.astype(BF16)
    normed = (source * inv_rms(source) * gain_ref[...]).astype(BF16)
    nt_ref[...] = normed.T

    group = lax.axis_index("batch")
    half = short_ref.shape[0]
    first = lax.axis_index("seq") * piece * SUB
    row = lax.broadcasted_iota(jnp.int32, (rows, 128), 0)
    pos = first + (row % SUB) * piece + i * steps + row // SUB
    short = group < half
    srow = jnp.minimum(group, half - 1)
    lrow = jnp.maximum(group - half, 0)
    begins = jnp.zeros((rows, 128), jnp.bool_)
    at = jnp.int32(0)
    for k in range(short_ref.shape[1]):
        begins = begins | (pos == jnp.where(short, at, -1))
        at = at + short_ref[srow, k]
    at = jnp.int32(0)
    for k in range(long_ref.shape[0]):
        begins = begins | (pos == jnp.where(short, -1, at))
        at = at + long_ref[k, lrow]
    keep = jnp.where(begins, 0.0, 1.0).astype(F32)

    @pl.when(i == 0)
    def _():
        ends.greet()
        prod_ref[...] = jnp.ones_like(prod_ref)
        sum_ref[...] = jnp.zeros_like(sum_ref)

    for j in range(hid // LANES):
        cols = [slice(g * hid + j * LANES, g * hid + (j + 1) * LANES) for g in range(3)]
        zf, zi, zc = [dot(normed, wg_ref[:, c]) + bias_ref[:, c] for c in cols]
        f = 1.0 / (1.0 + jnp.exp(-zf))
        g = 1.0 / (1.0 + jnp.exp(-zi))
        inv = 1.0 / (f + g)
        a = f * inv * jnp.concatenate([keep] * (LANES // 128), axis=1)
        b = g * inv
        here = cols[0]
        a_ref[:, here] = a
        b_ref[:, here] = b
        zc_ref[:, here] = zc
        fc_ref[:, here] = (1.0 - f).astype(BF16)
        ic_ref[:, here] = (1.0 - g).astype(BF16)
        u = b * zc
        prod = prod_ref[:, here]
        total = sum_ref[:, here]
        for r in range(steps):
            sl = slice(r * SUB, (r + 1) * SUB)
            prod = prod * a[sl]
            total = total * a[sl] + u[sl]
        prod_ref[:, here] = prod
        sum_ref[:, here] = total


    @pl.when(i == pl.num_programs(0) - 1)
    def _():
        pl.semaphore_wait(pltpu.get_barrier_semaphore(), devices - 1)
        ends.send(prod_ref, sum_ref, False)
        ends.receive(prod_ref, sum_ref, enter_ref, False)


KA = 0.3275911 * 2.0**-0.5
ERF = [0.5 * c for c in (0.254829592, -0.284496736, 1.421413741, -1.453152027, 1.061405429)]
PHI = 0.3989422804014327


def gelu_parts(x):
    t = 1.0 / (1.0 + KA * jnp.abs(x))
    e = jnp.exp2(x * x * (-0.5 * 1.4426950408889634))
    poly = t * (ERF[0] + t * (ERF[1] + t * (ERF[2] + t * (ERF[3] + t * ERF[4]))))
    tail = poly * e
    phi = jnp.where(x >= 0.0, 1.0 - tail, tail)
    return x * phi, phi + x * (e * PHI)


def mlp_kernel(
    a_ref, b_ref, zc_ref, xp_ref, nt_ref, dy_ref, carry_ref, wo_ref, wu_ref, wd_ref,
    obias_ref, gain_ref, ubias_ref, dbias_ref,
    gate_ref, slant_ref, acts_ref, gu_ref, rows_ref, turned_ref, gres_ref, result_ref,
    mu_ref, gdb_ref, gub_ref, ggain_ref, gob_ref,
    state, prod, perm, s_ref,
):
    i = pl.program_id(0)
    steps = dy_ref.shape[1]

    @pl.when(i == 0)
    def _():
        state[...] = carry_ref[...]
        prod[...] = jnp.ones_like(prod)
        for ref in (mu_ref, gdb_ref, gub_ref, ggain_ref, gob_ref):
            ref[...] = jnp.zeros_like(ref)

    st = state[...]
    for r in range(steps):
        sl = slice(r * SUB, (r + 1) * SUB)
        st = a_ref[sl, :] * st + b_ref[sl, :] * zc_ref[sl, :]
        s_ref[sl, :] = st
    state[...] = st
    sb = s_ref[...].astype(BF16)
    gate_ref[...] = b_ref[...].astype(BF16)
    slant_ref[...] = (b_ref[...] * (s_ref[...] - zc_ref[...])).astype(BF16)
    ff = wu_ref.shape[1]
    acts_ref[:, ff:] = sb
    source = xp_ref[...].astype(F32)
    resid = source + dot(sb, wo_ref[...]) + obias_ref[...]
    scale = inv_rms(resid)
    n2 = (resid * scale * gain_ref[...]).astype(BF16)
    half = turned_ref.shape[2]
    turned_ref[0] = n2.T.reshape(-1, half, n2.shape[0])
    turned_ref[1] = nt_ref[...].reshape(-1, half, n2.shape[0])
    dy32 = to_steps(dy_ref[...], perm)
    dy = dy32.astype(BF16)
    rows_ref[0] = dy
    gdb_ref[...] += fold_rows(dy32)
    down = None
    gn2 = None
    for j in range(wu_ref.shape[1] // LANES):
        cols = slice(j * LANES, (j + 1) * LANES)
        upper = dot(n2, wu_ref[:, cols]) + ubias_ref[:, cols]
        act, slope = gelu_parts(upper)
        act = act.astype(BF16)
        acts_ref[:, cols] = act
        gact = dot_t(dy, wd_ref[cols, :])
        gu = (gact * slope).astype(BF16)
        gu_ref[:, cols] = gu
        gub_ref[:, cols] += fold_rows(gu.astype(F32))
    down = dot(acts_ref[:, :ff], wd_ref[...])
    gn2 = dot_t(gu_ref[...], wu_ref[...])
    result = resid + down + dbias_ref[...]
    result_ref[...] = from_steps(result, perm, steps).astype(BF16)
    w = gn2 * gain_ref[...]
    ggain_ref[...] += fold_rows(gn2 * resid * scale)
    gres = dy32 + scale * w - resid * (scale * scale * scale) * jnp.mean(
        w * resid, axis=-1, keepdims=True
    )
    gres_ref[...] = gres
    gr = gres.astype(BF16)
    gob_ref[...] += fold_rows(gr.astype(F32))
    rows_ref[1] = gr
    gs = dot_t(gr, wo_ref[...])
    pr = prod[...]
    mu = mu_ref[...]
    for r in range(steps):
        sl = slice(r * SUB, (r + 1) * SUB)
        pr = pr * a_ref[sl, :]
        mu = mu + pr * gs[sl, :]
    prod[...] = pr
    mu_ref[...] = mu


def bits_of(size):
    w = 1
    out = []
    while w < size:
        out.append(w); w *= 2
    return out

def stage_ticks(j, stages):
    return 2 if j in (0, stages - 1) else LAG


class Plan:
    def __init__(self, seq, batch, rows):
        sb = [("seq", w) for w in bits_of(seq)]
        bb = [("batch", w) for w in bits_of(batch)][1:]
        self.orders = [sb + bb, sb[::-1] + bb, bb[:1] + sb + bb[1:]]
        self.K = len(sb) + len(bb)
        self.rows = rows
        self.sizes = [rows]
        self.halve = []
        for k in range(self.K + 1):
            h = self.sizes[-1] >= 16
            self.halve.append(h)
            self.sizes.append(self.sizes[-1] // 2 if h else self.sizes[-1])
        self.stages = 2 * (self.K + 1)
        self.colors = len(self.orders)
        self.begins = [0]
        for j in range(self.stages):
            self.begins.append(self.begins[-1] + stage_ticks(j, self.stages))
        self.base = []
        tot = 0
        for k in range(self.K + 1):
            self.base.append(tot); tot += self.sizes[k + 1]
        self.recv_rows = tot

def pick(color, values):
    out = values[-1]
    for i in range(len(values) - 1):
        out = jnp.where(color == i, values[i], out)
    return out

def step_info(plan, k, color):
    s = lax.axis_index("seq"); b = lax.axis_index("batch")
    if k == 0:
        return b % 2, (s, flip(b, 1))
    mine, ps, pb = [], [], []
    for order in plan.orders:
        axis, w = order[k - 1]
        if axis == "seq":
            mine.append((s // w) % 2); ps.append(flip(s, w)); pb.append(b)
        else:
            mine.append((b // w) % 2); ps.append(s); pb.append(flip(b, w))
    return pick(color, mine), (pick(color, ps), pick(color, pb))

def offsets(plan, c, color, upto):
    off = c * plan.rows
    for k in range(upto):
        if plan.halve[k]:
            bit, _ = step_info(plan, k, color)
            off = off + bit * plan.sizes[k + 1]
    return pl.multiple_of(off, 8)

def copy_of(plan, acc, recv, ssem, rsem, c, j):
    color = c % plan.colors
    slot = color * 2 + (c // plan.colors) % 2
    K = plan.K
    if j <= K:
        k = j
        bit, dev = step_info(plan, k, color)
        n = plan.sizes[k + 1]
        base = offsets(plan, c, color, k)
        src = base + (1 - bit) * n if plan.halve[k] else base
        return pltpu.make_async_remote_copy(
            src_ref=acc.at[pl.ds(pl.multiple_of(src, 8), n)], dst_ref=recv.at[slot, pl.ds(plan.base[k], n)],
            send_sem=ssem.at[slot, j], recv_sem=rsem.at[slot, j], device_id=dev, device_id_type=MESH)
    k = 2 * K + 1 - j
    if not plan.halve[k]:
        return None
    bit, dev = step_info(plan, k, color)
    n = plan.sizes[k + 1]
    mine = offsets(plan, c, color, k + 1)
    return pltpu.make_async_remote_copy(
        src_ref=acc.at[pl.ds(mine, n)], dst_ref=acc.at[pl.ds(mine, n)],
        send_sem=ssem.at[slot, j], recv_sem=rsem.at[slot, j], device_id=dev, device_id_type=MESH)

def finish(plan, acc, recv, ssem, rsem, free, c, j):
    cp = copy_of(plan, acc, recv, ssem, rsem, c, j)
    if cp is None:
        return
    cp.wait()
    if j <= plan.K:
        color = c % plan.colors
        slot = color * 2 + (c // plan.colors) % 2
        n = plan.sizes[j + 1]
        if plan.halve[j]:
            _, dev = step_info(plan, j, color)
            pl.semaphore_signal(free.at[slot, j], inc=1, device_id=dev, device_id_type=MESH)
        off = offsets(plan, c, color, j + 1)
        acc[pl.ds(off, n), :] = acc[pl.ds(off, n), :] + recv[slot, pl.ds(plan.base[j], n), :]

def tick(plan, nchunks, acc, recv, ssem, rsem, free, t, done):
    for j in range(plan.stages, -1, -1):
        c = t - plan.begins[j]
        @pl.when((c >= 0) & (c < nchunks))
        def _():
            if j > 0:
                finish(plan, acc, recv, ssem, rsem, free, c, j - 1)
            if j < plan.stages:
                cp = copy_of(plan, acc, recv, ssem, rsem, c, j)
                if cp is not None:
                    if j > plan.K:
                        color = c % plan.colors
                        slot = color * 2 + (c // plan.colors) % 2
                        pl.semaphore_wait(free.at[slot, 2 * plan.K + 1 - j], 1)
                    cp.start()
            else:
                done(c)


def small_copy(plan, small, got, ssem, rsem, k):
    _, dev = step_info(plan, k, 0)
    return pltpu.make_async_remote_copy(
        src_ref=small, dst_ref=got.at[k], send_sem=ssem.at[k], recv_sem=rsem.at[k],
        device_id=dev, device_id_type=MESH)


def tdot(a, b):
    return lax.dot_general(a, b, (((0,), (0,)), ((), ())), preferred_element_type=F32)


class Work:
    def __init__(self, d, hid, ff, rows, tiles, lag, seq, batch):
        self.rows = rows
        self.halves = d // rows
        self.down = ff // rows
        self.up = ff // d * self.halves
        self.out = hid // rows
        self.gates = 3 * hid // d * self.halves
        self.at_up = self.down
        self.at_out = self.at_up + self.up
        self.at_gates = self.at_out + self.out
        self.chunks = self.at_gates + self.gates
        self.plan = Plan(seq, batch, rows)
        self.lag = lag
        self.tiles = tiles
        self.first_tile = max(2, min(6, self.at_gates - tiles))
        self.small_at = max(self.first_tile + tiles, self.at_gates)
        self.ticks = max(self.chunks + self.plan.begins[-1], self.small_at + lag * (self.plan.K + 1)) + 1
        self.steps = max(self.chunks, self.small_at) + 1
        self.seq = seq


def back_tile(i, a_ref, gate_ref, slant_ref, fc_ref, ic_ref, gr_ref, xp_ref, gres_ref, wg_ref, wo_ref, gain_ref,
              gin_ref, gm, gmt, ggb, ggain, state, perm):
    steps = gin_ref.shape[1]
    rows = steps * SUB
    hid = wg_ref.shape[1] // 3
    width = gm.shape[2]
    at = pl.ds(pl.multiple_of(gm.shape[1] - (i + 1) * rows, rows), rows)
    for j in range(hid // LANES):
        here = slice(j * LANES, (j + 1) * LANES)
        gs = dot_t(gr_ref[0], wo_ref[here, :])
        mu = state[:, here]
        lams = [None] * steps
        for r in range(steps - 1, -1, -1):
            sl = slice(r * SUB, (r + 1) * SUB)
            lams[r] = gs[sl] + mu
            mu = a_ref[sl, here] * lams[r]
        state[:, here] = mu
        lam = jnp.concatenate(lams, axis=0)
        gzc = lam * gate_ref[:, here].astype(F32)
        big = lam * slant_ref[:, here].astype(F32)
        parts = (
            (big * fc_ref[:, here].astype(F32)).astype(BF16),
            (-big * ic_ref[:, here].astype(F32)).astype(BF16),
            gzc.astype(BF16),
        )
        for g in range(3):
            first = g * hid + j * LANES
            cols = slice(first, first + LANES)
            gm[first // width, at, first % width : first % width + LANES] = parts[g]
            gmt[:, cols] = parts[g]
            ggb[:, cols] += fold_rows(parts[g].astype(F32))
    gn = dot_t(gmt[...], wg_ref[...])
    source = xp_ref[...].astype(F32)
    scale = inv_rms(source)
    w = gn * gain_ref[...]
    ggain[...] += fold_rows(gn * source * scale)
    gin = gres_ref[...] + scale * w - source * (scale * scale * scale) * jnp.mean(
        w * source, axis=-1, keepdims=True
    )
    gin_ref[...] = from_steps(gin, perm, steps)


def sum_kernel(
    work,
    prod_ref, mu_ref, gdb_ref, gub_ref, ggain2_ref, gob_ref, gain_ref, wg_ref, wo_ref,
    acts_ref, rows_ref, turned_ref, gu_ref,
    a_ref, gate_ref, slant_ref, fc_ref, ic_ref, gr_ref, xp_ref, gres_ref,
    gin_ref, small_ref, sums_hbm,
    acc, recv, gm, gmt, state, ggb, ggain, perm, small, got, mine, theirs,
    ssem, rsem, free, osem, s2sem, r2sem, csem, crsem,
):
    t = pl.program_id(0)
    plan = work.plan
    rows = work.rows
    s = lax.axis_index("seq")
    b = lax.axis_index("batch")
    ends = Ends(work.seq, mine, theirs, csem, crsem)

    who = [(s, flip(b, 1))] + [(o, b) for o in ends.others]
    who += [(s, flip(b, w)) for axis, w in plan.orders[0] if axis == "batch"]

    @pl.when(t == 0)
    def _():
        bar = pltpu.get_barrier_semaphore()
        for p in who:
            pl.semaphore_signal(bar, inc=1, device_id=p, device_id_type=MESH)
        ggb[...] = jnp.zeros_like(ggb)
        ggain[...] = jnp.zeros_like(ggain)

    @pl.when(t == work.first_tile)
    def _():
        ends.receive(prod_ref, mu_ref, state, True)

    def put(value):
        acc[pl.ds(pl.multiple_of(t * rows, rows), rows), :] = value

    @pl.when((t < work.at_up) | ((t >= work.at_out) & (t < work.at_gates)))
    def _():
        put(tdot(acts_ref[...], rows_ref[0]))

    @pl.when((t >= work.at_up) & (t < work.at_out))
    def _():
        put(dot(turned_ref[0], gu_ref[...]))

    @pl.when((t >= work.at_gates) & (t < work.chunks))
    def _():
        put(dot(turned_ref[0], gm[(t - work.at_gates) // work.halves]))

    @pl.when(t == 0)
    def _():
        pl.semaphore_wait(pltpu.get_barrier_semaphore(), len(who))
        ends.send(prod_ref, mu_ref, True)

    @pl.when(t == work.small_at)
    def _():
        line = 0
        for v in (ggain, ggb, gob_ref, ggain2_ref, gub_ref, gdb_ref):
            total = jnp.sum(v[...], axis=0, keepdims=True)
            for k in range(total.shape[1] // LANES):
                small[line : line + 1, :] = total[:, k * LANES : (k + 1) * LANES]
                line += 1
        if line < small.shape[0]:
            small[line:, :] = jnp.zeros((small.shape[0] - line, LANES), F32)

    def to_result(c):
        at = pl.ds(pl.multiple_of(c * rows, rows), rows)
        return pltpu.make_async_copy(acc.at[at], sums_hbm.at[at], osem.at[c])

    def step(now):
        for k in range(plan.K + 2):
            @pl.when(now == work.small_at + k * work.lag)
            def _():
                if k > 0:
                    small_copy(plan, small, got, s2sem, r2sem, k - 1).wait()
                    small[...] = small[...] + got[k - 1]
                if k <= plan.K:
                    small_copy(plan, small, got, s2sem, r2sem, k).start()
        tick(plan, work.chunks, acc, recv, ssem, rsem, free, now, lambda c: to_result(c).start())

    step(t)

    i = t - work.first_tile

    @pl.when((i >= 0) & (i < work.tiles))
    def _():
        back_tile(i, a_ref, gate_ref, slant_ref, fc_ref, ic_ref, gr_ref, xp_ref, gres_ref, wg_ref, wo_ref,
                  gain_ref, gin_ref, gm, gmt, ggb, ggain, state, perm)

    @pl.when(t == work.steps - 1)
    def _():
        def drain(now, _):
            step(now)
            return 0

        lax.fori_loop(work.steps, work.ticks, drain, 0)
        small_ref[...] = small[...]

        def wait(c, _):
            to_result(c).wait()
            return 0

        lax.fori_loop(0, work.chunks, wait, 0)


def last_kernel(work, sizes, pieces, small_ref, gin, sums, gin_o, down_o, up_o, out_o, gates_o, *rest):
    vecs, (gin_v, sums_v, insem, sem) = rest[:-4], rest[-4:]
    rows = work.rows
    d = rows * work.halves
    step = gin.shape[1] // pieces
    moves = []

    def move(src, via, dst):
        k = len(moves)
        read = pltpu.make_async_copy(src, via, insem.at[k])
        read.start()
        moves.append((read, pltpu.make_async_copy(via, dst, sem.at[k])))

    for k in range(pieces):
        part = lambda ref: ref.at[:, pl.ds(k * step, step)]
        move(part(gin), part(gin_v), part(gin_o))
    for first, count, ref, tall in (
        (0, work.down, down_o, True),
        (work.at_up, work.up, up_o, False),
        (work.at_out, work.out, out_o, True),
        (work.at_gates, work.gates, gates_o, False),
    ):
        for k in range(count):
            at = pl.ds((first + k) * rows, rows)
            if tall:
                dst = ref.at[pl.ds(k * rows, rows)]
            else:
                dst = ref.at[pl.ds(k % work.halves * rows, rows), pl.ds(k // work.halves * d, d)]
            move(sums.at[at], sums_v.at[at], dst)
    line = 0
    for ref, n in zip(vecs, sizes):
        for k in range(n // LANES):
            ref[:, k * LANES : (k + 1) * LANES] = small_ref[line : line + 1, :]
            line += 1
    for read, write in moves:
        read.wait()
        write.start()
    for _, write in moves:
        write.wait()


def full(shape):
    return pl.BlockSpec(shape, lambda i: (0,) * len(shape), pipeline_mode=pl.Buffered(1))


def held(shape):
    return pl.BlockSpec(shape, lambda i: (0,) * len(shape))


def per_device(seq, batch, inputs, cotangent, short_lengths, long_lengths, norm_gain, w_gates, gate_bias, w_out,
               out_bias, mlp_gain, w_up, up_bias, w_down, down_bias, tile=256, back=256):
    tok, d = inputs.shape[1:]
    hid = w_out.shape[0]
    ff = w_up.shape[1]
    piece = tok // SUB
    steps = tile // SUB
    grid = tok // tile
    halves = 2
    x = inputs.reshape(SUB, piece, d)
    dy = cotangent.reshape(SUB, piece, d)
    gain1 = norm_gain.reshape(1, d)
    gain2 = mlp_gain.reshape(1, d)
    sds = jax.ShapeDtypeStruct
    rows = lambda n: pl.BlockSpec((tile, n), lambda i: (i, 0))
    natural = pl.BlockSpec((SUB, steps, d), lambda i: (0, i, 0))
    turned = pl.BlockSpec((d, tile), lambda i: (0, i))
    params = pltpu.CompilerParams(
        dimension_semantics=("arbitrary",), vmem_limit_bytes=56 << 20
    )
    a, b, zc, fc, ic, xp, nt, prod, enter = pl.pallas_call(
        functools.partial(gates_kernel, piece, seq),
        grid=(grid,),
        in_specs=[
            pl.BlockSpec(memory_space=pltpu.SMEM), pl.BlockSpec(memory_space=pltpu.SMEM),
            natural, full((1, d)), full((d, 3 * hid)), full((1, 3 * hid)),
        ],
        out_specs=[rows(hid)] * 5 + [rows(d), turned, held((SUB, hid)), held((SUB, hid))],
        out_shape=[sds((tok, hid), F32)] * 3 + [sds((tok, hid), BF16)] * 2
        + [sds((tok, d), BF16), sds((d, tok), BF16), sds((SUB, hid), F32), sds((SUB, hid), F32)],
        scratch_shapes=[pltpu.VMEM((d // 128, tile + SUB * SUB, 128), F32), pltpu.VMEM((SUB, hid), F32)]
        + ends_scratch(seq, hid),
        compiler_params=pltpu.CompilerParams(
            dimension_semantics=("arbitrary",), collective_id=1, has_side_effects=True, vmem_limit_bytes=56 << 20
        ),
    )(short_lengths, long_lengths.T, x, gain1, w_gates, gate_bias.reshape(1, 3 * hid))

    outs = pl.pallas_call(
        mlp_kernel,
        grid=(grid,),
        in_specs=[rows(hid)] * 3 + [rows(d), turned, natural, full((SUB, hid)), full((hid, d)), full((d, ff)), full((ff, d)),
                  full((1, d)), full((1, d)), full((1, ff)), full((1, d))],
        out_specs=[rows(hid), rows(hid), rows(ff + hid), rows(ff), pl.BlockSpec((2, tile, d), lambda i: (0, i, 0)),
                   pl.BlockSpec((2, halves, d // halves, tile), lambda i: (0, 0, 0, i)), rows(d), natural,
                   held((SUB, hid)), held((SUB, d)), held((SUB, ff)), held((SUB, d)), held((SUB, d))],
        out_shape=[sds((tok, hid), BF16), sds((tok, hid), BF16), sds((tok, ff + hid), BF16), sds((tok, ff), BF16), sds((2, tok, d), BF16),
                   sds((2, halves, d // halves, tok), BF16), sds((tok, d), F32),
                   sds((SUB, piece, d), BF16),
                   sds((SUB, hid), F32), sds((SUB, d), F32), sds((SUB, ff), F32), sds((SUB, d), F32), sds((SUB, d), F32)],
        scratch_shapes=[pltpu.VMEM((SUB, hid), F32), pltpu.VMEM((SUB, hid), F32), pltpu.VMEM((d // 128, tile + SUB * SUB, 128), F32),
                        pltpu.VMEM((tile, hid), F32)],
        compiler_params=params,
    )(a, b, zc, xp, nt, dy, enter, w_out, w_up, w_down, out_bias.reshape(1, d), gain2, up_bias.reshape(1, ff),
      down_bias.reshape(1, d))
    gate, slant, acts, gu, pairs, turns, gres, result, mu, gdb, gub, ggain2, gob = outs

    turns = turns.reshape(2 * halves, d // halves, tok)
    work = Work(d, hid, ff, d // halves, tok // back, LAG, seq, batch)
    plan = work.plan
    slots = plan.colors * 2
    bsteps = back // SUB
    lines = -(-(4 * d + 3 * hid + ff) // (8 * LANES)) * 8

    def at_tile(t):
        return work.tiles - 1 - jnp.clip(t - work.first_tile, 0, work.tiles - 1)

    btile = lambda n: pl.BlockSpec((back, n), lambda t: (at_tile(t), 0))
    any_space = pl.BlockSpec(memory_space=pl.ANY)

    def acts_at(t):
        late = jnp.clip(t - work.up, work.down, work.down + work.out - 1)
        return (0, jnp.where(t < work.down, t, late))

    def turned_at(t):
        up = jnp.clip(t - work.at_up, 0, work.up - 1) % halves
        gates = halves + jnp.clip(t - work.at_gates, 0, work.gates - 1) % halves
        return (jnp.where(t < work.at_out, up, gates), 0, 0)

    gin, small, sums = pl.pallas_call(
        functools.partial(sum_kernel, work),
        grid=(work.steps,),
        in_specs=[full((SUB, hid)), full((SUB, hid)), full((SUB, d)), full((SUB, ff)), full((SUB, d)), full((SUB, d)),
                  full((1, d)), full((d, 3 * hid)), full((hid, d)),
                  pl.BlockSpec((tok, work.rows), acts_at),
                  pl.BlockSpec((1, tok, d), lambda t: (jnp.where(t < work.at_up, 0, 1), 0, 0), pipeline_mode=pl.Buffered(1)),
                  pl.BlockSpec((1, work.rows, tok), turned_at),
                  pl.BlockSpec((tok, d), lambda t: (0, jnp.clip(t - work.at_up, 0, work.up - 1) // halves))]
        + [btile(hid)] * 5 + [pl.BlockSpec((1, back, d), lambda t: (1, at_tile(t), 0))] + [btile(d)] * 2,
        out_specs=[pl.BlockSpec((SUB, bsteps, d), lambda t: (0, at_tile(t), 0)), held((lines, LANES)), any_space],
        out_shape=[sds((SUB, piece, d), F32), sds((lines, LANES), F32), sds((work.chunks * work.rows, d), F32)],
        scratch_shapes=[
            pltpu.VMEM((work.chunks * work.rows, d), F32),
            pltpu.VMEM((slots, plan.recv_rows, d), F32),
            pltpu.VMEM((3 * hid // d, tok, d), BF16),
            pltpu.VMEM((back, 3 * hid), BF16),
            pltpu.VMEM((SUB, hid), F32),
            pltpu.VMEM((SUB, 3 * hid), F32),
            pltpu.VMEM((SUB, d), F32),
            pltpu.VMEM((d // 128, back + SUB * SUB, 128), F32),
            pltpu.VMEM((lines, LANES), F32),
            pltpu.VMEM((plan.K + 1, lines, LANES), F32),
            *ends_scratch(seq, hid)[:2],
            pltpu.SemaphoreType.DMA((slots, plan.stages)),
            pltpu.SemaphoreType.DMA((slots, plan.stages)),
            pltpu.SemaphoreType.REGULAR((slots, plan.K + 1)),
            pltpu.SemaphoreType.DMA((work.chunks,)),
            pltpu.SemaphoreType.DMA((plan.K + 1,)),
            pltpu.SemaphoreType.DMA((plan.K + 1,)),
            *ends_scratch(seq, hid)[2:],
        ],
        compiler_params=pltpu.CompilerParams(
            dimension_semantics=("arbitrary",), collective_id=0, has_side_effects=True, vmem_limit_bytes=62 << 20
        ),
    )(prod, mu, gdb, gub, ggain2, gob, gain1, w_gates, w_out, acts, pairs, turns, gu,
      a, gate, slant, fc, ic, pairs, xp, gres)
    sizes = (d, 3 * hid, d, d, ff, d)
    vmem = pl.BlockSpec(memory_space=pltpu.VMEM)
    gin, g_down, g_up, g_out, g_gates, *vecs = pl.pallas_call(
        functools.partial(last_kernel, work, sizes, grid),
        in_specs=[vmem, any_space, any_space],
        out_specs=[any_space] * 5 + [vmem] * 6,
        out_shape=[sds(gin.shape, F32), sds((ff, d), F32), sds((d, ff), F32), sds((hid, d), F32), sds((d, 3 * hid), F32)]
        + [sds((1, n), F32) for n in sizes],
        scratch_shapes=[pltpu.VMEM(gin.shape, F32), pltpu.VMEM(sums.shape, F32),
                        pltpu.SemaphoreType.DMA((grid + work.chunks,)), pltpu.SemaphoreType.DMA((grid + work.chunks,))],
        compiler_params=pltpu.CompilerParams(vmem_limit_bytes=62 << 20),
    )(small, gin, sums)
    ggain1, ggb, gob, ggain2, gub, gdb = [v.reshape(-1) for v in vecs]
    return (result.reshape(inputs.shape), gin.reshape(inputs.shape), ggain1, g_gates, ggb, g_out, gob,
            ggain2, g_up, gub, g_down, gdb)


def solution(mesh):
    rows = P("batch", "seq", None)
    return jax.shard_map(
        functools.partial(per_device, mesh.shape["seq"], mesh.shape["batch"]),
        mesh=mesh,
        in_specs=(rows, rows) + (P(),) * 12,
        out_specs=(rows, rows) + (P(),) * 10,
        check_vma=False,
    )
```

```python
import functools

import jax
import jax.numpy as jnp
from jax import lax
from jax.experimental import pallas as pl
from jax.experimental.pallas import tpu as pltpu
from jax.sharding import PartitionSpec as P

MESH = pl.DeviceIdType.MESH
F32 = jnp.float32
BF16 = jnp.bfloat16
epsilon = 1e-06
SUB = 8
LANES = 256
LAG = 3


def flip(v, w):
    return v + w - 2 * w * ((v // w) % 2)


def dot(a, b):
    return jnp.dot(a, b, preferred_element_type=F32)


def dot_t(a, b):
    return lax.dot_general(a, b, (((1,), (1,)), ((), ())), preferred_element_type=F32)


def fold_rows(v):
    return jnp.sum(v.reshape(v.shape[0] // SUB, SUB, v.shape[1]), axis=0)


def inv_rms(v):
    return lax.rsqrt(jnp.mean(v * v, axis=-1, keepdims=True) + epsilon)


def to_steps(block, scratch):
    pieces, steps, n = block.shape
    flat = block.astype(F32).reshape(pieces * steps, n)
    parts = []
    for k in range(n // 128):
        for c in range(pieces):
            scratch[k, c * (steps + SUB) : c * (steps + SUB) + steps, :] = flat[
                c * steps : (c + 1) * steps, k * 128 : (k + 1) * 128
            ]
        parts.append(
            jnp.concatenate(
                [scratch[k, pl.ds(r, pieces, stride=steps + SUB), :] for r in range(steps)], axis=0
            )
        )
    return jnp.concatenate(parts, axis=1)


def from_steps(value, scratch, steps):
    n = value.shape[1]
    parts = []
    for k in range(n // 128):
        for r in range(steps):
            scratch[k, pl.ds(r, SUB, stride=steps + SUB), :] = value[
                r * SUB : (r + 1) * SUB, k * 128 : (k + 1) * 128
            ]
        parts.append(
            jnp.concatenate(
                [scratch[k, c * (steps + SUB) : c * (steps + SUB) + steps, :] for c in range(SUB)], axis=0
            )
        )
    return jnp.concatenate(parts, axis=1).reshape(SUB, steps, n)


class Ends:
    def __init__(self, devices, mine, theirs, ssem, rsem):
        self.devices = devices
        self.mine = mine
        self.theirs = theirs
        self.at = lax.axis_index("seq")
        self.group = lax.axis_index("batch")
        self.others = [lax.rem(self.at + k, devices) for k in range(1, devices)]
        self.copies = [
            pltpu.make_async_remote_copy(
                src_ref=mine, dst_ref=theirs.at[k], send_sem=ssem.at[k], recv_sem=rsem.at[k],
                device_id=(other, self.group), device_id_type=MESH,
            )
            for k, other in enumerate(self.others)
        ]

    def greet(self):
        bar = pltpu.get_barrier_semaphore()
        for other in self.others:
            pl.semaphore_signal(bar, inc=1, device_id=(other, self.group), device_id_type=MESH)

    def send(self, prod_ref, sum_ref, reverse):
        width = prod_ref.shape[1]
        prod = jnp.ones((1, width), F32)
        total = jnp.zeros((1, width), F32)
        for c in range(SUB - 1, -1, -1) if reverse else range(SUB):
            prod = prod * prod_ref[c : c + 1, :]
            total = total * prod_ref[c : c + 1, :] + sum_ref[c : c + 1, :]
        half = SUB // 2
        part = width // half
        for k in range(half):
            self.mine[k : k + 1, :] = prod[:, k * part : (k + 1) * part]
            self.mine[half + k : half + k + 1, :] = total[:, k * part : (k + 1) * part]
        for copy in self.copies:
            copy.start()

    def receive(self, prod_ref, sum_ref, out_ref, reverse):
        for copy in self.copies:
            copy.wait()
        n = self.devices
        now = jnp.zeros((1, prod_ref.shape[1]), F32)
        for owner in range(n - 1, 0, -1) if reverse else range(n - 1):
            back = lax.rem(self.at - owner + n, n)
            slot = jnp.where(back == 0, 0, back - 1)
            got = self.theirs[slot]
            half = SUB // 2
            prod, total = [
                jnp.concatenate([got[k : k + 1] for k in range(f, f + half)], axis=1) for f in (0, half)
            ]
            new = prod * now + total
            now = jnp.where(owner > self.at if reverse else owner < self.at, new, now)
        for c in range(SUB - 1, -1, -1) if reverse else range(SUB):
            out_ref[c : c + 1, :] = now
            now = prod_ref[c : c + 1, :] * now + sum_ref[c : c + 1, :]


def ends_scratch(devices, width):
    return [
        pltpu.VMEM((SUB, width * 2 // SUB), F32),
        pltpu.VMEM((devices - 1, SUB, width * 2 // SUB), F32),
        pltpu.SemaphoreType.DMA((devices - 1,)),
        pltpu.SemaphoreType.DMA((devices - 1,)),
    ]


def gates_kernel(
    piece, devices, short_ref, long_ref, x_ref, gain_ref, wg_ref, bias_ref,
    a_ref, b_ref, zc_ref, fc_ref, ic_ref, xp_ref, nt_ref, prod_ref, enter_ref,
    perm, sum_ref, mine, theirs, ssem, rsem,
):
    i = pl.program_id(0)
    ends = Ends(devices, mine, theirs, ssem, rsem)
    steps = x_ref.shape[1]
    rows = steps * SUB
    hid = wg_ref.shape[1] // 3
    source = to_steps(x_ref[...], perm)
    xp_ref[...] = source.astype(BF16)
    normed = (source * inv_rms(source) * gain_ref[...]).astype(BF16)
    nt_ref[...] = normed.T

    group = lax.axis_index("batch")
    half = short_ref.shape[0]
    first = lax.axis_index("seq") * piece * SUB
    row = lax.broadcasted_iota(jnp.int32, (rows, 128), 0)
    pos = first + (row % SUB) * piece + i * steps + row // SUB
    short = group < half
    srow = jnp.minimum(group, half - 1)
    lrow = jnp.maximum(group - half, 0)
    begins = jnp.zeros((rows, 128), jnp.bool_)
    at = jnp.int32(0)
    for k in range(short_ref.shape[1]):
        begins = begins | (pos == jnp.where(short, at, -1))
        at = at + short_ref[srow, k]
    at = jnp.int32(0)
    for k in range(long_ref.shape[0]):
        begins = begins | (pos == jnp.where(short, -1, at))
        at = at + long_ref[k, lrow]
    keep = jnp.where(begins, 0.0, 1.0).astype(F32)

    @pl.when(i == 0)
    def _():
        ends.greet()
        prod_ref[...] = jnp.ones_like(prod_ref)
        sum_ref[...] = jnp.zeros_like(sum_ref)

    for j in range(hid // LANES):
        cols = [slice(g * hid + j * LANES, g * hid + (j + 1) * LANES) for g in range(3)]
        zf, zi, zc = [dot(normed, wg_ref[:, c]) + bias_ref[:, c] for c in cols]
        f = 1.0 / (1.0 + jnp.exp(-zf))
        g = 1.0 / (1.0 + jnp.exp(-zi))
        inv = 1.0 / (f + g)
        a = f * inv * jnp.concatenate([keep] * (LANES // 128), axis=1)
        b = g * inv
        here = cols[0]
        a_ref[:, here] = a
        b_ref[:, here] = b
        zc_ref[:, here] = zc
        fc_ref[:, here] = (1.0 - f).astype(BF16)
        ic_ref[:, here] = (1.0 - g).astype(BF16)
        u = b * zc
        prod = prod_ref[:, here]
        total = sum_ref[:, here]
        for r in range(steps):
            sl = slice(r * SUB, (r + 1) * SUB)
            prod = prod * a[sl]
            total = total * a[sl] + u[sl]
        prod_ref[:, here] = prod
        sum_ref[:, here] = total


    @pl.when(i == pl.num_programs(0) - 1)
    def _():
        pl.semaphore_wait(pltpu.get_barrier_semaphore(), devices - 1)
        ends.send(prod_ref, sum_ref, False)
        ends.receive(prod_ref, sum_ref, enter_ref, False)


KA = 0.3275911 * 2.0**-0.5
ERF = [0.5 * c for c in (0.254829592, -0.284496736, 1.421413741, -1.453152027, 1.061405429)]
PHI = 0.3989422804014327


def gelu_parts(x):
    t = 1.0 / (1.0 + KA * jnp.abs(x))
    e = jnp.exp2(x * x * (-0.5 * 1.4426950408889634))
    poly = t * (ERF[0] + t * (ERF[1] + t * (ERF[2] + t * (ERF[3] + t * ERF[4]))))
    tail = poly * e
    phi = jnp.where(x >= 0.0, 1.0 - tail, tail)
    return x * phi, phi + x * (e * PHI)


def mlp_kernel(
    a_ref, b_ref, zc_ref, xp_ref, nt_ref, dy_ref, carry_ref, wo_ref, wu_ref, wd_ref,
    obias_ref, gain_ref, ubias_ref, dbias_ref,
    gate_ref, slant_ref, acts_ref, gu_ref, rows_ref, turned_ref, gres_ref, result_ref,
    mu_ref, gdb_ref, gub_ref, ggain_ref, gob_ref,
    state, prod, perm, s_ref,
):
    i = pl.program_id(0)
    steps = dy_ref.shape[1]

    @pl.when(i == 0)
    def _():
        state[...] = carry_ref[...]
        prod[...] = jnp.ones_like(prod)
        for ref in (mu_ref, gdb_ref, gub_ref, ggain_ref, gob_ref):
            ref[...] = jnp.zeros_like(ref)

    st = state[...]
    for r in range(steps):
        sl = slice(r * SUB, (r + 1) * SUB)
        st = a_ref[sl, :] * st + b_ref[sl, :] * zc_ref[sl, :]
        s_ref[sl, :] = st
    state[...] = st
    sb = s_ref[...].astype(BF16)
    gate_ref[...] = b_ref[...].astype(BF16)
    slant_ref[...] = (b_ref[...] * (s_ref[...] - zc_ref[...])).astype(BF16)
    ff = wu_ref.shape[1]
    acts_ref[:, ff:] = sb
    source = xp_ref[...].astype(F32)
    resid = source + dot(sb, wo_ref[...]) + obias_ref[...]
    scale = inv_rms(resid)
    n2 = (resid * scale * gain_ref[...]).astype(BF16)
    half = turned_ref.shape[2]
    turned_ref[0] = n2.T.reshape(-1, half, n2.shape[0])
    turned_ref[1] = nt_ref[...].reshape(-1, half, n2.shape[0])
    dy32 = to_steps(dy_ref[...], perm)
    dy = dy32.astype(BF16)
    rows_ref[0] = dy
    gdb_ref[...] += fold_rows(dy32)
    down = None
    gn2 = None
    for j in range(wu_ref.shape[1] // LANES):
        cols = slice(j * LANES, (j + 1) * LANES)
        upper = dot(n2, wu_ref[:, cols]) + ubias_ref[:, cols]
        act, slope = gelu_parts(upper)
        act = act.astype(BF16)
        acts_ref[:, cols] = act
        gact = dot_t(dy, wd_ref[cols, :])
        gu = (gact * slope).astype(BF16)
        gu_ref[:, cols] = gu
        gub_ref[:, cols] += fold_rows(gu.astype(F32))
    down = dot(acts_ref[:, :ff], wd_ref[...])
    gn2 = dot_t(gu_ref[...], wu_ref[...])
    result = resid + down + dbias_ref[...]
    result_ref[...] = from_steps(result, perm, steps).astype(BF16)
    w = gn2 * gain_ref[...]
    ggain_ref[...] += fold_rows(gn2 * resid * scale)
    gres = dy32 + scale * w - resid * (scale * scale * scale) * jnp.mean(
        w * resid, axis=-1, keepdims=True
    )
    gres_ref[...] = gres
    gr = gres.astype(BF16)
    gob_ref[...] += fold_rows(gr.astype(F32))
    rows_ref[1] = gr
    gs = dot_t(gr, wo_ref[...])
    pr = prod[...]
    mu = mu_ref[...]
    for r in range(steps):
        sl = slice(r * SUB, (r + 1) * SUB)
        pr = pr * a_ref[sl, :]
        mu = mu + pr * gs[sl, :]
    prod[...] = pr
    mu_ref[...] = mu


def bits_of(size):
    w = 1
    out = []
    while w < size:
        out.append(w); w *= 2
    return out

def stage_ticks(j, stages):
    return 2 if j in (0, stages - 1) else LAG


class Plan:
    def __init__(self, seq, batch, rows):
        sb = [("seq", w) for w in bits_of(seq)]
        bb = [("batch", w) for w in bits_of(batch)][1:]
        self.orders = [sb + bb, sb[::-1] + bb, bb[:1] + sb + bb[1:]]
        self.K = len(sb) + len(bb)
        self.rows = rows
        self.sizes = [rows]
        self.halve = []
        for k in range(self.K + 1):
            h = self.sizes[-1] >= 16
            self.halve.append(h)
            self.sizes.append(self.sizes[-1] // 2 if h else self.sizes[-1])
        self.stages = 2 * (self.K + 1)
        self.colors = len(self.orders)
        self.begins = [0]
        for j in range(self.stages):
            self.begins.append(self.begins[-1] + stage_ticks(j, self.stages))
        self.base = []
        tot = 0
        for k in range(self.K + 1):
            self.base.append(tot); tot += self.sizes[k + 1]
        self.recv_rows = tot

def pick(color, values):
    out = values[-1]
    for i in range(len(values) - 1):
        out = jnp.where(color == i, values[i], out)
    return out

def step_info(plan, k, color):
    s = lax.axis_index("seq"); b = lax.axis_index("batch")
    if k == 0:
        return b % 2, (s, flip(b, 1))
    mine, ps, pb = [], [], []
    for order in plan.orders:
        axis, w = order[k - 1]
        if axis == "seq":
            mine.append((s // w) % 2); ps.append(flip(s, w)); pb.append(b)
        else:
            mine.append((b // w) % 2); ps.append(s); pb.append(flip(b, w))
    return pick(color, mine), (pick(color, ps), pick(color, pb))

def offsets(plan, c, color, upto):
    off = c * plan.rows
    for k in range(upto):
        if plan.halve[k]:
            bit, _ = step_info(plan, k, color)
            off = off + bit * plan.sizes[k + 1]
    return pl.multiple_of(off, 8)

def copy_of(plan, acc, recv, ssem, rsem, c, j):
    color = c % plan.colors
    slot = color * 2 + (c // plan.colors) % 2
    K = plan.K
    if j <= K:
        k = j
        bit, dev = step_info(plan, k, color)
        n = plan.sizes[k + 1]
        base = offsets(plan, c, color, k)
        src = base + (1 - bit) * n if plan.halve[k] else base
        return pltpu.make_async_remote_copy(
            src_ref=acc.at[pl.ds(pl.multiple_of(src, 8), n)], dst_ref=recv.at[slot, pl.ds(plan.base[k], n)],
            send_sem=ssem.at[slot, j], recv_sem=rsem.at[slot, j], device_id=dev, device_id_type=MESH)
    k = 2 * K + 1 - j
    if not plan.halve[k]:
        return None
    bit, dev = step_info(plan, k, color)
    n = plan.sizes[k + 1]
    mine = offsets(plan, c, color, k + 1)
    return pltpu.make_async_remote_copy(
        src_ref=acc.at[pl.ds(mine, n)], dst_ref=acc.at[pl.ds(mine, n)],
        send_sem=ssem.at[slot, j], recv_sem=rsem.at[slot, j], device_id=dev, device_id_type=MESH)

def finish(plan, acc, recv, ssem, rsem, free, c, j):
    cp = copy_of(plan, acc, recv, ssem, rsem, c, j)
    if cp is None:
        return
    cp.wait()
    if j <= plan.K:
        color = c % plan.colors
        slot = color * 2 + (c // plan.colors) % 2
        n = plan.sizes[j + 1]
        if plan.halve[j]:
            _, dev = step_info(plan, j, color)
            pl.semaphore_signal(free.at[slot, j], inc=1, device_id=dev, device_id_type=MESH)
        off = offsets(plan, c, color, j + 1)
        acc[pl.ds(off, n), :] = acc[pl.ds(off, n), :] + recv[slot, pl.ds(plan.base[j], n), :]

def tick(plan, nchunks, acc, recv, ssem, rsem, free, t, done):
    for j in range(plan.stages, -1, -1):
        c = t - plan.begins[j]
        @pl.when((c >= 0) & (c < nchunks))
        def _():
            if j > 0:
                finish(plan, acc, recv, ssem, rsem, free, c, j - 1)
            if j < plan.stages:
                cp = copy_of(plan, acc, recv, ssem, rsem, c, j)
                if cp is not None:
                    if j > plan.K:
                        color = c % plan.colors
                        slot = color * 2 + (c // plan.colors) % 2
                        pl.semaphore_wait(free.at[slot, 2 * plan.K + 1 - j], 1)
                    cp.start()
            else:
                done(c)


def small_copy(plan, small, got, ssem, rsem, k):
    _, dev = step_info(plan, k, 0)
    return pltpu.make_async_remote_copy(
        src_ref=small, dst_ref=got.at[k], send_sem=ssem.at[k], recv_sem=rsem.at[k],
        device_id=dev, device_id_type=MESH)


def tdot(a, b):
    return lax.dot_general(a, b, (((0,), (0,)), ((), ())), preferred_element_type=F32)


class Work:
    def __init__(self, d, hid, ff, rows, tiles, lag, seq, batch):
        self.rows = rows
        self.halves = d // rows
        self.down = ff // rows
        self.up = ff // d * self.halves
        self.out = hid // rows
        self.gates = 3 * hid // d * self.halves
        self.at_up = self.down
        self.at_out = self.at_up + self.up
        self.at_gates = self.at_out + self.out
        self.chunks = self.at_gates + self.gates
        self.plan = Plan(seq, batch, rows)
        self.lag = lag
        self.tiles = tiles
        self.first_tile = max(2, min(6, self.at_gates - tiles))
        self.small_at = max(self.first_tile + tiles, self.at_gates)
        self.ticks = max(self.chunks + self.plan.begins[-1], self.small_at + lag * (self.plan.K + 1)) + 1
        self.steps = max(self.chunks, self.small_at) + 1
        self.seq = seq


def back_tile(i, a_ref, gate_ref, slant_ref, fc_ref, ic_ref, gr_ref, xp_ref, gres_ref, wg_ref, wo_ref, gain_ref,
              gin_ref, gm, gmt, ggb, ggain, state, perm):
    steps = gin_ref.shape[1]
    rows = steps * SUB
    hid = wg_ref.shape[1] // 3
    width = gm.shape[2]
    at = pl.ds(pl.multiple_of(gm.shape[1] - (i + 1) * rows, rows), rows)
    for j in range(hid // LANES):
        here = slice(j * LANES, (j + 1) * LANES)
        gs = dot_t(gr_ref[0], wo_ref[here, :])
        mu = state[:, here]
        lams = [None] * steps
        for r in range(steps - 1, -1, -1):
            sl = slice(r * SUB, (r + 1) * SUB)
            lams[r] = gs[sl] + mu
            mu = a_ref[sl, here] * lams[r]
        state[:, here] = mu
        lam = jnp.concatenate(lams, axis=0)
        gzc = lam * gate_ref[:, here].astype(F32)
        big = lam * slant_ref[:, here].astype(F32)
        parts = (
            (big * fc_ref[:, here].astype(F32)).astype(BF16),
            (-big * ic_ref[:, here].astype(F32)).astype(BF16),
            gzc.astype(BF16),
        )
        for g in range(3):
            first = g * hid + j * LANES
            cols = slice(first, first + LANES)
            gm[first // width, at, first % width : first % width + LANES] = parts[g]
            gmt[:, cols] = parts[g]
            ggb[:, cols] += fold_rows(parts[g].astype(F32))
    gn = dot_t(gmt[...], wg_ref[...])
    source = xp_ref[...].astype(F32)
    scale = inv_rms(source)
    w = gn * gain_ref[...]
    ggain[...] += fold_rows(gn * source * scale)
    gin = gres_ref[...] + scale * w - source * (scale * scale * scale) * jnp.mean(
        w * source, axis=-1, keepdims=True
    )
    gin_ref[...] = from_steps(gin, perm, steps)


def sum_kernel(
    work,
    prod_ref, mu_ref, gdb_ref, gub_ref, ggain2_ref, gob_ref, gain_ref, wg_ref, wo_ref,
    acts_ref, rows_ref, turned_ref, gu_ref,
    a_ref, gate_ref, slant_ref, fc_ref, ic_ref, gr_ref, xp_ref, gres_ref,
    gin_ref, small_ref, sums_hbm,
    acc, recv, gm, gmt, state, ggb, ggain, perm, small, got, mine, theirs,
    ssem, rsem, free, osem, s2sem, r2sem, csem, crsem,
):
    t = pl.program_id(0)
    plan = work.plan
    rows = work.rows
    s = lax.axis_index("seq")
    b = lax.axis_index("batch")
    ends = Ends(work.seq, mine, theirs, csem, crsem)

    who = [(s, flip(b, 1))] + [(o, b) for o in ends.others]
    who += [(s, flip(b, w)) for axis, w in plan.orders[0] if axis == "batch"]

    @pl.when(t == 0)
    def _():
        bar = pltpu.get_barrier_semaphore()
        for p in who:
            pl.semaphore_signal(bar, inc=1, device_id=p, device_id_type=MESH)
        ggb[...] = jnp.zeros_like(ggb)
        ggain[...] = jnp.zeros_like(ggain)

    @pl.when(t == work.first_tile)
    def _():
        ends.receive(prod_ref, mu_ref, state, True)

    def put(value):
        acc[pl.ds(pl.multiple_of(t * rows, rows), rows), :] = value

    @pl.when((t < work.at_up) | ((t >= work.at_out) & (t < work.at_gates)))
    def _():
        put(tdot(acts_ref[...], rows_ref[0]))

    @pl.when((t >= work.at_up) & (t < work.at_out))
    def _():
        put(dot(turned_ref[0], gu_ref[...]))

    @pl.when((t >= work.at_gates) & (t < work.chunks))
    def _():
        put(dot(turned_ref[0], gm[(t - work.at_gates) // work.halves]))

    @pl.when(t == 0)
    def _():
        pl.semaphore_wait(pltpu.get_barrier_semaphore(), len(who))
        ends.send(prod_ref, mu_ref, True)

    @pl.when(t == work.small_at)
    def _():
        line = 0
        for v in (ggain, ggb, gob_ref, ggain2_ref, gub_ref, gdb_ref):
            total = jnp.sum(v[...], axis=0, keepdims=True)
            for k in range(total.shape[1] // LANES):
                small[line : line + 1, :] = total[:, k * LANES : (k + 1) * LANES]
                line += 1
        if line < small.shape[0]:
            small[line:, :] = jnp.zeros((small.shape[0] - line, LANES), F32)

    def to_result(c):
        at = pl.ds(pl.multiple_of(c * rows, rows), rows)
        return pltpu.make_async_copy(acc.at[at], sums_hbm.at[at], osem.at[c])

    def step(now):
        for k in range(plan.K + 2):
            @pl.when(now == work.small_at + k * work.lag)
            def _():
                if k > 0:
                    small_copy(plan, small, got, s2sem, r2sem, k - 1).wait()
                    small[...] = small[...] + got[k - 1]
                if k <= plan.K:
                    small_copy(plan, small, got, s2sem, r2sem, k).start()
        tick(plan, work.chunks, acc, recv, ssem, rsem, free, now, lambda c: to_result(c).start())

    step(t)

    i = t - work.first_tile

    @pl.when((i >= 0) & (i < work.tiles))
    def _():
        back_tile(i, a_ref, gate_ref, slant_ref, fc_ref, ic_ref, gr_ref, xp_ref, gres_ref, wg_ref, wo_ref,
                  gain_ref, gin_ref, gm, gmt, ggb, ggain, state, perm)

    @pl.when(t == work.steps - 1)
    def _():
        def drain(now, _):
            step(now)
            return 0

        lax.fori_loop(work.steps, work.ticks, drain, 0)
        small_ref[...] = small[...]

        def wait(c, _):
            to_result(c).wait()
            return 0

        lax.fori_loop(0, work.chunks, wait, 0)


def last_kernel(work, sizes, pieces, small_ref, gin, sums, gin_o, down_o, up_o, out_o, gates_o, *rest):
    vecs, (gin_v, sums_v, insem, sem) = rest[:-4], rest[-4:]
    rows = work.rows
    d = rows * work.halves
    step = gin.shape[1] // pieces
    moves = []

    def move(src, via, dst):
        k = len(moves)
        read = pltpu.make_async_copy(src, via, insem.at[k])
        read.start()
        moves.append((read, pltpu.make_async_copy(via, dst, sem.at[k])))

    for k in range(pieces):
        part = lambda ref: ref.at[:, pl.ds(k * step, step)]
        move(part(gin), part(gin_v), part(gin_o))
    for first, count, ref, tall in (
        (0, work.down, down_o, True),
        (work.at_up, work.up, up_o, False),
        (work.at_out, work.out, out_o, True),
        (work.at_gates, work.gates, gates_o, False),
    ):
        for k in range(count):
            at = pl.ds((first + k) * rows, rows)
            if tall:
                dst = ref.at[pl.ds(k * rows, rows)]
            else:
                dst = ref.at[pl.ds(k % work.halves * rows, rows), pl.ds(k // work.halves * d, d)]
            move(sums.at[at], sums_v.at[at], dst)
    line = 0
    for ref, n in zip(vecs, sizes):
        for k in range(n // LANES):
            ref[:, k * LANES : (k + 1) * LANES] = small_ref[line : line + 1, :]
            line += 1
    for read, write in moves:
        read.wait()
        write.start()
    for _, write in moves:
        write.wait()


def full(shape):
    return pl.BlockSpec(shape, lambda i: (0,) * len(shape), pipeline_mode=pl.Buffered(1))


def held(shape):
    return pl.BlockSpec(shape, lambda i: (0,) * len(shape))


def per_device(seq, batch, inputs, cotangent, short_lengths, long_lengths, norm_gain, w_gates, gate_bias, w_out,
               out_bias, mlp_gain, w_up, up_bias, w_down, down_bias, tile=256, back=256):
    tok, d = inputs.shape[1:]
    hid = w_out.shape[0]
    ff = w_up.shape[1]
    piece = tok // SUB
    steps = tile // SUB
    grid = tok // tile
    halves = 2
    x = inputs.reshape(SUB, piece, d)
    dy = cotangent.reshape(SUB, piece, d)
    gain1 = norm_gain.reshape(1, d)
    gain2 = mlp_gain.reshape(1, d)
    sds = jax.ShapeDtypeStruct
    rows = lambda n: pl.BlockSpec((tile, n), lambda i: (i, 0))
    natural = pl.BlockSpec((SUB, steps, d), lambda i: (0, i, 0))
    turned = pl.BlockSpec((d, tile), lambda i: (0, i))
    params = pltpu.CompilerParams(
        dimension_semantics=("arbitrary",), vmem_limit_bytes=56 << 20
    )
    a, b, zc, fc, ic, xp, nt, prod, enter = pl.pallas_call(
        functools.partial(gates_kernel, piece, seq),
        grid=(grid,),
        in_specs=[
            pl.BlockSpec(memory_space=pltpu.SMEM), pl.BlockSpec(memory_space=pltpu.SMEM),
            natural, full((1, d)), full((d, 3 * hid)), full((1, 3 * hid)),
        ],
        out_specs=[rows(hid)] * 5 + [rows(d), turned, held((SUB, hid)), held((SUB, hid))],
        out_shape=[sds((tok, hid), F32)] * 3 + [sds((tok, hid), BF16)] * 2
        + [sds((tok, d), BF16), sds((d, tok), BF16), sds((SUB, hid), F32), sds((SUB, hid), F32)],
        scratch_shapes=[pltpu.VMEM((d // 128, tile + SUB * SUB, 128), F32), pltpu.VMEM((SUB, hid), F32)]
        + ends_scratch(seq, hid),
        compiler_params=pltpu.CompilerParams(
            dimension_semantics=("arbitrary",), collective_id=1, has_side_effects=True, vmem_limit_bytes=56 << 20
        ),
    )(short_lengths, long_lengths.T, x, gain1, w_gates, gate_bias.reshape(1, 3 * hid))

    outs = pl.pallas_call(
        mlp_kernel,
        grid=(grid,),
        in_specs=[rows(hid)] * 3 + [rows(d), turned, natural, full((SUB, hid)), full((hid, d)), full((d, ff)), full((ff, d)),
                  full((1, d)), full((1, d)), full((1, ff)), full((1, d))],
        out_specs=[rows(hid), rows(hid), rows(ff + hid), rows(ff), pl.BlockSpec((2, tile, d), lambda i: (0, i, 0)),
                   pl.BlockSpec((2, halves, d // halves, tile), lambda i: (0, 0, 0, i)), rows(d), natural,
                   held((SUB, hid)), held((SUB, d)), held((SUB, ff)), held((SUB, d)), held((SUB, d))],
        out_shape=[sds((tok, hid), BF16), sds((tok, hid), BF16), sds((tok, ff + hid), BF16), sds((tok, ff), BF16), sds((2, tok, d), BF16),
                   sds((2, halves, d // halves, tok), BF16), sds((tok, d), F32),
                   sds((SUB, piece, d), BF16),
                   sds((SUB, hid), F32), sds((SUB, d), F32), sds((SUB, ff), F32), sds((SUB, d), F32), sds((SUB, d), F32)],
        scratch_shapes=[pltpu.VMEM((SUB, hid), F32), pltpu.VMEM((SUB, hid), F32), pltpu.VMEM((d // 128, tile + SUB * SUB, 128), F32),
                        pltpu.VMEM((tile, hid), F32)],
        compiler_params=params,
    )(a, b, zc, xp, nt, dy, enter, w_out, w_up, w_down, out_bias.reshape(1, d), gain2, up_bias.reshape(1, ff),
      down_bias.reshape(1, d))
    gate, slant, acts, gu, pairs, turns, gres, result, mu, gdb, gub, ggain2, gob = outs

    turns = turns.reshape(2 * halves, d // halves, tok)
    work = Work(d, hid, ff, d // halves, tok // back, LAG, seq, batch)
    plan = work.plan
    slots = plan.colors * 2
    bsteps = back // SUB
    lines = -(-(4 * d + 3 * hid + ff) // (8 * LANES)) * 8

    def at_tile(t):
        return work.tiles - 1 - jnp.clip(t - work.first_tile, 0, work.tiles - 1)

    btile = lambda n: pl.BlockSpec((back, n), lambda t: (at_tile(t), 0))
    any_space = pl.BlockSpec(memory_space=pl.ANY)

    def acts_at(t):
        late = jnp.clip(t - work.up, work.down, work.down + work.out - 1)
        return (0, jnp.where(t < work.down, t, late))

    def turned_at(t):
        up = jnp.clip(t - work.at_up, 0, work.up - 1) % halves
        gates = halves + jnp.clip(t - work.at_gates, 0, work.gates - 1) % halves
        return (jnp.where(t < work.at_out, up, gates), 0, 0)

    gin, small, sums = pl.pallas_call(
        functools.partial(sum_kernel, work),
        grid=(work.steps,),
        in_specs=[full((SUB, hid)), full((SUB, hid)), full((SUB, d)), full((SUB, ff)), full((SUB, d)), full((SUB, d)),
                  full((1, d)), full((d, 3 * hid)), full((hid, d)),
                  pl.BlockSpec((tok, work.rows), acts_at),
                  pl.BlockSpec((1, tok, d), lambda t: (jnp.where(t < work.at_up, 0, 1), 0, 0), pipeline_mode=pl.Buffered(1)),
                  pl.BlockSpec((1, work.rows, tok), turned_at),
                  pl.BlockSpec((tok, d), lambda t: (0, jnp.clip(t - work.at_up, 0, work.up - 1) // halves))]
        + [btile(hid)] * 5 + [pl.BlockSpec((1, back, d), lambda t: (1, at_tile(t), 0))] + [btile(d)] * 2,
        out_specs=[pl.BlockSpec((SUB, bsteps, d), lambda t: (0, at_tile(t), 0)), held((lines, LANES)), any_space],
        out_shape=[sds((SUB, piece, d), F32), sds((lines, LANES), F32), sds((work.chunks * work.rows, d), F32)],
        scratch_shapes=[
            pltpu.VMEM((work.chunks * work.rows, d), F32),
            pltpu.VMEM((slots, plan.recv_rows, d), F32),
            pltpu.VMEM((3 * hid // d, tok, d), BF16),
            pltpu.VMEM((back, 3 * hid), BF16),
            pltpu.VMEM((SUB, hid), F32),
            pltpu.VMEM((SUB, 3 * hid), F32),
            pltpu.VMEM((SUB, d), F32),
            pltpu.VMEM((d // 128, back + SUB * SUB, 128), F32),
            pltpu.VMEM((lines, LANES), F32),
            pltpu.VMEM((plan.K + 1, lines, LANES), F32),
            *ends_scratch(seq, hid)[:2],
            pltpu.SemaphoreType.DMA((slots, plan.stages)),
            pltpu.SemaphoreType.DMA((slots, plan.stages)),
            pltpu.SemaphoreType.REGULAR((slots, plan.K + 1)),
            pltpu.SemaphoreType.DMA((work.chunks,)),
            pltpu.SemaphoreType.DMA((plan.K + 1,)),
            pltpu.SemaphoreType.DMA((plan.K + 1,)),
            *ends_scratch(seq, hid)[2:],
        ],
        compiler_params=pltpu.CompilerParams(
            dimension_semantics=("arbitrary",), collective_id=0, has_side_effects=True, vmem_limit_bytes=62 << 20
        ),
    )(prod, mu, gdb, gub, ggain2, gob, gain1, w_gates, w_out, acts, pairs, turns, gu,
      a, gate, slant, fc, ic, pairs, xp, gres)
    sizes = (d, 3 * hid, d, d, ff, d)
    vmem = pl.BlockSpec(memory_space=pltpu.VMEM)
    gin, g_down, g_up, g_out, g_gates, *vecs = pl.pallas_call(
        functools.partial(last_kernel, work, sizes, grid),
        in_specs=[vmem, any_space, any_space],
        out_specs=[any_space] * 5 + [vmem] * 6,
        out_shape=[sds(gin.shape, F32), sds((ff, d), F32), sds((d, ff), F32), sds((hid, d), F32), sds((d, 3 * hid), F32)]
        + [sds((1, n), F32) for n in sizes],
        scratch_shapes=[pltpu.VMEM(gin.shape, F32), pltpu.VMEM(sums.shape, F32),
                        pltpu.SemaphoreType.DMA((grid + work.chunks,)), pltpu.SemaphoreType.DMA((grid + work.chunks,))],
        compiler_params=pltpu.CompilerParams(vmem_limit_bytes=62 << 20),
    )(small, gin, sums)
    ggain1, ggb, gob, ggain2, gub, gdb = [v.reshape(-1) for v in vecs]
    return (result.reshape(inputs.shape), gin.reshape(inputs.shape), ggain1, g_gates, ggb, g_out, gob,
            ggain2, g_up, gub, g_down, gdb)


def solution(mesh):
    rows = P("batch", "seq", None)
    return jax.shard_map(
        functools.partial(per_device, mesh.shape["seq"], mesh.shape["batch"]),
        mesh=mesh,
        in_specs=(rows, rows) + (P(),) * 12,
        out_specs=(rows, rows) + (P(),) * 10,
        check_vma=False,
    )
```
